32 devices in a mesh: fsdp: 8 (over z, y), tp: 4 (over x, core).
Axes of the slice: x: 2, y: 2, z: 4, core: 2. Of those that a mesh axis runs over, the one named last changes fastest.
Arguments:
- tokens: bfloat16 [2048, 2048], P(('fsdp', 'tp')), may hold values from -6 to 6
- cotangent: bfloat16 [2048, 2048], P(('fsdp', 'tp')), may hold values from -6 to 6
- doc_starts: int32 [8], replicated, may hold values from 0 to 2047, as said below
- skip_flags: int32 [8], replicated, may hold values from 0 to 1
- gain_attn: bfloat16 [2048], P('fsdp'), may hold values from 0.5 to 1.5
- w_query: bfloat16 [2048, 2048], P('fsdp', 'tp'), may hold values from -0.125 to 0.125
- w_key: bfloat16 [2048, 512], P('fsdp', 'tp'), may hold values from -0.125 to 0.125
- w_value: bfloat16 [2048, 512], P('fsdp', 'tp'), may hold values from -0.125 to 0.125
- w_out: bfloat16 [2048, 2048], P('tp', 'fsdp'), may hold values from -1 to 1
- gain_mlp: bfloat16 [2048], P('fsdp'), may hold values from 0.5 to 1.5
- w_gate: bfloat16 [2048, 5632], P('fsdp', 'tp'), may hold values from -0.125 to 0.125
- w_up: bfloat16 [2048, 5632], P('fsdp', 'tp'), may hold values from -0.125 to 0.125
- w_down: bfloat16 [5632, 2048], P('tp', 'fsdp'), may hold values from -0.078125 to 0.078125
Outputs:
- layer_out: bfloat16 [2048, 2048], P(('fsdp', 'tp'))
- d_tokens: bfloat16 [2048, 2048], P(('fsdp', 'tp'))
- grad_gain_attn: float32 [2048], P('fsdp')
- grad_query: float32 [2048, 2048], P('fsdp', 'tp')
- grad_key: float32 [2048, 512], P('fsdp', 'tp')
- grad_value: float32 [2048, 512], P('fsdp', 'tp')
- grad_out: float32 [2048, 2048], P('tp', 'fsdp')
- grad_gain_mlp: float32 [2048], P('fsdp')
- grad_gate: float32 [2048, 5632], P('fsdp', 'tp')
- grad_up: float32 [2048, 5632], P('fsdp', 'tp')
- grad_down: float32 [5632, 2048], P('tp', 'fsdp')
The draws below stay inside these ranges and needn't reach their ends.
Inputs may be any that keep to these rules, and one draw needn't show every extreme that they name: `doc_starts`: strictly increasing first rows of the 8 documents of the packed sequence, the first 0.
All inputs are finite; a program needn't handle non-finite values.
Results may differ from the reference program's by a relative error of at most 0.023.
Values may be sent and summed in bfloat16 or wider, within the bound.
No kernel may reach another device: no remote copies, remote signals or barrier semaphores. Data moves between devices by JAX's collectives and lax.ppermute only.
A program may use at most 192 MiB of HBM per device.

```python
import jax
import jax.numpy as jnp
from jax import lax

D = 2048
HEADS = 16
KV_HEADS = 4
HEAD_DIM = 128
FF = 5632
TOK_DEV = 256
DOCS = 8
TOKENS = 2048


def document_plan(key):
    pick, sizes = jax.random.split(key)
    longest = jax.random.randint(pick, (), 1, DOCS - 1)
    unit = max(TOK_DEV // (2 * DOCS), 1)
    lengths = jax.random.randint(sizes, (DOCS,), 1, unit + 1)
    index = jnp.arange(DOCS)
    others = jnp.sum(jnp.where(index == longest, 0, lengths))
    lengths = jnp.where(index == longest, TOKENS - others, lengths)
    return (longest, lengths)


def draw_doc_starts(key, part):
    base = key
    longest, lengths = document_plan(base)
    return (jnp.cumsum(lengths) - lengths).astype(jnp.int32)


def draw_skip_flags(key, part):
    base, key = (key, jax.random.fold_in(key, 5))
    longest, lengths = document_plan(base)
    coin, other = jax.random.split(key)
    flags = jax.random.randint(coin, (DOCS,), 0, 2)
    moved = jax.random.randint(other, (), 1, DOCS)
    forced = (longest + moved) % DOCS
    index = jnp.arange(DOCS)
    flags = jnp.where(index == forced, 1, flags)
    flags = jnp.where(index == longest, 0, flags)
    return flags.astype(jnp.int32)


def spiked(array, stream_key, source, target, shards_of, factor):
    def block_of(position):
        return (jnp.arange(array.shape[position]) // (array.shape[position] // shards_of)).reshape((-1,) + (1,) * (array.ndim - 1 - position))

    near = jax.random.permutation(stream_key, shards_of)[block_of(target)]
    far = (block_of(target) + shards_of // 2) % shards_of
    return jnp.where((block_of(source) == near) | (block_of(source) == far), factor * array, array)


def shard_levels(stream_key, dims, shards, least, top_value):
    def one(position, shards_of):
        heights = jax.random.uniform(jax.random.fold_in(jax.random.fold_in(stream_key, 6), position), (shards_of,), jnp.float32, least / len(shards), top_value / len(shards))
        return jnp.repeat(jnp.exp(heights), dims[position] // shards_of).reshape((-1,) + (1,) * (len(dims) - position - 1))

    loudness = one(*shards[0])
    for cut in shards[1:]:
        loudness = loudness * one(*cut)
    return loudness


def gaussian(rng, shape, scale, reach, pieces=(), kind=jnp.bfloat16):
    entries = jax.random.normal(rng, shape, jnp.float32) * scale
    if len(pieces) > 0:
        entries = shard_levels(rng, shape, pieces, -0.22, 0.18) * entries
    return jnp.clip(entries, min=-reach, max=reach).astype(kind)


def noise_with(own_key, extent, scale, reach, shards, heavy, held_as=jnp.bfloat16):
    entries = scale * jax.random.normal(own_key, extent, jnp.float32)
    if shards:
        entries = entries * shard_levels(own_key, extent, shards, -0.22, 0.18)
    return jnp.clip(spiked(entries, jax.random.fold_in(own_key, 3), *heavy), -reach, reach).astype(held_as)


def setup_inputs(seed: int = 0) -> dict:
    streams_of = jax.random.split(jax.random.key(seed), 14)
    return {
        "tokens": noise_with(streams_of[0], (TOKENS, D), 1.0, 6.0, ((0, 32),), (0, 1, 32, 2.75)),
        "cotangent": gaussian(streams_of[1], (TOKENS, D), 1.0, 6.0, ((0, 32),)),
        "doc_starts": draw_doc_starts(jax.random.fold_in(streams_of[13], 71), 0),
        "skip_flags": draw_skip_flags(jax.random.fold_in(streams_of[13], 71), 0),
        "gain_attn": jnp.clip(1.0 + 0.1 * jax.random.normal(streams_of[4], (D,), jnp.float32), 0.5, 1.5).astype(jnp.bfloat16),
        "w_query": gaussian(streams_of[5], (D, HEADS * HEAD_DIM), D ** -0.5, 0.125, ((0, 8), (1, 4))),
        "w_key": gaussian(streams_of[6], (D, KV_HEADS * HEAD_DIM), D ** -0.5, 0.125, ((0, 8), (1, 4))),
        "w_value": gaussian(streams_of[7], (D, KV_HEADS * HEAD_DIM), D ** -0.5, 0.125, ((0, 8), (1, 4))),
        "w_out": gaussian(streams_of[8], (HEADS * HEAD_DIM, D), (HEADS * HEAD_DIM // 64) ** -0.5, 1.0, ((0, 4), (1, 8))),
        "gain_mlp": jnp.clip(1.0 + 0.1 * jax.random.normal(streams_of[9], (D,), jnp.float32), 0.5, 1.5).astype(jnp.bfloat16),
        "w_gate": gaussian(streams_of[10], (D, FF), D ** -0.5, 0.125, ((0, 8), (1, 4))),
        "w_up": gaussian(streams_of[11], (D, FF), D ** -0.5, 0.125, ((0, 8), (1, 4))),
        "w_down": gaussian(streams_of[12], (FF, D), FF ** -0.5, 0.078125, ((0, 4), (1, 8))),
    }


EPS = 1e-05
THETA = 10000.0
FLOOR = -1e+30
HIGH = lax.Precision.HIGHEST

@jax.custom_vjp
def low(v):
    return lax.optimization_barrier(v.astype(jnp.bfloat16)).astype(jnp.float32)

@jax.custom_vjp
def low_back(v):
    return v

def low_keep(v):
    return (low(v), None)

def low_pass(kept, grad):
    return (grad,)

def back_keep(v):
    return (v, None)

def back_low(kept, grad):
    return (low(grad),)
low.defvjp(low_keep, low_pass)
low_back.defvjp(back_keep, back_low)

def turn(values):
    half = values.shape[-1] // 2
    return jnp.concatenate([-values[..., half:], values[..., :half]], axis=-1)

def angles(places, width):
    half = width // 2
    freq = 1.0 / THETA ** (jnp.arange(half, dtype=jnp.float32) * 2.0 / width)
    angle = places.astype(jnp.float32)[:, None] * freq[None, :]
    cosine = jnp.cos(angle)
    sine = jnp.sin(angle)
    return (jnp.concatenate([cosine, cosine], -1), jnp.concatenate([sine, sine], -1))

def rotate(values, cosine, sine):
    return values * cosine + turn(values) * sine

def documents(doc_starts, skip_flags, row_index):
    inside = (doc_starts[None, :] <= row_index[:, None]).astype(jnp.int32)
    segment = lax.optimization_barrier(jnp.sum(inside, axis=1)) - 1
    begins = lax.optimization_barrier(jnp.max(jnp.where(inside > 0, doc_starts[None, :], 0), axis=1))
    chosen = (segment[:, None] == jnp.arange(doc_starts.shape[0], dtype=jnp.int32)[None, :]).astype(jnp.int32)
    skipped = lax.optimization_barrier(jnp.sum(chosen * skip_flags[None, :], axis=1))
    return (segment, row_index - begins, (1 - skipped).astype(jnp.float32))

def product(left, right):
    return jnp.dot(left, right, precision=HIGH, preferred_element_type=jnp.float32)

def attend(queries, keys, values, segment):
    row_count = queries.shape[0]
    span = min(256, row_count)
    groups = HEADS // KV_HEADS
    blocks = queries.reshape(row_count // span, span, KV_HEADS, groups, HEAD_DIM)
    key_rows = jnp.arange(row_count, dtype=jnp.int32)
    factor = HEAD_DIM ** (-0.5)

    def one_block(element):
        query_block, index = element
        query_rows = index * span + jnp.arange(span, dtype=jnp.int32)
        query_segment = lax.dynamic_slice_in_dim(segment, index * span, span, 0)
        raw = low_back(jnp.einsum('qkgd,tkd->kgqt', query_block, keys, precision=HIGH))
        allowed = (query_segment[:, None] == segment[None, :]) & (key_rows[None, :] <= query_rows[:, None])
        scores = jnp.where(allowed, raw * factor, FLOOR)
        weights = low(jax.nn.softmax(scores, axis=-1))
        mixed = jnp.einsum('kgqt,tkd->qkgd', weights, values, precision=HIGH)
        return mixed.reshape(span, HEADS * HEAD_DIM)
    outputs = lax.map(jax.checkpoint(one_block), (blocks, jnp.arange(row_count // span, dtype=jnp.int32)))
    return outputs.reshape(row_count, HEADS * HEAD_DIM)

def reference(tokens, cotangent, doc_starts, skip_flags, gain_attn, w_query, w_key, w_value, w_out, gain_mlp, w_gate, w_up, w_down):
    row_index = jnp.arange(TOKENS, dtype=jnp.int32)
    segment, places, keep_mask = documents(doc_starts, skip_flags, row_index)
    cosine, sine = angles(places, HEAD_DIM)
    keep = keep_mask[:, None]
    cos_heads = cosine[:, None, :]
    sin_heads = sine[:, None, :]

    def layer(inputs, gain_one, query_w, key_w, value_w, out_w, gain_two, gate_w, up_w, down_w):
        normed = low(inputs * lax.rsqrt(lax.optimization_barrier(jnp.mean(inputs * inputs, axis=-1, keepdims=True)) + EPS) * gain_one)
        queries = low(rotate(low_back(product(normed, query_w)).reshape(TOKENS, HEADS, HEAD_DIM), cos_heads, sin_heads))
        keys = low(rotate(low_back(product(normed, key_w)).reshape(TOKENS, KV_HEADS, HEAD_DIM), cos_heads, sin_heads))
        values = low_back(low(product(normed, value_w))).reshape(TOKENS, KV_HEADS, HEAD_DIM)
        attended = low_back(low(attend(queries, keys, values, segment)))
        middle = inputs + keep * low_back(product(attended, out_w))
        normed_two = low(middle * lax.rsqrt(lax.optimization_barrier(jnp.mean(middle * middle, axis=-1, keepdims=True)) + EPS) * gain_two)
        gate_values = low_back(product(normed_two, gate_w))
        up_values = low_back(product(normed_two, up_w))
        hidden = low(jax.nn.silu(gate_values) * up_values)
        return middle + keep * low_back(product(hidden, down_w))
    floats = [item.astype(jnp.float32) for item in (tokens, gain_attn, w_query, w_key, w_value, w_out, gain_mlp, w_gate, w_up, w_down)]
    layer_out, pull = jax.vjp(layer, *floats)
    grads = pull(cotangent.astype(jnp.float32))
    return (layer_out.astype(jnp.bfloat16), grads[0].astype(jnp.bfloat16), grads[1], grads[2], grads[3], grads[4], grads[5], grads[6], grads[7], grads[8], grads[9])
```

```python
import functools

import jax
import jax.numpy as jnp
from jax import lax
from jax.experimental import pallas as pl
from jax.experimental.pallas import tpu as pltpu
from jax.sharding import PartitionSpec as P

HEAD_DIM = 128
EPS = 1e-05
THETA = 10000.0
FLOOR = -1e30
LOG2E = 1.4426950408889634
F32 = jnp.float32
BF16 = jnp.bfloat16
HI = 4


def turn(values):
    half = values.shape[-1] // 2
    return jnp.concatenate([-values[..., half:], values[..., :half]], axis=-1)


def angles(places, width):
    half = width // 2
    freq = 1.0 / THETA ** (jnp.arange(half, dtype=F32) * 2.0 / width)
    angle = places.astype(F32)[:, None] * freq[None, :]
    cosine = jnp.cos(angle)
    sine = jnp.sin(angle)
    return (jnp.concatenate([cosine, cosine], -1), jnp.concatenate([sine, sine], -1))


def rotate(values, cosine, sine):
    return values * cosine + turn(values) * sine


def unrotate(grads, cosine, sine):
    return grads * cosine - turn(grads * sine)


def documents(doc_starts, skip_flags, row_index):
    inside = doc_starts[None, :] <= row_index[:, None]
    segment = jnp.sum(inside.astype(jnp.int32), axis=1) - 1
    begins = jnp.max(jnp.where(inside, doc_starts[None, :], 0), axis=1)
    chosen = segment[:, None] == jnp.arange(doc_starts.shape[0], dtype=jnp.int32)[None, :]
    skipped = jnp.sum(jnp.where(chosen, skip_flags[None, :], 0), axis=1)
    return (begins, (1 - skipped).astype(F32))


def product(left, right):
    return jnp.dot(left, right, preferred_element_type=F32)


def against(left, right):
    return lax.dot_general(left, right, (((1,), (1,)), ((), ())), preferred_element_type=F32)


def outer_sum(left, right):
    return lax.dot_general(left, right, (((0,), (0,)), ((), ())), preferred_element_type=F32)


def allowed_keys(block, size, koff_ref, qrow_ref, beg_ref):
    krow = koff_ref[...] + block * size
    return (krow <= qrow_ref[...]) & (krow >= beg_ref[...])


def attend_kernel(heads, bounds, q_ref, kv_ref, qrow_ref, beg_ref, koff_ref, o_ref, lse_ref, top, mass, acc):
    size = koff_ref.shape[1]
    factor = HEAD_DIM**-0.5 * LOG2E
    top[...] = jnp.full_like(top, FLOOR)
    mass[...] = jnp.zeros_like(mass)
    acc[...] = jnp.zeros_like(acc)

    def step(block, carry):
        rows = pl.ds(pl.multiple_of(block * size, size), size)
        keys = kv_ref[rows, :HEAD_DIM]
        values = kv_ref[rows, HEAD_DIM:]
        mask = allowed_keys(block, size, koff_ref, qrow_ref, beg_ref)
        for h in range(heads):
            cols = slice(h * HEAD_DIM, (h + 1) * HEAD_DIM)
            scores = jnp.where(mask, against(q_ref[:, cols], keys) * factor, FLOOR)
            before = top[h]
            now = jnp.maximum(before, jnp.max(scores, axis=1, keepdims=True))
            weights = jnp.exp2(scores - now)
            fading = jnp.exp2(before - now)
            top[h] = now
            mass[h] = mass[h] * fading + jnp.sum(weights, axis=1, keepdims=True)
            acc[h] = acc[h] * fading + product(weights.astype(BF16), values)
        return carry

    lax.fori_loop(bounds[0], bounds[1] + 1, step, 0)
    for h in range(heads):
        o_ref[:, h * HEAD_DIM : (h + 1) * HEAD_DIM] = (acc[h] / mass[h]).astype(BF16)
        lse_ref[h] = top[h] + jnp.log2(mass[h])


def attend_back_kernel(
    heads, bounds, q_ref, kv_ref, o_ref, do_ref, lse_ref, qrow_ref, beg_ref, koff_ref, dq_ref, dkv_ref, delta, acc
):
    size = koff_ref.shape[1]
    factor = HEAD_DIM**-0.5
    acc[...] = jnp.zeros_like(acc)
    dkv_ref[...] = jnp.zeros_like(dkv_ref)
    for h in range(heads):
        cols = slice(h * HEAD_DIM, (h + 1) * HEAD_DIM)
        delta[h] = jnp.sum(do_ref[:, cols].astype(F32) * o_ref[:, cols].astype(F32), axis=1, keepdims=True)

    def step(block, carry):
        rows = pl.ds(pl.multiple_of(block * size, size), size)
        keys = kv_ref[rows, :HEAD_DIM]
        values = kv_ref[rows, HEAD_DIM:]
        mask = allowed_keys(block, size, koff_ref, qrow_ref, beg_ref)
        dkeys = jnp.zeros((size, HEAD_DIM), F32)
        dvalues = jnp.zeros((size, HEAD_DIM), F32)
        for h in range(heads):
            cols = slice(h * HEAD_DIM, (h + 1) * HEAD_DIM)
            queries = q_ref[:, cols]
            grads = do_ref[:, cols]
            scores = jnp.where(mask, against(queries, keys) * (factor * LOG2E), FLOOR)
            probs = jnp.exp2(scores - lse_ref[h])
            dvalues = dvalues + outer_sum(probs.astype(BF16), grads)
            dprobs = against(grads, values)
            dscores = (probs * ((dprobs - delta[h]) * factor)).astype(BF16)
            acc[h] = acc[h] + product(dscores, keys)
            dkeys = dkeys + outer_sum(dscores, queries)
        dkv_ref[rows, :HEAD_DIM] = dkeys.astype(BF16)
        dkv_ref[rows, HEAD_DIM:] = dvalues.astype(BF16)
        return carry

    lax.fori_loop(bounds[0], bounds[1] + 1, step, 0)
    for h in range(heads):
        dq_ref[:, h * HEAD_DIM : (h + 1) * HEAD_DIM] = acc[h]


VMEM_SPEC = pl.BlockSpec(memory_space=pltpu.VMEM)
SMEM_SPEC = pl.BlockSpec(memory_space=pltpu.SMEM)


def attend(bounds, q, kv, qrow, beg, koff):
    rows, width = q.shape
    heads = width // HEAD_DIM
    return pl.pallas_call(
        functools.partial(attend_kernel, heads),
        out_shape=(
            jax.ShapeDtypeStruct((rows, width), BF16),
            jax.ShapeDtypeStruct((heads, rows, 1), F32),
        ),
        in_specs=[SMEM_SPEC] + [VMEM_SPEC] * 5,
        out_specs=(VMEM_SPEC, VMEM_SPEC),
        scratch_shapes=[
            pltpu.VMEM((heads, rows, 1), F32),
            pltpu.VMEM((heads, rows, 1), F32),
            pltpu.VMEM((heads, rows, HEAD_DIM), F32),
        ],
        compiler_params=pltpu.CompilerParams(vmem_limit_bytes=32 * 1024 * 1024),
        cost_estimate=pl.CostEstimate(flops=4 * rows * width * kv.shape[0], bytes_accessed=4 << 20, transcendentals=0),
    )(bounds, q, kv, qrow, beg, koff)


def attend_back(bounds, q, kv, o, do, lse, qrow, beg, koff):
    rows, width = q.shape
    heads = width // HEAD_DIM
    return pl.pallas_call(
        functools.partial(attend_back_kernel, heads),
        out_shape=(
            jax.ShapeDtypeStruct((rows, width), F32),
            jax.ShapeDtypeStruct(kv.shape, BF16),
        ),
        in_specs=[SMEM_SPEC] + [VMEM_SPEC] * 8,
        out_specs=(VMEM_SPEC, VMEM_SPEC),
        scratch_shapes=[
            pltpu.VMEM((heads, rows, 1), F32),
            pltpu.VMEM((heads, rows, HEAD_DIM), F32),
        ],
        compiler_params=pltpu.CompilerParams(vmem_limit_bytes=32 * 1024 * 1024),
        cost_estimate=pl.CostEstimate(flops=10 * rows * width * kv.shape[0], bytes_accessed=8 << 20, transcendentals=0),
    )(bounds, q, kv, o, do, lse, qrow, beg, koff)


class Exchange:
    def __init__(self, mesh):
        self.shards = mesh.shape["fsdp"]
        self.hi = HI
        self.lo = self.shards // HI
        self.tp = mesh.shape["tp"]
        self.hi_groups = [[h * self.lo + b for h in range(self.hi)] for b in range(self.lo)]

    def hi_shift(self, v, s):
        pairs = [
            (h * self.lo + b, ((h + s) % self.hi) * self.lo + b) for h in range(self.hi) for b in range(self.lo)
        ]
        return lax.ppermute(v, "fsdp", pairs)

    def lo_shift(self, v, s):
        pairs = [
            (h * self.lo + b, h * self.lo + (b + s) % self.lo) for h in range(self.hi) for b in range(self.lo)
        ]
        return lax.ppermute(v, "fsdp", pairs)

    def flip(self, v, mask):
        return lax.ppermute(v, "tp", [(t, t ^ mask) for t in range(self.tp)])

    def hi_swap(self, v):
        return lax.all_to_all(v, "fsdp", 0, 0, axis_index_groups=self.hi_groups)

    def order_lo(self, pieces):
        b = lax.axis_index("fsdp") % self.lo
        if self.lo == 2:
            own, other = pieces
            return jnp.stack([jnp.where(b == 0, own, other), jnp.where(b == 0, other, own)], axis=1)
        hi, n, k = pieces[0].shape
        out = jnp.zeros((hi, self.lo, n, k), pieces[0].dtype)
        for s, piece in enumerate(pieces):
            out = lax.dynamic_update_slice(out, piece[:, None], (0, (b - s) % self.lo, 0, 0))
        return out

    def gather_lo(self, v):
        return [v] + [self.lo_shift(v, s) for s in range(1, self.lo)]

    def gather_rows(self, w):
        n, k = w.shape
        got = self.hi_swap(jnp.broadcast_to(w[None], (self.hi, n, k)))
        return self.order_lo(self.gather_lo(got)).reshape(self.shards * n, k)

    def lo_part(self, blocks, s):
        b = lax.axis_index("fsdp") % self.lo
        return lax.dynamic_index_in_dim(blocks, (b + s) % self.lo, 1, keepdims=False)

    def reduce_lo(self, g):
        rows, k = g.shape
        blocks = g.reshape(self.hi, self.lo, rows // self.shards, k)
        got = [self.lo_shift(self.lo_part(blocks, s).astype(BF16), s) for s in range(1, self.lo)]
        total = self.lo_part(blocks, 0).astype(F32)
        for piece in got:
            total = total + piece.astype(F32)
        return total.astype(BF16)

    def scatter_rows(self, g):
        return jnp.sum(self.hi_swap(self.reduce_lo(g)).astype(F32), axis=0)

    def tp_gather(self, v):
        v = jnp.concatenate([v, self.flip(v, 2)], axis=0)
        return jnp.concatenate([v, self.flip(v, 1)], axis=0)

    def tp_reduce(self, g):
        half = g.shape[0] // 2
        g = g[:half] + self.flip(g[half:].astype(BF16), 1).astype(F32)
        quarter = half // 2
        return g[:quarter] + self.flip(g[quarter:].astype(BF16), 2).astype(F32)

    def mlp_gather(self, v):
        v = jnp.concatenate([v] + [self.hi_shift(v, s) for s in range(1, self.hi)], axis=0)
        return jnp.concatenate([v, self.flip(v, 1)], axis=0)

    def mlp_reduce(self, g):
        half = g.shape[0] // 2
        g = (g[:half] + self.flip(g[half:].astype(BF16), 1).astype(F32))
        n = half // self.hi
        total = g[:n]
        low = g.astype(BF16)
        for s in range(1, self.hi):
            total = total + self.hi_shift(low[s * n : (s + 1) * n], -s).astype(F32)
        return total

    def spread_columns(self, w):
        n, k = w.shape
        chunk = -(-k // (self.hi * 128)) * 128
        w = jnp.pad(w, ((0, 0), (0, self.hi * chunk - k)))
        got = self.hi_swap(w.reshape(n, self.hi, chunk).transpose(1, 0, 2))
        pieces = self.gather_lo(got)
        others = [self.flip(p, 2) for p in pieces]
        return (
            self.order_lo(pieces).reshape(self.shards * n, chunk),
            self.order_lo(others).reshape(self.shards * n, chunk),
        )

    def collect_columns(self, own, other, k):
        total = own + self.flip(other.astype(BF16), 2).astype(F32)
        got = self.hi_swap(self.reduce_lo(total))
        hi, n, chunk = got.shape
        return got.transpose(1, 0, 2).reshape(n, hi * chunk)[:, :k].astype(F32)


def local(
    ex,
    tokens,
    cotangent,
    doc_starts,
    skip_flags,
    gain_attn,
    w_query,
    w_key,
    w_value,
    w_out,
    gain_mlp,
    w_gate,
    w_up,
    w_down,
):
    count, width = tokens.shape
    fsdp = lax.axis_index("fsdp")
    tp = lax.axis_index("tp")
    q_width = w_query.shape[1]
    k_width = w_key.shape[1]
    hidden_width = w_gate.shape[1]

    offsets = jnp.arange(count, dtype=jnp.int32)
    koff = jnp.concatenate([(tp ^ m) * count + offsets for m in (0, 2, 1, 3)])
    block_rows = koff.shape[0]
    row_index = fsdp * block_rows + koff
    begins, keep_rows = documents(doc_starts, skip_flags, row_index)
    keep_own = keep_rows[:count, None]
    cosine, sine = angles(row_index - begins, HEAD_DIM)
    qrow = row_index[:, None]
    beg = begins[:, None]
    bounds = jnp.stack([jnp.min(begins) // block_rows, fsdp]).astype(jnp.int32)

    gains = lax.all_gather(jnp.stack([gain_attn, gain_mlp]), "fsdp", axis=1, tiled=True).astype(F32)
    w_kv = ex.gather_rows(jnp.concatenate([w_key, w_value], axis=1))
    w_q = ex.gather_rows(w_query)
    w_o = ex.gather_rows(w_out.T)
    gate_own, gate_other = ex.spread_columns(w_gate)
    up_own, up_other = ex.spread_columns(w_up)
    down_own, down_other = ex.spread_columns(w_down.T)
    w_gu = jnp.concatenate([gate_own, gate_other, up_own, up_other], axis=1)
    w_d = jnp.concatenate([down_own, down_other], axis=1)

    whole = ex.tp_gather(tokens).astype(F32)
    scale_attn = lax.rsqrt(jnp.mean(whole * whole, axis=-1, keepdims=True) + EPS)
    normed_attn = (whole * scale_attn * gains[0][None, :]).astype(BF16)
    kv_raw = product(normed_attn, w_kv)
    keys = rotate(kv_raw[:, :k_width], cosine, sine)
    kv = jnp.concatenate([keys, kv_raw[:, k_width:]], axis=1).astype(BF16)
    kv_all = lax.all_to_all(jnp.broadcast_to(kv[None], (ex.shards,) + kv.shape), "fsdp", 0, 0)
    kv_all = kv_all.reshape(ex.shards * block_rows, 2 * k_width)
    heads = q_width // HEAD_DIM
    q_raw = product(normed_attn, w_q).reshape(block_rows, heads, HEAD_DIM)
    queries = rotate(q_raw, cosine[:, None, :], sine[:, None, :]).astype(BF16).reshape(block_rows, q_width)
    attended, lse = attend(bounds, queries, kv_all, qrow, beg, koff[None, :])
    attn_branch = ex.tp_reduce(against(attended, w_o))
    middle = tokens.astype(F32) + keep_own * attn_branch
    scale_mlp = lax.rsqrt(jnp.mean(middle * middle, axis=-1, keepdims=True) + EPS)
    normed_own = (middle * scale_mlp * gains[1][None, :]).astype(BF16)

    grads_own = cotangent.astype(F32)
    d_mlp = ex.mlp_gather((keep_own * grads_own).astype(BF16))
    normed_mlp = ex.mlp_gather(normed_own)
    gate_up = product(normed_mlp, w_gu)
    units = w_d.shape[1]
    gate = gate_up[:, :units]
    up = gate_up[:, units:]
    sigma = jax.nn.sigmoid(gate)
    hidden = (gate * sigma * up).astype(BF16)
    mlp_branch = ex.mlp_reduce(against(hidden, w_d))
    layer_out = (middle + keep_own * mlp_branch).astype(BF16)

    d_hidden = product(d_mlp, w_d)
    d_gate = (d_hidden * up * sigma * (1.0 + gate * (1.0 - sigma))).astype(BF16)
    d_up = (d_hidden * gate * sigma).astype(BF16)
    d_gu = jnp.concatenate([d_gate, d_up], axis=1)
    d_normed = ex.mlp_reduce(against(d_gu, w_gu))
    half = units // 2
    g_gu = outer_sum(normed_mlp, d_gu)
    grad_gate = ex.collect_columns(g_gu[:, :half], g_gu[:, half:units], hidden_width)
    grad_up = ex.collect_columns(g_gu[:, units : units + half], g_gu[:, units + half :], hidden_width)
    g_d = outer_sum(d_mlp, hidden)
    grad_down = ex.collect_columns(g_d[:, :half], g_d[:, half:], hidden_width).T

    gain_sum_mlp = jnp.sum(d_normed * middle * scale_mlp, axis=0)
    scaled = d_normed * gains[1][None, :]
    d_middle = (
        grads_own
        + scale_mlp * scaled
        - middle * scale_mlp**3 * jnp.mean(scaled * middle, axis=-1, keepdims=True)
    )

    d_attn = ex.tp_gather((keep_own * d_middle).astype(BF16))
    d_attended = product(d_attn, w_o).astype(BF16)
    grad_out = ex.scatter_rows(outer_sum(d_attn, attended)).T
    dq_rot, dkv_part = attend_back(bounds, queries, kv_all, attended, d_attended, lse, qrow, beg, koff[None, :])
    dkv = jnp.sum(
        lax.all_to_all(dkv_part.reshape(ex.shards, block_rows, 2 * k_width), "fsdp", 0, 0).astype(F32), axis=0
    )
    d_query = (
        unrotate(dq_rot.reshape(block_rows, heads, HEAD_DIM), cosine[:, None, :], sine[:, None, :])
        .astype(BF16)
        .reshape(block_rows, q_width)
    )
    grad_query = ex.scatter_rows(outer_sum(normed_attn, d_query))
    d_kv = jnp.concatenate([unrotate(dkv[:, :k_width], cosine, sine), dkv[:, k_width:]], axis=1).astype(BF16)
    grad_kv = ex.scatter_rows(outer_sum(normed_attn, d_kv))
    d_normed_attn = ex.tp_reduce(against(d_query, w_q) + against(d_kv, w_kv))
    own = whole[:count]
    scale_own = scale_attn[:count]
    gain_sum_attn = jnp.sum(d_normed_attn * own * scale_own, axis=0)
    scaled_attn = d_normed_attn * gains[0][None, :]
    d_tokens = (
        d_middle
        + scale_own * scaled_attn
        - own * scale_own**3 * jnp.mean(scaled_attn * own, axis=-1, keepdims=True)
    ).astype(BF16)

    shard = gain_attn.shape[0]
    sums = jnp.stack([gain_sum_attn.reshape(ex.shards, shard), gain_sum_mlp.reshape(ex.shards, shard)], axis=1)
    sums = jnp.sum(lax.all_to_all(sums, "fsdp", 0, 0), axis=0)
    sums = sums + ex.flip(sums, 2)
    sums = sums + ex.flip(sums, 1)

    return (
        layer_out,
        d_tokens,
        sums[0],
        grad_query,
        grad_kv[:, :k_width],
        grad_kv[:, k_width:],
        grad_out,
        sums[1],
        grad_gate,
        grad_up,
        grad_down,
    )


def solution(mesh):
    rows = P(("fsdp", "tp"), None)
    in_specs = (
        rows,
        rows,
        P(),
        P(),
        P("fsdp"),
        P("fsdp", "tp"),
        P("fsdp", "tp"),
        P("fsdp", "tp"),
        P("tp", "fsdp"),
        P("fsdp"),
        P("fsdp", "tp"),
        P("fsdp", "tp"),
        P("tp", "fsdp"),
    )
    out_specs = (
        rows,
        rows,
        P("fsdp"),
        P("fsdp", "tp"),
        P("fsdp", "tp"),
        P("fsdp", "tp"),
        P("tp", "fsdp"),
        P("fsdp"),
        P("fsdp", "tp"),
        P("fsdp", "tp"),
        P("tp", "fsdp"),
    )
    return jax.shard_map(
        functools.partial(local, Exchange(mesh)), mesh=mesh, in_specs=in_specs, out_specs=out_specs, check_vma=False
    )
```

```python
import functools

import jax
import jax.numpy as jnp
from jax import lax
from jax.experimental import pallas as pl
from jax.experimental.pallas import tpu as pltpu
from jax.sharding import PartitionSpec as P

HEAD_DIM = 128
EPS = 1e-05
THETA = 10000.0
FLOOR = -1e30
LOG2E = 1.4426950408889634
MIB = 1024 * 1024
F32 = jnp.float32
BF16 = jnp.bfloat16
HI = 4


def angles(places, width):
    half = width // 2
    freq = 1.0 / THETA ** (jnp.arange(half, dtype=F32) * 2.0 / width)
    angle = places.astype(F32)[:, None] * freq[None, :]
    cosine = jnp.cos(angle)
    sine = jnp.sin(angle)
    return (jnp.concatenate([cosine, cosine], -1), jnp.concatenate([sine, sine], -1))


def documents(doc_starts, skip_flags, row_index):
    inside = doc_starts[None, :] <= row_index[:, None]
    segment = jnp.sum(inside.astype(jnp.int32), axis=1) - 1
    begins = jnp.max(jnp.where(inside, doc_starts[None, :], 0), axis=1)
    chosen = segment[:, None] == jnp.arange(doc_starts.shape[0], dtype=jnp.int32)[None, :]
    skipped = jnp.sum(jnp.where(chosen, skip_flags[None, :], 0), axis=1)
    return (begins, (1 - skipped).astype(F32))


def product(left, right):
    return jnp.dot(left, right, preferred_element_type=F32)


def against(left, right):
    return lax.dot_general(left, right, (((1,), (1,)), ((), ())), preferred_element_type=F32)


def outer_sum(left, right):
    return lax.dot_general(left, right, (((0,), (0,)), ((), ())), preferred_element_type=F32)


def block_rows_of(block, bounds, lo, size):
    piece = lax.rem(lax.rem(block, lo) - bounds[2] + lo, lo)
    place = piece * HI + lax.div(block, lo)
    return pl.ds(pl.multiple_of(place * size, size), size)


def closed_keys(block, size, koff_ref, qrow_ref, beg_ref):
    krow = koff_ref[...] + block * size
    return jnp.where((krow <= qrow_ref[...]) & (krow >= beg_ref[...]), 0.0, FLOOR)


def attend_kernel(heads, lo, bounds, q_ref, kv_ref, qrow_ref, beg_ref, koff_ref, o_ref, lse_ref, top, mass, acc):
    size = koff_ref.shape[0]
    factor = HEAD_DIM**-0.5 * LOG2E
    top[...] = jnp.full_like(top, FLOOR)
    mass[...] = jnp.zeros_like(mass)
    acc[...] = jnp.zeros_like(acc)

    def step(block, carry):
        rows = block_rows_of(block, bounds, lo, size)
        keys = kv_ref[rows, :HEAD_DIM]
        values = kv_ref[rows, HEAD_DIM:].astype(F32).T.astype(BF16)
        closed = closed_keys(block, size, koff_ref, qrow_ref, beg_ref)
        for h in range(heads):
            scores = against(keys, q_ref[:, h * HEAD_DIM : (h + 1) * HEAD_DIM]) * factor + closed
            before = top[h]
            now = jnp.maximum(before, jnp.max(scores, axis=0, keepdims=True))
            weights = jnp.exp2(scores - now)
            fading = jnp.exp2(before - now)
            top[h] = now
            mass[h] = mass[h] * fading + jnp.sum(weights, axis=0, keepdims=True)
            acc[h] = acc[h] * fading + product(values, weights.astype(BF16))
        return carry

    lax.fori_loop(bounds[0], bounds[1] + 1, step, 0)
    for h in range(heads):
        o_ref[:, h * HEAD_DIM : (h + 1) * HEAD_DIM] = (acc[h] / mass[h]).T.astype(BF16)
        lse_ref[h] = top[h] + jnp.log2(mass[h])


def attend_back_kernel(
    heads, lo, bounds, q_ref, kv_ref, o_ref, do_ref, lse_ref, qrow_ref, beg_ref, koff_ref, cos_ref, sin_ref,
    dq_ref, dkv_ref, delta, acc
):
    size = koff_ref.shape[0]
    factor = HEAD_DIM**-0.5
    acc[...] = jnp.zeros_like(acc)
    dkv_ref[...] = jnp.zeros_like(dkv_ref)
    for h in range(heads):
        cols = slice(h * HEAD_DIM, (h + 1) * HEAD_DIM)
        both = do_ref[:, cols].astype(F32) * o_ref[:, cols].astype(F32)
        delta[h] = jnp.sum(both.T, axis=0, keepdims=True)

    def step(block, carry):
        rows = block_rows_of(block, bounds, lo, size)
        keys = kv_ref[rows, :HEAD_DIM]
        values = kv_ref[rows, HEAD_DIM:]
        turned_keys = keys.astype(F32).T.astype(BF16)
        closed = closed_keys(block, size, koff_ref, qrow_ref, beg_ref)
        dkeys = jnp.zeros((size, HEAD_DIM), F32)
        dvalues = jnp.zeros((size, HEAD_DIM), F32)
        for h in range(heads):
            cols = slice(h * HEAD_DIM, (h + 1) * HEAD_DIM)
            queries = q_ref[:, cols]
            grads = do_ref[:, cols]
            scores = against(keys, queries) * (factor * LOG2E) + closed
            probs = jnp.exp2(scores - lse_ref[h])
            dvalues = dvalues + product(probs.astype(BF16), grads)
            dprobs = against(values, grads)
            dscores = (probs * ((dprobs - delta[h]) * factor)).astype(BF16)
            acc[h] = acc[h] + product(turned_keys, dscores)
            dkeys = dkeys + product(dscores, queries)
        dkv_ref[rows, :HEAD_DIM] = dkeys.astype(BF16)
        dkv_ref[rows, HEAD_DIM:] = dvalues.astype(BF16)
        return carry

    lax.fori_loop(bounds[0], bounds[1] + 1, step, 0)
    for h in range(heads):
        grads = acc[h].T
        back = grads * cos_ref[...] - pltpu.roll(grads, HEAD_DIM // 2, 1) * sin_ref[...]
        dq_ref[:, h * HEAD_DIM : (h + 1) * HEAD_DIM] = back.astype(BF16)


VMEM_SPEC = pl.BlockSpec(memory_space=pltpu.VMEM)
SMEM_SPEC = pl.BlockSpec(memory_space=pltpu.SMEM)
NOTHING = pl.CostEstimate(flops=1, bytes_accessed=1, transcendentals=0)


def attend(bounds, q, kv, qrow, beg, koff, lo):
    rows, width = q.shape
    heads = width // HEAD_DIM
    return pl.pallas_call(
        functools.partial(attend_kernel, heads, lo),
        out_shape=(
            jax.ShapeDtypeStruct((rows, width), BF16),
            jax.ShapeDtypeStruct((heads, 1, rows), F32),
        ),
        in_specs=[SMEM_SPEC] + [VMEM_SPEC] * 5,
        out_specs=(VMEM_SPEC, VMEM_SPEC),
        scratch_shapes=[
            pltpu.VMEM((heads, 1, rows), F32),
            pltpu.VMEM((heads, 1, rows), F32),
            pltpu.VMEM((heads, HEAD_DIM, rows), F32),
        ],
        compiler_params=pltpu.CompilerParams(vmem_limit_bytes=16 * MIB),
        cost_estimate=NOTHING,
    )(bounds, q, kv, qrow, beg, koff)


def attend_back(bounds, q, kv, o, do, lse, qrow, beg, koff, cosine, signed, lo):
    rows, width = q.shape
    heads = width // HEAD_DIM
    return pl.pallas_call(
        functools.partial(attend_back_kernel, heads, lo),
        out_shape=(
            jax.ShapeDtypeStruct((rows, width), BF16),
            jax.ShapeDtypeStruct(kv.shape, BF16),
        ),
        in_specs=[SMEM_SPEC] + [VMEM_SPEC] * 10,
        out_specs=(VMEM_SPEC, VMEM_SPEC),
        scratch_shapes=[
            pltpu.VMEM((heads, 1, rows), F32),
            pltpu.VMEM((heads, HEAD_DIM, rows), F32),
        ],
        compiler_params=pltpu.CompilerParams(vmem_limit_bytes=16 * MIB),
        cost_estimate=NOTHING,
    )(bounds, q, kv, o, do, lse, qrow, beg, koff, cosine, signed)


class Exchange:
    def __init__(self, mesh):
        self.shards = mesh.shape["fsdp"]
        self.hi = HI
        self.lo = self.shards // HI
        self.tp = mesh.shape["tp"]
        self.hi_groups = [[h * self.lo + b for h in range(self.hi)] for b in range(self.lo)]

    def hi_shift(self, v, s):
        pairs = [
            (h * self.lo + b, ((h + s) % self.hi) * self.lo + b) for h in range(self.hi) for b in range(self.lo)
        ]
        return lax.ppermute(v, "fsdp", pairs)

    def lo_shift(self, v, s):
        pairs = [
            (h * self.lo + b, h * self.lo + (b + s) % self.lo) for h in range(self.hi) for b in range(self.lo)
        ]
        return lax.ppermute(v, "fsdp", pairs)

    def flip(self, v, mask):
        return lax.ppermute(v, "tp", [(t, t ^ mask) for t in range(self.tp)])

    def hi_swap(self, v):
        return lax.all_to_all(v, "fsdp", 0, 0, axis_index_groups=self.hi_groups)

    def hi_copies(self, w):
        return self.hi_swap(jnp.broadcast_to(w[None], (self.hi,) + w.shape))

    def lo_gather(self, v):
        return tuple(self.lo_shift(v, -s) for s in range(1, self.lo))

    def lo_scatter(self, v):
        m = v.shape[0] // (self.lo - 1)
        return tuple(self.lo_shift(v[s * m : (s + 1) * m], s + 1) for s in range(self.lo - 1))

    def hi_gather(self, v):
        return tuple(self.hi_shift(v, s) for s in range(1, self.hi))

    def hi_scatter(self, v):
        m = v.shape[0] // (self.hi - 1)
        return tuple(self.hi_shift(v[s * m : (s + 1) * m], -s - 1) for s in range(self.hi - 1))

    def turned_lo(self, parts, start):
        if self.lo == 2:
            return [jnp.where(start == 0, parts[0], parts[1]), jnp.where(start == 0, parts[1], parts[0])]
        both = jnp.concatenate([part[None] for part in parts + parts], axis=0)
        both = lax.dynamic_slice_in_dim(both, start, self.lo, axis=0)
        return [both[s] for s in range(self.lo)]

    def to_pieces(self, v):
        n = v.shape[1] // self.shards
        b = lax.axis_index("fsdp") % self.lo
        parts = [
            jnp.concatenate([v[:, (h * self.lo + l) * n : (h * self.lo + l + 1) * n] for h in range(self.hi)], axis=1)
            for l in range(self.lo)
        ]
        return jnp.concatenate(self.turned_lo(parts, b), axis=1)

    def from_pieces(self, v):
        n = v.shape[1] // self.shards
        b = lax.axis_index("fsdp") % self.lo
        own = self.hi * n
        parts = [v[:, s * own : (s + 1) * own] for s in range(self.lo)]
        parts = self.turned_lo(parts, (self.lo - b) % self.lo)
        return jnp.concatenate(
            [parts[l][:, h * n : (h + 1) * n] for h in range(self.hi) for l in range(self.lo)], axis=1
        )

    def quarters(self, w):
        n, k = w.shape
        chunk = -(-k // (self.hi * 128)) * 128
        w = jnp.pad(w, ((0, 0), (0, self.hi * chunk - k)))
        return w.reshape(n, self.hi, chunk).transpose(1, 0, 2)


def kernel_call(kernel, outs, args, flops, scratch=(), limit=16):
    return pl.pallas_call(
        kernel,
        out_shape=outs,
        in_specs=[VMEM_SPEC] * len(args),
        out_specs=jax.tree.map(lambda _: VMEM_SPEC, outs),
        scratch_shapes=list(scratch),
        compiler_params=pltpu.CompilerParams(vmem_limit_bytes=limit * MIB),
        cost_estimate=NOTHING,
    )(*args)


def shape(dims, kind):
    return jax.ShapeDtypeStruct(tuple(dims), kind)


def flat(pieces):
    return [p.reshape(-1, p.shape[-1]) for p in pieces]


def through(x_ref, pieces):
    depth = x_ref.shape[1] // len(pieces)
    total = None
    for s, piece in enumerate(pieces):
        part = product(x_ref[:, s * depth : (s + 1) * depth], piece[...])
        total = part if total is None else total + part
    return total


def turned(v, cosine, signed):
    return v * cosine + pltpu.roll(v, HEAD_DIM // 2, 1) * signed


def key_value(x, pieces, cosine, signed):
    def kernel(x_ref, *refs):
        *ws, cos_ref, sin_ref, out_ref = refs
        raw = through(x_ref, ws)
        out_ref[:, :HEAD_DIM] = turned(raw[:, :HEAD_DIM], cos_ref[...], sin_ref[...]).astype(BF16)
        out_ref[:, HEAD_DIM:] = raw[:, HEAD_DIM:].astype(BF16)

    rows, k = x.shape[0], pieces[0].shape[1]
    return kernel_call(kernel, shape((rows, k), BF16), (x, *pieces, cosine, signed), 2 * rows * k * x.shape[1])


def query(x, pieces, cosine, signed):
    def kernel(x_ref, *refs):
        *ws, cos_ref, sin_ref, out_ref = refs
        raw = through(x_ref, ws)
        for c in range(0, out_ref.shape[1], HEAD_DIM):
            cols = slice(c, c + HEAD_DIM)
            out_ref[:, cols] = turned(raw[:, cols], cos_ref[...], sin_ref[...]).astype(BF16)

    rows, k = x.shape[0], pieces[0].shape[1]
    return kernel_call(kernel, shape((rows, k), BF16), (x, *pieces, cosine, signed), 2 * rows * k * x.shape[1])


def project(x, pieces):
    def kernel(x_ref, *refs):
        *ws, out_ref = refs
        out_ref[...] = through(x_ref, ws).astype(BF16)

    rows, k = x.shape[0], pieces[0].shape[1]
    return kernel_call(kernel, shape((rows, k), BF16), (x, *pieces), 2 * rows * k * x.shape[1])


def expand(terms, extra=None):
    rows = terms[0][0].shape[0]
    half = rows // 2
    lo = len(terms[0][1])
    depth = terms[0][1][0].shape[0]
    width = lo * depth

    def kernel(*refs):
        keep_ref, send_ref = refs[-2:]
        groups = [refs[g * (lo + 1) : (g + 1) * (lo + 1)] for g in range(len(terms))]
        for s in range(lo):
            cols = slice(s * depth, (s + 1) * depth)
            total = None
            for group in groups:
                part = against(group[0][...], group[1 + s][...])
                total = part if total is None else total + part
            keep_ref[:, cols] = total[:half]
            send_ref[:, cols] = total[half:].astype(BF16)

    flops = sum(2 * rows * t[0].shape[1] * width for t in terms)
    args = tuple(a for t in terms for a in (t[0], *t[1]))
    return kernel_call(kernel, (shape((half, width), F32), shape((half, width), BF16)), args, flops)


def feed_forward(x, gates, ups):
    rows = x.shape[0]
    lo = len(gates) // 2
    chunk = gates[0].shape[1]

    def kernel(x_ref, *refs):
        gate_ref, up_ref, hidden_ref = refs[-3:]
        for side in range(2):
            cols = slice(side * chunk, (side + 1) * chunk)
            gate = through(x_ref, refs[side * lo : (side + 1) * lo])
            up = through(x_ref, refs[(2 + side) * lo : (3 + side) * lo])
            gate_ref[:, cols] = gate
            up_ref[:, cols] = up
            hidden_ref[:, cols] = (gate * jax.nn.sigmoid(gate) * up).astype(BF16)

    dims = (rows, 2 * chunk)
    outs = (shape(dims, F32), shape(dims, F32), shape(dims, BF16))
    return kernel_call(kernel, outs, (x, *gates, *ups), 8 * rows * chunk * x.shape[1])


def feed_back(d, downs, gate, up):
    rows, width = gate.shape
    chunk = width // 2
    lo = len(downs) // 2

    def kernel(d_ref, *refs):
        gate_ref, up_ref, dgate_ref, dup_ref = refs[-4:]
        for side in range(2):
            cols = slice(side * chunk, (side + 1) * chunk)
            gates = gate_ref[:, cols]
            sigma = jax.nn.sigmoid(gates)
            scaled = through(d_ref, refs[side * lo : (side + 1) * lo]) * sigma
            dgate_ref[:, cols] = (scaled * up_ref[:, cols] * (1.0 + gates * (1.0 - sigma))).astype(BF16)
            dup_ref[:, cols] = (scaled * gates).astype(BF16)

    dims = (rows, width)
    return kernel_call(
        kernel, (shape(dims, BF16), shape(dims, BF16)), (d, *downs, gate, up), 4 * rows * chunk * d.shape[1]
    )


def weight_sums(x, d, first, k, lo, extra=None):
    rows, width = x.shape
    own = width // lo

    def kernel(x_ref, d_ref, *refs):
        keep_ref, send_ref = refs[-2:]
        dcols = d_ref[:, first : first + k]
        for s in range(lo):
            part = slice(s * own, (s + 1) * own)
            total = outer_sum(x_ref[:, part], dcols)
            if extra is not None:
                total = total + refs[0][part, :].astype(F32)
            if s == 0:
                keep_ref[...] = total
            else:
                send_ref[(s - 1) * own : s * own, :] = total.astype(BF16)

    args = (x, d) + (() if extra is None else (extra,))
    outs = (shape((own, k), F32), shape((width - own, k), BF16))
    return kernel_call(kernel, outs, args, 2 * rows * k * width)


def weight_sums_sent(x, d, first, k):
    def kernel(x_ref, d_ref, out_ref):
        out_ref[...] = outer_sum(x_ref[...], d_ref[:, first : first + k]).astype(BF16)

    rows, width = x.shape
    return kernel_call(kernel, shape((width, k), BF16), (x, d), 2 * rows * k * width)


def tie(*values):
    return lax.optimization_barrier(values)


def local(
    ex,
    tokens,
    cotangent,
    doc_starts,
    skip_flags,
    gain_attn,
    w_query,
    w_key,
    w_value,
    w_out,
    gain_mlp,
    w_gate,
    w_up,
    w_down,
):
    count, width = tokens.shape
    q_width = w_query.shape[1]
    k_width = w_key.shape[1]
    hidden_width = w_gate.shape[1]
    n = w_gate.shape[0]
    chunk = -(-hidden_width // (ex.hi * 128)) * 128
    block_rows = count * ex.tp
    fsdp = lax.axis_index("fsdp")
    tp = lax.axis_index("tp")
    offsets = jnp.arange(count, dtype=jnp.int32)
    koff = jnp.concatenate([(tp ^ m) * count + offsets for m in (0, 2, 1, 3)])


    def gained(w, gain):
        return (w.astype(F32) * gain.astype(F32)[:, None]).astype(BF16)

    def normed(x):
        x = x.astype(F32)
        return x, lax.rsqrt(jnp.mean(x * x, axis=-1, keepdims=True) + EPS)

    def rows_of(doc_starts, skip_flags):
        row_index = fsdp * block_rows + koff
        begins, keep_rows = documents(doc_starts, skip_flags, row_index)
        cosine, sine = angles(row_index - begins, HEAD_DIM)
        half = HEAD_DIM // 2
        signed = jnp.concatenate([-sine[:, :half], sine[:, half:]], axis=1)
        bounds = jnp.stack([jnp.min(begins) // block_rows, fsdp, fsdp % ex.lo]).astype(jnp.int32)
        return cosine, signed, row_index[None, :], begins[None, :], bounds, keep_rows[:count, None]

    def cotangents(cotangent, keep):
        cot = ex.to_pieces(cotangent)
        return cot, (keep * cot.astype(F32)).astype(BF16)

    def joined(v, *got):
        return jnp.concatenate([v, *got], axis=0)

    def normed_rows(first, got):
        x, scale = normed(joined(first, got))
        return (x * scale).astype(BF16)

    def attention(qu, own_piece, others, qrow, beg, bounds):
        kv_all = jnp.concatenate(flat((own_piece, *others)), axis=0)
        attended, lse = attend(bounds, qu, kv_all, qrow, beg, koff[:, None], ex.lo)
        return attended, lse, kv_all

    def attention_back(qu, kva, att, datt, lse, qrow, beg, bounds, cosine, signed):
        dq, dkv = attend_back(bounds, qu, kva, att, datt, lse, qrow, beg, koff[:, None], cosine, signed, ex.lo)
        m = dkv.shape[0] // ex.lo
        return dq, dkv[:m], dkv[m:]

    def halves(keep, got):
        g = keep + got.astype(F32)
        return g[: g.shape[0] // 2], g[g.shape[0] // 2 :].astype(BF16)

    def first_block(keep, got):
        g = keep + got.astype(F32)
        return g[:count], g[count:].astype(BF16)

    def summed(kept, got):
        for v in got:
            kept = kept + v.astype(F32)
        return kept

    def middle_of(kept, got, tok, keep):
        middle, scale = normed(tok.astype(F32) + keep * (kept + got.astype(F32)))
        return middle, (middle * scale).astype(BF16)

    def sides(p0, p1, p2, p3):
        return flat((p0, *p1, p2, *p3))

    def feed_back_rows(dgate, dup, *ws):
        gates, ups = sides(*ws[:4]), sides(*ws[4:])
        return expand(
            [
                (dgate[:, :chunk], gates[: ex.lo]),
                (dgate[:, chunk:], gates[ex.lo :]),
                (dup[:, :chunk], ups[: ex.lo]),
                (dup[:, chunk:], ups[ex.lo :]),
            ]
        )

    def down_rows(hid, *ws):
        downs = sides(*ws)
        return expand([(hid[:, :chunk], downs[: ex.lo]), (hid[:, chunk:], downs[ex.lo :])])

    def layer_rows(kept, got, middle, keep):
        return ex.from_pieces((middle + keep * summed(kept, got)).astype(BF16))

    def middle_back(kept, got, middle, cot, keep):
        scaled = summed(kept, got)
        scale = normed(middle)[1]
        d_middle = (
            cot.astype(F32)
            + scale * scaled
            - middle * scale**3 * jnp.mean(scaled * middle, axis=-1, keepdims=True)
        )
        return d_middle, (keep * d_middle).astype(BF16)

    def lo_total(kept, got):
        total = summed(kept.astype(F32), got).astype(BF16)
        return total.reshape(ex.hi, -1, total.shape[1])

    def hi_total(got):
        return jnp.sum(got.astype(F32), axis=0)

    def spread(got):
        return jnp.concatenate([got[h] for h in range(ex.hi)], axis=1)[:, :hidden_width].astype(F32)

    def spread_gained(got, w, gain):
        total = spread(got)
        return total * gain.astype(F32)[:, None], jnp.sum(total * w.astype(F32), axis=1)

    def query_grads(got, gain):
        return hi_total(got) * gain.astype(F32)[:, None]

    def key_grads(got, gain):
        total = query_grads(got, gain)
        return total[:, :k_width], total[:, k_width:]

    def keys_back(got, cosine, signed):
        total = hi_total(got)
        half = k_width // 2
        dk = total[:, :k_width]
        turned_back = dk * cosine - jnp.concatenate([dk[:, half:], dk[:, :half]], axis=1) * signed
        return jnp.concatenate([turned_back, total[:, k_width:]], axis=1).astype(BF16)

    def attention_rows_back(dq, q0, q1, dkv, kv0, kv1):
        return expand([(dq, flat((q0, *q1))), (dkv, flat((kv0, *kv1)))])

    def tokens_back(kept, got, tok, d_mid):
        scaled = kept + got.astype(F32)
        x, scale = normed(tok)
        d_tokens = d_mid + scale * scaled - x * scale**3 * jnp.mean(scaled * x, axis=-1, keepdims=True)
        sums = jnp.sum(scaled * x * scale, axis=0, keepdims=True)
        return ex.from_pieces(d_tokens.astype(BF16)), ex.from_pieces(sums).reshape(ex.shards, n)

    def gain_sums(got, gain, sum_g, sum_u):
        return jnp.stack([jnp.sum(got, axis=0) / gain.astype(F32), sum_g + sum_u])


    w_query, gain_attn = tie(w_query, gain_attn)
    s_q = gained(w_query, gain_attn)
    q0 = ex.hi_copies(s_q)
    w_key, w_value, gain_attn = tie(w_key, w_value, gain_attn)
    s_kv = gained(jnp.concatenate([w_key, w_value], axis=1), gain_attn)
    s_kv, tokens = tie(s_kv, tokens)
    tok = ex.to_pieces(tokens)
    tok_x = ex.flip(tok, 2)
    tok, w_gate, gain_mlp = tie(tok, w_gate, gain_mlp)
    s_g = ex.quarters(gained(w_gate, gain_mlp))
    s_g, doc_starts, skip_flags = tie(s_g, doc_starts, skip_flags)
    cosine, signed, qrow, beg, bounds, keep = rows_of(doc_starts, skip_flags)
    keep, tok_x = tie(keep, tok_x)
    tok_x, tok = tie(tok_x, tok)
    tok2 = joined(tok, tok_x)
    tok_c = ex.flip(tok2, 1)
    tok2, w_out = tie(tok2, w_out)
    s_o = w_out.T
    s_o, tok_c = tie(s_o, tok_c)
    tok_c, tok2 = tie(tok_c, tok2)
    xh = normed_rows(tok2, tok_c)
    xh, s_kv = tie(xh, s_kv)
    kv0 = ex.hi_copies(s_kv)
    xh, q0 = tie(xh, q0)
    q1 = ex.lo_gather(q0)
    q0, w_up, gain_mlp = tie(q0, w_up, gain_mlp)
    s_u = ex.quarters(gained(w_up, gain_mlp))
    s_u, w_down = tie(s_u, w_down)
    s_d = ex.quarters(w_down.T)
    s_d, s_u = tie(s_d, s_u)
    u0 = ex.hi_swap(s_u)
    s_d, kv0 = tie(s_d, kv0)
    kv0, cotangent, keep = tie(kv0, cotangent, keep)
    cot, dm_own = cotangents(cotangent, keep)
    dm_own, q1 = tie(dm_own, q1)
    q1, kv0 = tie(q1, kv0)
    kv1 = ex.lo_gather(kv0)
    q1, s_o = tie(q1, s_o)
    o0 = ex.hi_copies(s_o)
    q1, u0 = tie(q1, u0)
    u2 = ex.flip(u0, 2)
    u0, xh, q0, q1, cosine, signed = tie(u0, xh, q0, q1, cosine, signed)
    qu = query(xh, flat((q0, *q1)), cosine, signed)
    qu, kv1 = tie(qu, kv1)
    kv1, u0 = tie(kv1, u0)
    u1 = ex.lo_gather(u0)
    kv1, xh, kv0, cosine, signed = tie(kv1, xh, kv0, cosine, signed)
    kv = key_value(xh, flat((kv0, *kv1)), cosine, signed)
    kv, u2 = tie(kv, u2)
    u2, kv = tie(u2, kv)
    kr0 = ex.hi_copies(kv)
    u2, o0 = tie(u2, o0)
    o0, u1 = tie(o0, u1)
    u1, o0 = tie(u1, o0)
    o1 = ex.lo_gather(o0)
    u3 = tuple(ex.flip(v, 2) for v in u1)
    u1, kr0 = tie(u1, kr0)
    kr0, s_g = tie(kr0, s_g)
    g0 = ex.hi_swap(s_g)
    kr0, u3 = tie(kr0, u3)
    u3, o1 = tie(u3, o1)
    o1, kr0 = tie(o1, kr0)
    kr1 = ex.lo_gather(kr0)
    o1, dm_own = tie(o1, dm_own)
    dm_z = ex.hi_gather(dm_own)
    o1, g0 = tie(o1, g0)
    g2 = ex.flip(g0, 2)
    g0, kr1 = tie(g0, kr1)
    kr1, g0 = tie(kr1, g0)
    g1 = ex.lo_gather(g0)
    kr1, qu, kr0, qrow, beg, bounds = tie(kr1, qu, kr0, qrow, beg, bounds)
    att, lse, kva = attention(qu, kr0, kr1, qrow, beg, bounds)
    kva, g2 = tie(kva, g2)
    g2, dm_z = tie(g2, dm_z)
    dm_z, g1 = tie(dm_z, g1)
    g3 = tuple(ex.flip(v, 2) for v in g1)
    g1, s_d = tie(g1, s_d)
    d0 = ex.hi_swap(s_d)
    g1, att, o0, o1 = tie(g1, att, o0, o1)
    ao_k, ao_s = expand([(att, flat((o0, *o1)))])
    ao_r = ex.flip(ao_s, 1)
    ao_k, dm_own, dm_z = tie(ao_k, dm_own, dm_z)
    dm4 = joined(dm_own, *dm_z)
    dm_c = ex.flip(dm4, 1)
    dm4, ao_r = tie(dm4, ao_r)
    ao_r, ao_k = tie(ao_r, ao_k)
    ao_k2, ao_s2 = halves(ao_k, ao_r)
    ao_s2, dm_c = tie(ao_s2, dm_c)
    dm_c, dm4 = tie(dm_c, dm4)
    dm = joined(dm4, dm_c)
    dm, g3 = tie(dm, g3)
    g3, ao_s2 = tie(g3, ao_s2)
    ao_r2 = ex.flip(ao_s2, 2)
    g3, d0 = tie(g3, d0)
    d1 = ex.lo_gather(d0)
    d2 = ex.flip(d0, 2)
    d0, ao_r2 = tie(d0, ao_r2)
    ao_r2, ao_k2, tok, keep = tie(ao_r2, ao_k2, tok, keep)
    middle, nrm = middle_of(ao_k2, ao_r2, tok, keep)
    nrm_z = ex.hi_gather(nrm)
    nrm, d1 = tie(nrm, d1)
    d3 = tuple(ex.flip(v, 2) for v in d1)
    d1, d2 = tie(d1, d2)
    d2, nrm_z = tie(d2, nrm_z)
    nrm_z, nrm = tie(nrm_z, nrm)
    nm4 = joined(nrm, *nrm_z)
    nm_c = ex.flip(nm4, 1)
    nm4, d3 = tie(nm4, d3)
    d3, nm_c = tie(d3, nm_c)
    nm_c, nm4 = tie(nm_c, nm4)
    nm = joined(nm4, nm_c)
    nm, g0, g1, g2, g3, u0, u1, u2, u3 = tie(nm, g0, g1, g2, g3, u0, u1, u2, u3)
    gate, up, hid = feed_forward(nm, sides(g0, g1, g2, g3), sides(u0, u1, u2, u3))
    hid, dm, d0, d1, d2, d3, gate, up = tie(hid, dm, d0, d1, d2, d3, gate, up)
    dgate, dup = feed_back(dm, sides(d0, d1, d2, d3), gate, up)
    dup, nm = tie(dup, nm)
    gu_x = weight_sums_sent(nm, dup, chunk, chunk)
    gu_r = ex.flip(gu_x, 2)
    dup, dgate, g0, g1, g2, g3, u0, u1, u2, u3 = tie(dup, dgate, g0, g1, g2, g3, u0, u1, u2, u3)
    e_k, e_s = feed_back_rows(dgate, dup, g0, g1, g2, g3, u0, u1, u2, u3)
    c3_r = ex.flip(e_s, 1)
    e_k, dm, hid = tie(e_k, dm, hid)
    gd_x = weight_sums_sent(dm, hid, chunk, chunk)
    gd_x, hid, d0, d1, d2, d3 = tie(gd_x, hid, d0, d1, d2, d3)
    m_k, m_s = down_rows(hid, d0, d1, d2, d3)
    m_s, c3_r = tie(m_s, c3_r)
    c3_r, m_s = tie(c3_r, m_s)
    mo_r = ex.flip(m_s, 1)
    c3_r, e_k = tie(c3_r, e_k)
    c3_k, c3_s = first_block(e_k, c3_r)
    c3_z = ex.hi_scatter(c3_s)
    c3_k, mo_r = tie(c3_k, mo_r)
    mo_r, m_k = tie(mo_r, m_k)
    mo_k, mo_s = first_block(m_k, mo_r)
    mo_s, nm, dgate = tie(mo_s, nm, dgate)
    gg_x = weight_sums_sent(nm, dgate, chunk, chunk)
    gg_x, gu_r = tie(gg_x, gu_r)
    gu_r, gd_x = tie(gu_r, gd_x)
    gd_r = ex.flip(gd_x, 2)
    gu_r, nm, dup = tie(gu_r, nm, dup)
    gu_k, gu_s = weight_sums(nm, dup, 0, chunk, ex.lo, gu_r)
    gu_y = ex.lo_scatter(gu_s)
    gu_k, mo_s = tie(gu_k, mo_s)
    mo_z = ex.hi_scatter(mo_s)
    gu_k, c3_z = tie(gu_k, c3_z)
    c3_z, c3_k, middle, cot, keep = tie(c3_z, c3_k, middle, cot, keep)
    d_mid, da_own = middle_back(c3_k, c3_z, middle, cot, keep)
    da_own, gu_y = tie(da_own, gu_y)
    gu_y, gu_k = tie(gu_y, gu_k)
    gu_l = lo_total(gu_k, gu_y)
    gu_l, mo_z = tie(gu_l, mo_z)
    mo_z, gu_l = tie(mo_z, gu_l)
    gu_z = ex.hi_swap(gu_l)
    mo_z, gd_r = tie(mo_z, gd_r)
    gd_r, da_own = tie(gd_r, da_own)
    da_x = ex.flip(da_own, 2)
    gd_r, dm, hid = tie(gd_r, dm, hid)
    gd_k, gd_s = weight_sums(dm, hid, 0, chunk, ex.lo, gd_r)
    gd_y = ex.lo_scatter(gd_s)
    gd_k, mo_k, mo_z, middle, keep = tie(gd_k, mo_k, mo_z, middle, keep)
    layer_out = layer_rows(mo_k, mo_z, middle, keep)
    layer_out, gg_x = tie(layer_out, gg_x)
    gg_r = ex.flip(gg_x, 2)
    layer_out, da_x = tie(layer_out, da_x)
    da_x, da_own = tie(da_x, da_own)
    da2 = joined(da_own, da_x)
    da_c = ex.flip(da2, 1)
    da2, da_c = tie(da2, da_c)
    da_c, da2 = tie(da_c, da2)
    da = joined(da2, da_c)
    da, o0, o1 = tie(da, o0, o1)
    datt = project(da, flat((o0, *o1)))
    (
        datt,
        qu,
        kva,
        att,
        lse,
        qrow,
        beg,
        bounds,
        cosine,
        signed,
    ) = tie(
        datt,
        qu,
        kva,
        att,
        lse,
        qrow,
        beg,
        bounds,
        cosine,
        signed,
    )
    dq, dk_k, dk_s = attention_back(qu, kva, att, datt, lse, qrow, beg, bounds, cosine, signed)
    dk_s, gu_z = tie(dk_s, gu_z)
    gu_z, gd_y = tie(gu_z, gd_y)
    gd_y, dk_s = tie(gd_y, dk_s)
    dk_y = ex.lo_scatter(dk_s)
    gd_y, gd_k = tie(gd_y, gd_k)
    gd_l = lo_total(gd_k, gd_y)
    gd_z = ex.hi_swap(gd_l)
    gu_z, gg_r = tie(gu_z, gg_r)
    gg_r, nm, dgate = tie(gg_r, nm, dgate)
    gg_k, gg_s = weight_sums(nm, dgate, 0, chunk, ex.lo, gg_r)
    gg_s, xh, dq = tie(gg_s, xh, dq)
    gq_k, gq_s = weight_sums(xh, dq, 0, q_width, ex.lo)
    gq_s, da, att = tie(gq_s, da, att)
    go_k, go_s = weight_sums(da, att, 0, q_width, ex.lo)
    go_s, gg_s = tie(go_s, gg_s)
    gg_y = ex.lo_scatter(gg_s)
    go_s, dk_y = tie(go_s, dk_y)
    dk_y, dk_k = tie(dk_y, dk_k)
    dk_l = lo_total(dk_k, dk_y)
    dk_l, gu_z, w_up, gain_mlp = tie(dk_l, gu_z, w_up, gain_mlp)
    grad_up, sum_u = spread_gained(gu_z, w_up, gain_mlp)
    sum_u, gd_z = tie(sum_u, gd_z)
    gd_z, dk_l = tie(gd_z, dk_l)
    dk_z = ex.hi_swap(dk_l)
    gd_z, gq_s = tie(gd_z, gq_s)
    gq_y = ex.lo_scatter(gq_s)
    gd_z, gg_y = tie(gd_z, gg_y)
    gg_y, gd_z = tie(gg_y, gd_z)
    grad_down = spread(gd_z).T
    grad_down, gg_k, gg_y = tie(grad_down, gg_k, gg_y)
    gg_l = lo_total(gg_k, gg_y)
    gg_z = ex.hi_swap(gg_l)
    grad_down, dk_z = tie(grad_down, dk_z)
    dk_z, cosine, signed = tie(dk_z, cosine, signed)
    dkv = keys_back(dk_z, cosine, signed)
    dkv, dq, q0, q1, kv0, kv1 = tie(dkv, dq, q0, q1, kv0, kv1)
    n_k, n_s = attention_rows_back(dq, q0, q1, dkv, kv0, kv1)
    n_r = ex.flip(n_s, 1)
    n_k, xh, dkv = tie(n_k, xh, dkv)
    gk_k, gk_s = weight_sums(xh, dkv, 0, 2 * k_width, ex.lo)
    gk_s, n_r = tie(gk_s, n_r)
    n_r, n_k = tie(n_r, n_k)
    n_k2, n_s2 = halves(n_k, n_r)
    n_r2 = ex.flip(n_s2, 2)
    n_k2, go_s = tie(n_k2, go_s)
    go_y = ex.lo_scatter(go_s)
    n_k2, gq_y = tie(n_k2, gq_y)
    gq_y, gq_k = tie(gq_y, gq_k)
    gq_l = lo_total(gq_k, gq_y)
    gq_z = ex.hi_swap(gq_l)
    n_k2, n_r2 = tie(n_k2, n_r2)
    n_r2, gg_z = tie(n_r2, gg_z)
    gg_z, w_gate, gain_mlp = tie(gg_z, w_gate, gain_mlp)
    grad_gate, sum_g = spread_gained(gg_z, w_gate, gain_mlp)
    sum_g, n_k2, n_r2, tok, d_mid = tie(sum_g, n_k2, n_r2, tok, d_mid)
    d_tokens, sums = tokens_back(n_k2, n_r2, tok, d_mid)
    sums, go_y = tie(sums, go_y)
    go_y, gk_s = tie(go_y, gk_s)
    gk_y = ex.lo_scatter(gk_s)
    go_y, go_k = tie(go_y, go_k)
    go_l = lo_total(go_k, go_y)
    go_l, sums = tie(go_l, sums)
    sums_z = lax.all_to_all(sums, "fsdp", 0, 0)
    go_l, gq_z = tie(go_l, gq_z)
    gq_z, go_l = tie(gq_z, go_l)
    go_z = ex.hi_swap(go_l)
    gq_z, sums_z = tie(gq_z, sums_z)
    sums_z, gq_z, gain_attn = tie(sums_z, gq_z, gain_attn)
    grad_query = query_grads(gq_z, gain_attn)
    grad_query, gk_y = tie(grad_query, gk_y)
    gk_y, sums_z, gain_attn, sum_g, sum_u = tie(gk_y, sums_z, gain_attn, sum_g, sum_u)
    gains = gain_sums(sums_z, gain_attn, sum_g, sum_u)
    gains_x = ex.flip(gains, 2)
    gains, gk_k, gk_y = tie(gains, gk_k, gk_y)
    gk_l = lo_total(gk_k, gk_y)
    gk_l, gains_x = tie(gk_l, gains_x)
    gains_x, gains = tie(gains_x, gains)
    gains2 = gains + gains_x
    gains_c = ex.flip(gains2, 1)
    gains2, gains_c = tie(gains2, gains_c)
    gains_c, gains2 = tie(gains_c, gains2)
    grad_gain_attn, grad_gain_mlp = gains2 + gains_c
    grad_gain_mlp, go_z = tie(grad_gain_mlp, go_z)
    go_z, gk_l = tie(go_z, gk_l)
    gk_z = ex.hi_swap(gk_l)
    grad_out = hi_total(go_z).T
    grad_out, gk_z = tie(grad_out, gk_z)
    gk_z, gain_attn = tie(gk_z, gain_attn)
    grad_key, grad_value = key_grads(gk_z, gain_attn)
    return (
        layer_out,
        d_tokens,
        grad_gain_attn,
        grad_query,
        grad_key,
        grad_value,
        grad_out,
        grad_gain_mlp,
        grad_gate,
        grad_up,
        grad_down,
    )


def solution(mesh):
    rows = P(("fsdp", "tp"), None)
    in_specs = (
        rows,
        rows,
        P(),
        P(),
        P("fsdp"),
        P("fsdp", "tp"),
        P("fsdp", "tp"),
        P("fsdp", "tp"),
        P("tp", "fsdp"),
        P("fsdp"),
        P("fsdp", "tp"),
        P("fsdp", "tp"),
        P("tp", "fsdp"),
    )
    out_specs = (
        rows,
        rows,
        P("fsdp"),
        P("fsdp", "tp"),
        P("fsdp", "tp"),
        P("fsdp", "tp"),
        P("tp", "fsdp"),
        P("fsdp"),
        P("fsdp", "tp"),
        P("fsdp", "tp"),
        P("tp", "fsdp"),
    )
    return jax.shard_map(
        functools.partial(local, Exchange(mesh)), mesh=mesh, in_specs=in_specs, out_specs=out_specs, check_vma=False
    )
```

```python
import functools

import jax
import jax.numpy as jnp
from jax import lax
from jax.experimental import pallas as pl
from jax.experimental.pallas import tpu as pltpu
from jax.sharding import PartitionSpec as P

HEAD_DIM = 128
EPS = 1e-05
THETA = 10000.0
FLOOR = -1e30
LOG2E = 1.4426950408889634
MIB = 1024 * 1024
F32 = jnp.float32
BF16 = jnp.bfloat16
HI = 4


def angles(places, width):
    half = width // 2
    freq = 1.0 / THETA ** (jnp.arange(half, dtype=F32) * 2.0 / width)
    angle = places.astype(F32)[:, None] * freq[None, :]
    cosine = jnp.cos(angle)
    sine = jnp.sin(angle)
    return (jnp.concatenate([cosine, cosine], -1), jnp.concatenate([sine, sine], -1))


def documents(doc_starts, skip_flags, row_index):
    inside = doc_starts[None, :] <= row_index[:, None]
    segment = jnp.sum(inside.astype(jnp.int32), axis=1) - 1
    begins = jnp.max(jnp.where(inside, doc_starts[None, :], 0), axis=1)
    chosen = segment[:, None] == jnp.arange(doc_starts.shape[0], dtype=jnp.int32)[None, :]
    skipped = jnp.sum(jnp.where(chosen, skip_flags[None, :], 0), axis=1)
    return (begins, (1 - skipped).astype(F32))


def product(left, right):
    return jnp.dot(left, right, preferred_element_type=F32)


def against(left, right):
    return lax.dot_general(left, right, (((1,), (1,)), ((), ())), preferred_element_type=F32)


def outer_sum(left, right):
    return lax.dot_general(left, right, (((0,), (0,)), ((), ())), preferred_element_type=F32)


def block_rows_of(block, bounds, lo, size):
    piece = lax.rem(lax.rem(block, lo) - bounds[2] + lo, lo)
    place = piece * HI + lax.div(block, lo)
    return pl.ds(pl.multiple_of(place * size, size), size)


def closed_keys(block, size, koff_ref, qrow_ref, beg_ref):
    krow = koff_ref[...] + block * size
    return jnp.where((krow <= qrow_ref[...]) & (krow >= beg_ref[...]), 0.0, FLOOR)


def attend_kernel(heads, lo, bounds, q_ref, kv_ref, qrow_ref, beg_ref, koff_ref, o_ref, lse_ref, top, mass, acc):
    size = koff_ref.shape[0]
    factor = HEAD_DIM**-0.5 * LOG2E
    top[...] = jnp.full_like(top, FLOOR)
    mass[...] = jnp.zeros_like(mass)
    acc[...] = jnp.zeros_like(acc)

    def step(block, carry):
        rows = block_rows_of(block, bounds, lo, size)
        keys = kv_ref[rows, :HEAD_DIM]
        values = kv_ref[rows, HEAD_DIM:].astype(F32).T.astype(BF16)
        closed = closed_keys(block, size, koff_ref, qrow_ref, beg_ref)
        for h in range(heads):
            scores = against(keys, q_ref[:, h * HEAD_DIM : (h + 1) * HEAD_DIM]) * factor + closed
            before = top[h]
            now = jnp.maximum(before, jnp.max(scores, axis=0, keepdims=True))
            weights = jnp.exp2(scores - now)
            fading = jnp.exp2(before - now)
            top[h] = now
            mass[h] = mass[h] * fading + jnp.sum(weights, axis=0, keepdims=True)
            acc[h] = acc[h] * fading + product(values, weights.astype(BF16))
        return carry

    lax.fori_loop(bounds[0], bounds[1] + 1, step, 0)
    for h in range(heads):
        o_ref[:, h * HEAD_DIM : (h + 1) * HEAD_DIM] = (acc[h] / mass[h]).T.astype(BF16)
        lse_ref[h] = top[h] + jnp.log2(mass[h])


def attend_back_kernel(
    heads, lo, bounds, q_ref, kv_ref, o_ref, do_ref, lse_ref, qrow_ref, beg_ref, koff_ref, cos_ref, sin_ref,
    dq_ref, dkv_ref, delta, acc
):
    size = koff_ref.shape[0]
    factor = HEAD_DIM**-0.5
    acc[...] = jnp.zeros_like(acc)
    dkv_ref[...] = jnp.zeros_like(dkv_ref)
    for h in range(heads):
        cols = slice(h * HEAD_DIM, (h + 1) * HEAD_DIM)
        both = do_ref[:, cols].astype(F32) * o_ref[:, cols].astype(F32)
        delta[h] = jnp.sum(both.T, axis=0, keepdims=True)

    def step(block, carry):
        rows = block_rows_of(block, bounds, lo, size)
        keys = kv_ref[rows, :HEAD_DIM]
        values = kv_ref[rows, HEAD_DIM:]
        turned_keys = keys.astype(F32).T.astype(BF16)
        closed = closed_keys(block, size, koff_ref, qrow_ref, beg_ref)
        dkeys = jnp.zeros((size, HEAD_DIM), F32)
        dvalues = jnp.zeros((size, HEAD_DIM), F32)
        for h in range(heads):
            cols = slice(h * HEAD_DIM, (h + 1) * HEAD_DIM)
            queries = q_ref[:, cols]
            grads = do_ref[:, cols]
            scores = against(keys, queries) * (factor * LOG2E) + closed
            probs = jnp.exp2(scores - lse_ref[h])
            dvalues = dvalues + product(probs.astype(BF16), grads)
            dprobs = against(values, grads)
            dscores = (probs * ((dprobs - delta[h]) * factor)).astype(BF16)
            acc[h] = acc[h] + product(turned_keys, dscores)
            dkeys = dkeys + product(dscores, queries)
        dkv_ref[rows, :HEAD_DIM] = dkeys.astype(BF16)
        dkv_ref[rows, HEAD_DIM:] = dvalues.astype(BF16)
        return carry

    lax.fori_loop(bounds[0], bounds[1] + 1, step, 0)
    for h in range(heads):
        grads = acc[h].T
        back = grads * cos_ref[...] - pltpu.roll(grads, HEAD_DIM // 2, 1) * sin_ref[...]
        dq_ref[:, h * HEAD_DIM : (h + 1) * HEAD_DIM] = back.astype(BF16)


VMEM_SPEC = pl.BlockSpec(memory_space=pltpu.VMEM)
SMEM_SPEC = pl.BlockSpec(memory_space=pltpu.SMEM)
NOTHING = pl.CostEstimate(flops=1, bytes_accessed=1, transcendentals=0)


def attend(bounds, q, kv, qrow, beg, koff, lo):
    rows, width = q.shape
    heads = width // HEAD_DIM
    return pl.pallas_call(
        functools.partial(attend_kernel, heads, lo),
        out_shape=(
            jax.ShapeDtypeStruct((rows, width), BF16),
            jax.ShapeDtypeStruct((heads, 1, rows), F32),
        ),
        in_specs=[SMEM_SPEC] + [VMEM_SPEC] * 5,
        out_specs=(VMEM_SPEC, VMEM_SPEC),
        scratch_shapes=[
            pltpu.VMEM((heads, 1, rows), F32),
            pltpu.VMEM((heads, 1, rows), F32),
            pltpu.VMEM((heads, HEAD_DIM, rows), F32),
        ],
        compiler_params=pltpu.CompilerParams(vmem_limit_bytes=16 * MIB),
        cost_estimate=NOTHING,
    )(bounds, q, kv, qrow, beg, koff)


def attend_back(bounds, q, kv, o, do, lse, qrow, beg, koff, cosine, signed, lo):
    rows, width = q.shape
    heads = width // HEAD_DIM
    return pl.pallas_call(
        functools.partial(attend_back_kernel, heads, lo),
        out_shape=(
            jax.ShapeDtypeStruct((rows, width), BF16),
            jax.ShapeDtypeStruct(kv.shape, BF16),
        ),
        in_specs=[SMEM_SPEC] + [VMEM_SPEC] * 10,
        out_specs=(VMEM_SPEC, VMEM_SPEC),
        scratch_shapes=[
            pltpu.VMEM((heads, 1, rows), F32),
            pltpu.VMEM((heads, HEAD_DIM, rows), F32),
        ],
        compiler_params=pltpu.CompilerParams(vmem_limit_bytes=16 * MIB),
        cost_estimate=NOTHING,
    )(bounds, q, kv, o, do, lse, qrow, beg, koff, cosine, signed)


class Exchange:
    def __init__(self, mesh):
        self.shards = mesh.shape["fsdp"]
        self.hi = HI
        self.lo = self.shards // HI
        self.tp = mesh.shape["tp"]
        self.hi_groups = [[h * self.lo + b for h in range(self.hi)] for b in range(self.lo)]

    def lo_shift(self, v, s):
        pairs = [
            (h * self.lo + b, h * self.lo + (b + s) % self.lo) for h in range(self.hi) for b in range(self.lo)
        ]
        return lax.ppermute(v, "fsdp", pairs)

    def flip(self, v, mask):
        return lax.ppermute(v, "tp", [(t, t ^ mask) for t in range(self.tp)])

    def hi_swap(self, v):
        return lax.all_to_all(v, "fsdp", 0, 0, axis_index_groups=self.hi_groups)

    def hi_copies(self, w):
        return self.hi_swap(jnp.broadcast_to(w[None], (self.hi,) + w.shape))

    def lo_gather(self, v):
        return tuple(self.lo_shift(v, -s) for s in range(1, self.lo))

    def lo_scatter(self, v):
        m = v.shape[0] // (self.lo - 1)
        return tuple(self.lo_shift(v[s * m : (s + 1) * m], s + 1) for s in range(self.lo - 1))

    def hi_rows(self, v):
        return self.hi_copies(v).reshape(self.hi * v.shape[0], v.shape[1])

    def turned_lo(self, parts, start):
        if self.lo == 2:
            return [jnp.where(start == 0, parts[0], parts[1]), jnp.where(start == 0, parts[1], parts[0])]
        both = jnp.concatenate([part[None] for part in parts + parts], axis=0)
        both = lax.dynamic_slice_in_dim(both, start, self.lo, axis=0)
        return [both[s] for s in range(self.lo)]

    def to_pieces(self, v):
        n = v.shape[1] // self.shards
        b = lax.axis_index("fsdp") % self.lo
        parts = [
            jnp.concatenate([v[:, (h * self.lo + l) * n : (h * self.lo + l + 1) * n] for h in range(self.hi)], axis=1)
            for l in range(self.lo)
        ]
        return jnp.concatenate(self.turned_lo(parts, b), axis=1)

    def from_pieces(self, v):
        n = v.shape[1] // self.shards
        b = lax.axis_index("fsdp") % self.lo
        own = self.hi * n
        parts = [v[:, s * own : (s + 1) * own] for s in range(self.lo)]
        parts = self.turned_lo(parts, (self.lo - b) % self.lo)
        return jnp.concatenate(
            [parts[l][:, h * n : (h + 1) * n] for h in range(self.hi) for l in range(self.lo)], axis=1
        )

    def quarters(self, w):
        n, k = w.shape
        chunk = -(-k // (self.hi * 128)) * 128
        w = jnp.pad(w, ((0, 0), (0, self.hi * chunk - k)))
        return w.reshape(n, self.hi, chunk).transpose(1, 0, 2)


def kernel_call(kernel, outs, args, flops, scratch=(), limit=16):
    return pl.pallas_call(
        kernel,
        out_shape=outs,
        in_specs=[VMEM_SPEC] * len(args),
        out_specs=jax.tree.map(lambda _: VMEM_SPEC, outs),
        scratch_shapes=list(scratch),
        compiler_params=pltpu.CompilerParams(vmem_limit_bytes=limit * MIB),
        cost_estimate=NOTHING,
    )(*args)


def shape(dims, kind):
    return jax.ShapeDtypeStruct(tuple(dims), kind)


def flat(pieces):
    return [p.reshape(-1, p.shape[-1]) for p in pieces]


def through(x_ref, pieces):
    depth = x_ref.shape[1] // len(pieces)
    total = None
    for s, piece in enumerate(pieces):
        part = product(x_ref[:, s * depth : (s + 1) * depth], piece[...])
        total = part if total is None else total + part
    return total


def turned(v, cosine, signed):
    return v * cosine + pltpu.roll(v, HEAD_DIM // 2, 1) * signed


def key_value(x, pieces, cosine, signed):
    def kernel(x_ref, *refs):
        *ws, cos_ref, sin_ref, out_ref = refs
        raw = through(x_ref, ws)
        out_ref[:, :HEAD_DIM] = turned(raw[:, :HEAD_DIM], cos_ref[...], sin_ref[...]).astype(BF16)
        out_ref[:, HEAD_DIM:] = raw[:, HEAD_DIM:].astype(BF16)

    rows, k = x.shape[0], pieces[0].shape[1]
    return kernel_call(kernel, shape((rows, k), BF16), (x, *pieces, cosine, signed), 2 * rows * k * x.shape[1])


def query(x, pieces, cosine, signed):
    def kernel(x_ref, *refs):
        *ws, cos_ref, sin_ref, out_ref = refs
        raw = through(x_ref, ws)
        for c in range(0, out_ref.shape[1], HEAD_DIM):
            cols = slice(c, c + HEAD_DIM)
            out_ref[:, cols] = turned(raw[:, cols], cos_ref[...], sin_ref[...]).astype(BF16)

    rows, k = x.shape[0], pieces[0].shape[1]
    return kernel_call(kernel, shape((rows, k), BF16), (x, *pieces, cosine, signed), 2 * rows * k * x.shape[1])


def project(x, pieces):
    def kernel(x_ref, *refs):
        *ws, out_ref = refs
        out_ref[...] = through(x_ref, ws).astype(BF16)

    rows, k = x.shape[0], pieces[0].shape[1]
    return kernel_call(kernel, shape((rows, k), BF16), (x, *pieces), 2 * rows * k * x.shape[1])


def expand(terms, extra=None):
    rows = terms[0][0].shape[0]
    half = rows // 2
    lo = len(terms[0][1])
    depth = terms[0][1][0].shape[0]
    width = lo * depth

    def kernel(*refs):
        keep_ref, send_ref = refs[-2:]
        groups = [refs[g * (lo + 1) : (g + 1) * (lo + 1)] for g in range(len(terms))]
        for s in range(lo):
            cols = slice(s * depth, (s + 1) * depth)
            total = None
            for group in groups:
                part = against(group[0][...], group[1 + s][...])
                total = part if total is None else total + part
            keep_ref[:, cols] = total[:half]
            send_ref[:, cols] = total[half:].astype(BF16)

    flops = sum(2 * rows * t[0].shape[1] * width for t in terms)
    args = tuple(a for t in terms for a in (t[0], *t[1]))
    return kernel_call(kernel, (shape((half, width), F32), shape((half, width), BF16)), args, flops)


def feed_forward(upper, lower, gates, ups):
    half, depth = upper.shape
    rows = 2 * half
    lo = len(gates) // 2
    chunk = gates[0].shape[1]

    def kernel(upper_ref, lower_ref, *refs):
        x_ref, gate_ref, up_ref, hidden_ref = refs[-4:]
        x_ref[:half] = upper_ref[...]
        x_ref[half:] = lower_ref[...]
        for side in range(2):
            cols = slice(side * chunk, (side + 1) * chunk)
            gate = through(x_ref, refs[side * lo : (side + 1) * lo])
            up = through(x_ref, refs[(2 + side) * lo : (3 + side) * lo])
            gate_ref[:, cols] = gate
            up_ref[:, cols] = up
            hidden_ref[:, cols] = (gate * jax.nn.sigmoid(gate) * up).astype(BF16)

    dims = (rows, 2 * chunk)
    outs = (shape((rows, depth), BF16), shape(dims, F32), shape(dims, F32), shape(dims, BF16))
    return kernel_call(kernel, outs, (upper, lower, *gates, *ups), 1, limit=20)


def feed_back(upper, lower, downs, gate, up):
    half, depth = upper.shape
    rows, width = gate.shape
    chunk = width // 2
    lo = len(downs) // 2

    def kernel(upper_ref, lower_ref, *refs):
        gate_ref, up_ref, d_ref, dgate_ref, dup_ref = refs[-5:]
        d_ref[:half] = upper_ref[...]
        d_ref[half:] = lower_ref[...]
        for side in range(2):
            cols = slice(side * chunk, (side + 1) * chunk)
            gates = gate_ref[:, cols]
            sigma = jax.nn.sigmoid(gates)
            scaled = through(d_ref, refs[side * lo : (side + 1) * lo]) * sigma
            dgate_ref[:, cols] = (scaled * up_ref[:, cols] * (1.0 + gates * (1.0 - sigma))).astype(BF16)
            dup_ref[:, cols] = (scaled * gates).astype(BF16)

    dims = (rows, width)
    outs = (shape((rows, depth), BF16), shape(dims, BF16), shape(dims, BF16))
    return kernel_call(kernel, outs, (upper, lower, *downs, gate, up), 1, limit=20)


def weight_sums(x, d, first, k, lo, extra=None):
    rows, width = x.shape
    own = width // lo

    def kernel(x_ref, d_ref, *refs):
        keep_ref, send_ref = refs[-2:]
        dcols = d_ref[:, first : first + k]
        for s in range(lo):
            part = slice(s * own, (s + 1) * own)
            total = outer_sum(x_ref[:, part], dcols)
            if extra is not None:
                total = total + refs[0][part, :].astype(F32)
            if s == 0:
                keep_ref[...] = total
            else:
                send_ref[(s - 1) * own : s * own, :] = total.astype(BF16)

    args = (x, d) + (() if extra is None else (extra,))
    outs = (shape((own, k), F32), shape((width - own, k), BF16))
    return kernel_call(kernel, outs, args, 2 * rows * k * width)


def weight_sums_sent(x, d, first, k):
    def kernel(x_ref, d_ref, out_ref):
        out_ref[...] = outer_sum(x_ref[...], d_ref[:, first : first + k]).astype(BF16)

    rows, width = x.shape
    return kernel_call(kernel, shape((width, k), BF16), (x, d), 2 * rows * k * width)


def tie(*values):
    return lax.optimization_barrier(values)


def local(
    ex,
    tokens,
    cotangent,
    doc_starts,
    skip_flags,
    gain_attn,
    w_query,
    w_key,
    w_value,
    w_out,
    gain_mlp,
    w_gate,
    w_up,
    w_down,
):
    count, width = tokens.shape
    q_width = w_query.shape[1]
    k_width = w_key.shape[1]
    hidden_width = w_gate.shape[1]
    n = w_gate.shape[0]
    chunk = -(-hidden_width // (ex.hi * 128)) * 128
    block_rows = count * ex.tp
    fsdp = lax.axis_index("fsdp")
    tp = lax.axis_index("tp")
    offsets = jnp.arange(count, dtype=jnp.int32)
    koff = jnp.concatenate([(tp ^ m) * count + offsets for m in (0, 2, 1, 3)])


    def gained(w, gain):
        return (w.astype(F32) * gain.astype(F32)[:, None]).astype(BF16)

    def normed(x):
        x = x.astype(F32)
        return x, lax.rsqrt(jnp.mean(x * x, axis=-1, keepdims=True) + EPS)

    def rows_of(doc_starts, skip_flags):
        row_index = fsdp * block_rows + koff
        begins, keep_rows = documents(doc_starts, skip_flags, row_index)
        cosine, sine = angles(row_index - begins, HEAD_DIM)
        half = HEAD_DIM // 2
        signed = jnp.concatenate([-sine[:, :half], sine[:, half:]], axis=1)
        bounds = jnp.stack([jnp.min(begins) // block_rows, fsdp, fsdp % ex.lo]).astype(jnp.int32)
        return cosine, signed, row_index[None, :], begins[None, :], bounds, keep_rows[:count, None]

    def cotangents(cotangent, keep):
        cot = ex.to_pieces(cotangent)
        return cot, (keep * cot.astype(F32)).astype(BF16)

    def joined(v, *got):
        return jnp.concatenate([v, *got], axis=0)

    def normed_rows(first, got):
        x, scale = normed(joined(first, got))
        return (x * scale).astype(BF16)

    def attention(qu, own_piece, others, qrow, beg, bounds):
        kv_all = jnp.concatenate(flat((own_piece, *others)), axis=0)
        attended, lse = attend(bounds, qu, kv_all, qrow, beg, koff[:, None], ex.lo)
        return attended, lse, kv_all

    def attention_back(qu, kva, att, datt, lse, qrow, beg, bounds, cosine, signed):
        dq, dkv = attend_back(bounds, qu, kva, att, datt, lse, qrow, beg, koff[:, None], cosine, signed, ex.lo)
        m = dkv.shape[0] // ex.lo
        return dq, dkv[:m], dkv[m:]

    def halves(keep, got):
        g = keep + got.astype(F32)
        return g[: g.shape[0] // 2], g[g.shape[0] // 2 :].astype(BF16)

    def added(keep, got):
        return (keep + got.astype(F32)).astype(BF16).reshape(ex.hi, count, width)

    def summed(kept, got):
        for v in got:
            kept = kept + v.astype(F32)
        return kept

    def middle_of(kept, got, tok, keep):
        middle, scale = normed(tok.astype(F32) + keep * (kept + got.astype(F32)))
        return middle, (middle * scale).astype(BF16)

    def sides(p0, p1, p2, p3):
        return flat((p0, *p1, p2, *p3))

    def feed_back_rows(dgate, dup, *ws):
        gates, ups = sides(*ws[:4]), sides(*ws[4:])
        return expand(
            [
                (dgate[:, :chunk], gates[: ex.lo]),
                (dgate[:, chunk:], gates[ex.lo :]),
                (dup[:, :chunk], ups[: ex.lo]),
                (dup[:, chunk:], ups[ex.lo :]),
            ]
        )

    def down_rows(hid, *ws):
        downs = sides(*ws)
        return expand([(hid[:, :chunk], downs[: ex.lo]), (hid[:, chunk:], downs[ex.lo :])])

    def hi_total(got):
        return jnp.sum(got.astype(F32), axis=0)

    def layer_rows(got, middle, keep):
        return ex.from_pieces((middle + keep * hi_total(got)).astype(BF16))

    def middle_back(got, middle, cot, keep):
        scaled = hi_total(got)
        scale = normed(middle)[1]
        d_middle = (
            cot.astype(F32)
            + scale * scaled
            - middle * scale**3 * jnp.mean(scaled * middle, axis=-1, keepdims=True)
        )
        return d_middle, (keep * d_middle).astype(BF16)

    def lo_total(kept, got):
        total = summed(kept.astype(F32), got).astype(BF16)
        return total.reshape(ex.hi, -1, total.shape[1])

    def spread(got):
        return jnp.concatenate([got[h] for h in range(ex.hi)], axis=1)[:, :hidden_width].astype(F32)

    def spread_gained(got, w, gain):
        total = spread(got)
        return total * gain.astype(F32)[:, None], jnp.sum(total * w.astype(F32), axis=1)

    def query_grads(got, gain, *weights):
        total = hi_total(got)
        w = jnp.concatenate(weights, axis=1).astype(F32)
        return total * gain.astype(F32)[:, None], jnp.sum(total * w, axis=1)

    def key_grads(got, gain, *weights):
        total, part = query_grads(got, gain, *weights)
        return total[:, :k_width], total[:, k_width:], part

    def keys_back(got, cosine, signed):
        total = hi_total(got)
        half = k_width // 2
        dk = total[:, :k_width]
        turned_back = dk * cosine - jnp.concatenate([dk[:, half:], dk[:, :half]], axis=1) * signed
        return jnp.concatenate([turned_back, total[:, k_width:]], axis=1).astype(BF16)

    def attention_rows_back(dq, q0, q1, dkv, kv0, kv1):
        return expand([(dq, flat((q0, *q1))), (dkv, flat((kv0, *kv1)))])

    def tokens_back(kept, got, tok, d_mid):
        scaled = kept + got.astype(F32)
        x, scale = normed(tok)
        d_tokens = d_mid + scale * scaled - x * scale**3 * jnp.mean(scaled * x, axis=-1, keepdims=True)
        return ex.from_pieces(d_tokens.astype(BF16))


    w_query, gain_attn = tie(w_query, gain_attn)
    s_q = gained(w_query, gain_attn)
    s_q, tokens = tie(s_q, tokens)
    tok = ex.to_pieces(tokens)
    tok_x = ex.flip(tok, 2)
    tok, s_q = tie(tok, s_q)
    q0 = ex.hi_copies(s_q)
    tok, w_key, w_value, gain_attn = tie(tok, w_key, w_value, gain_attn)
    s_kv = gained(jnp.concatenate([w_key, w_value], axis=1), gain_attn)
    s_kv, w_gate, gain_mlp = tie(s_kv, w_gate, gain_mlp)
    s_g = ex.quarters(gained(w_gate, gain_mlp))
    s_g, tok_x = tie(s_g, tok_x)
    tok_x, tok = tie(tok_x, tok)
    tok2 = joined(tok, tok_x)
    tok_c = ex.flip(tok2, 1)
    tok2, w_up, gain_mlp = tie(tok2, w_up, gain_mlp)
    s_u = ex.quarters(gained(w_up, gain_mlp))
    s_u, w_out = tie(s_u, w_out)
    s_o = w_out.T
    s_o, doc_starts, skip_flags = tie(s_o, doc_starts, skip_flags)
    cosine, signed, qrow, beg, bounds, keep = rows_of(doc_starts, skip_flags)
    keep, tok_c = tie(keep, tok_c)
    tok_c, tok2 = tie(tok_c, tok2)
    xh = normed_rows(tok2, tok_c)
    xh, s_kv = tie(xh, s_kv)
    kv0 = ex.hi_copies(s_kv)
    xh, q0 = tie(xh, q0)
    q1 = ex.lo_gather(q0)
    q0, w_down = tie(q0, w_down)
    s_d = ex.quarters(w_down.T)
    s_d, s_u = tie(s_d, s_u)
    u0 = ex.hi_swap(s_u)
    s_d, kv0 = tie(s_d, kv0)
    kv1 = ex.lo_gather(kv0)
    kv0, q1 = tie(kv0, q1)
    q1, cotangent, keep = tie(q1, cotangent, keep)
    cot, dm_own = cotangents(cotangent, keep)
    dm_own, s_o = tie(dm_own, s_o)
    o0 = ex.hi_copies(s_o)
    dm_own, u0 = tie(dm_own, u0)
    u2 = ex.flip(u0, 2)
    u0, s_g = tie(u0, s_g)
    g0 = ex.hi_swap(s_g)
    u0, xh, q0, q1, cosine, signed = tie(u0, xh, q0, q1, cosine, signed)
    qu = query(xh, flat((q0, *q1)), cosine, signed)
    qu, kv1 = tie(qu, kv1)
    kv1, u0 = tie(kv1, u0)
    u1 = ex.lo_gather(u0)
    kv1, xh, kv0, cosine, signed = tie(kv1, xh, kv0, cosine, signed)
    kv = key_value(xh, flat((kv0, *kv1)), cosine, signed)
    kv, u2 = tie(kv, u2)
    u2, kv = tie(u2, kv)
    kr0 = ex.hi_copies(kv)
    u2, o0 = tie(u2, o0)
    o1 = ex.lo_gather(o0)
    o0, u1 = tie(o0, u1)
    u3 = tuple(ex.flip(v, 2) for v in u1)
    u1, kr0 = tie(u1, kr0)
    kr0, o1 = tie(kr0, o1)
    o1, u3 = tie(o1, u3)
    u3, kr0 = tie(u3, kr0)
    kr1 = ex.lo_gather(kr0)
    u3, g0 = tie(u3, g0)
    g2 = ex.flip(g0, 2)
    g0, kr1 = tie(g0, kr1)
    kr1, dm_own = tie(kr1, dm_own)
    dm4 = ex.hi_rows(dm_own)
    kr1, g0 = tie(kr1, g0)
    g1 = ex.lo_gather(g0)
    kr1, qu, kr0, qrow, beg, bounds = tie(kr1, qu, kr0, qrow, beg, bounds)
    att, lse, kva = attention(qu, kr0, kr1, qrow, beg, bounds)
    kva, g2 = tie(kva, g2)
    g2, g1 = tie(g2, g1)
    g1, s_d = tie(g1, s_d)
    d0 = ex.hi_swap(s_d)
    g1, dm4 = tie(g1, dm4)
    dm4, att, o0, o1 = tie(dm4, att, o0, o1)
    ao_k, ao_s = expand([(att, flat((o0, *o1)))])
    ao_s, dm4 = tie(ao_s, dm4)
    dm_c = ex.flip(dm4, 1)
    ao_s, g1 = tie(ao_s, g1)
    g3 = tuple(ex.flip(v, 2) for v in g1)
    ao_r = ex.flip(ao_s, 1)
    ao_k, g3 = tie(ao_k, g3)
    g3, ao_r = tie(g3, ao_r)
    ao_r, ao_k = tie(ao_r, ao_k)
    ao_k2, ao_s2 = halves(ao_k, ao_r)
    ao_r2 = ex.flip(ao_s2, 2)
    ao_k2, d0 = tie(ao_k2, d0)
    d1 = ex.lo_gather(d0)
    d2 = ex.flip(d0, 2)
    d0, ao_r2 = tie(d0, ao_r2)
    ao_r2, ao_k2, tok, keep = tie(ao_r2, ao_k2, tok, keep)
    middle, nrm = middle_of(ao_k2, ao_r2, tok, keep)
    nm4 = ex.hi_rows(nrm)
    middle, d1 = tie(middle, d1)
    d1, d2 = tie(d1, d2)
    d2, d1 = tie(d2, d1)
    d3 = tuple(ex.flip(v, 2) for v in d1)
    d2, d3 = tie(d2, d3)
    d3, nm4 = tie(d3, nm4)
    nm_c = ex.flip(nm4, 1)
    nm4, nm_c = tie(nm4, nm_c)
    nm_c, nm4, g0, g1, g2, g3, u0, u1, u2, u3 = tie(nm_c, nm4, g0, g1, g2, g3, u0, u1, u2, u3)
    nm, gate, up, hid = feed_forward(nm4, nm_c, sides(g0, g1, g2, g3), sides(u0, u1, u2, u3))
    hid, dm_c = tie(hid, dm_c)
    dm_c, dm4, d0, d1, d2, d3, gate, up = tie(dm_c, dm4, d0, d1, d2, d3, gate, up)
    dm, dgate, dup = feed_back(dm4, dm_c, sides(d0, d1, d2, d3), gate, up)
    dup, nm = tie(dup, nm)
    gu_x = weight_sums_sent(nm, dup, chunk, chunk)
    gu_r = ex.flip(gu_x, 2)
    dup, dgate, g0, g1, g2, g3, u0, u1, u2, u3 = tie(dup, dgate, g0, g1, g2, g3, u0, u1, u2, u3)
    e_k, e_s = feed_back_rows(dgate, dup, g0, g1, g2, g3, u0, u1, u2, u3)
    c3_r = ex.flip(e_s, 1)
    e_k, dm, hid = tie(e_k, dm, hid)
    gd_x = weight_sums_sent(dm, hid, chunk, chunk)
    gd_x, c3_r = tie(gd_x, c3_r)
    c3_r, e_k = tie(c3_r, e_k)
    c3_s = added(e_k, c3_r)
    c3_z = ex.hi_swap(c3_s)
    gd_x, hid, d0, d1, d2, d3 = tie(gd_x, hid, d0, d1, d2, d3)
    m_k, m_s = down_rows(hid, d0, d1, d2, d3)
    mo_r = ex.flip(m_s, 1)
    m_k, mo_r = tie(m_k, mo_r)
    mo_r, m_k = tie(mo_r, m_k)
    mo_s = added(m_k, mo_r)
    mo_s, nm, dgate = tie(mo_s, nm, dgate)
    gg_x = weight_sums_sent(nm, dgate, chunk, chunk)
    gg_x, gu_r = tie(gg_x, gu_r)
    gu_r, gd_x = tie(gu_r, gd_x)
    gd_r = ex.flip(gd_x, 2)
    gu_r, c3_z = tie(gu_r, c3_z)
    c3_z, nm, dup, gu_r = tie(c3_z, nm, dup, gu_r)
    gu_k, gu_s = weight_sums(nm, dup, 0, chunk, ex.lo, gu_r)
    gu_s, mo_s = tie(gu_s, mo_s)
    mo_z = ex.hi_swap(mo_s)
    gu_y = ex.lo_scatter(gu_s)
    gu_k, c3_z, middle, cot, keep = tie(gu_k, c3_z, middle, cot, keep)
    d_mid, da_own = middle_back(c3_z, middle, cot, keep)
    da_own, gu_y = tie(da_own, gu_y)
    gu_y, gu_k = tie(gu_y, gu_k)
    gu_l = lo_total(gu_k, gu_y)
    gu_l, mo_z = tie(gu_l, mo_z)
    mo_z, gd_r = tie(mo_z, gd_r)
    gd_r, dm, hid = tie(gd_r, dm, hid)
    gd_k, gd_s = weight_sums(dm, hid, 0, chunk, ex.lo, gd_r)
    gd_y = ex.lo_scatter(gd_s)
    gd_k, mo_z, middle, keep = tie(gd_k, mo_z, middle, keep)
    layer_out = layer_rows(mo_z, middle, keep)
    layer_out, gg_x = tie(layer_out, gg_x)
    gg_r = ex.flip(gg_x, 2)
    layer_out, da_own = tie(layer_out, da_own)
    da_x = ex.flip(da_own, 2)
    layer_out, gu_l = tie(layer_out, gu_l)
    gu_z = ex.hi_swap(gu_l)
    layer_out, da_x = tie(layer_out, da_x)
    da_x, da_own = tie(da_x, da_own)
    da2 = joined(da_own, da_x)
    da_c = ex.flip(da2, 1)
    da2, da_c = tie(da2, da_c)
    da_c, da2 = tie(da_c, da2)
    da = joined(da2, da_c)
    da, o0, o1 = tie(da, o0, o1)
    datt = project(da, flat((o0, *o1)))
    (
        datt,
        qu,
        kva,
        att,
        lse,
        qrow,
        beg,
        bounds,
        cosine,
        signed,
    ) = tie(
        datt,
        qu,
        kva,
        att,
        lse,
        qrow,
        beg,
        bounds,
        cosine,
        signed,
    )
    dq, dk_k, dk_s = attention_back(qu, kva, att, datt, lse, qrow, beg, bounds, cosine, signed)
    dk_s, gu_z = tie(dk_s, gu_z)
    gu_z, gd_y = tie(gu_z, gd_y)
    gd_y, dk_s = tie(gd_y, dk_s)
    dk_y = ex.lo_scatter(dk_s)
    gd_y, gd_k = tie(gd_y, gd_k)
    gd_l = lo_total(gd_k, gd_y)
    gd_z = ex.hi_swap(gd_l)
    gu_z, xh, dq = tie(gu_z, xh, dq)
    gq_k, gq_s = weight_sums(xh, dq, 0, q_width, ex.lo)
    gq_s, gg_r = tie(gq_s, gg_r)
    gg_r, nm, dgate = tie(gg_r, nm, dgate)
    gg_k, gg_s = weight_sums(nm, dgate, 0, chunk, ex.lo, gg_r)
    gg_y = ex.lo_scatter(gg_s)
    gg_k, dk_y = tie(gg_k, dk_y)
    dk_y, gq_s = tie(dk_y, gq_s)
    gq_y = ex.lo_scatter(gq_s)
    dk_y, dk_k = tie(dk_y, dk_k)
    dk_l = lo_total(dk_k, dk_y)
    dk_l, gu_z, w_up, gain_mlp = tie(dk_l, gu_z, w_up, gain_mlp)
    grad_up, sum_u = spread_gained(gu_z, w_up, gain_mlp)
    sum_u, dk_l = tie(sum_u, dk_l)
    dk_z = ex.hi_swap(dk_l)
    sum_u, gg_y = tie(sum_u, gg_y)
    gg_y, gg_k = tie(gg_y, gg_k)
    gg_l = lo_total(gg_k, gg_y)
    gg_z = ex.hi_swap(gg_l)
    sum_u, gd_z = tie(sum_u, gd_z)
    gd_z, dk_z = tie(gd_z, dk_z)
    dk_z, cosine, signed = tie(dk_z, cosine, signed)
    dkv = keys_back(dk_z, cosine, signed)
    dkv, dq, q0, q1, kv0, kv1 = tie(dkv, dq, q0, q1, kv0, kv1)
    n_k, n_s = attention_rows_back(dq, q0, q1, dkv, kv0, kv1)
    n_s, da, att = tie(n_s, da, att)
    go_k, go_s = weight_sums(da, att, 0, q_width, ex.lo)
    go_y = ex.lo_scatter(go_s)
    go_k, n_s = tie(go_k, n_s)
    n_r = ex.flip(n_s, 1)
    go_k, gd_z = tie(go_k, gd_z)
    grad_down = spread(gd_z).T
    grad_down, n_r = tie(grad_down, n_r)
    n_r, n_k = tie(n_r, n_k)
    n_k2, n_s2 = halves(n_k, n_r)
    n_r2 = ex.flip(n_s2, 2)
    n_k2, gq_y = tie(n_k2, gq_y)
    gq_y, gq_k = tie(gq_y, gq_k)
    gq_l = lo_total(gq_k, gq_y)
    gq_l, gg_z = tie(gq_l, gg_z)
    gg_z, gq_l = tie(gg_z, gq_l)
    gq_z = ex.hi_swap(gq_l)
    gg_z, n_r2 = tie(gg_z, n_r2)
    n_r2, gg_z, w_gate, gain_mlp = tie(n_r2, gg_z, w_gate, gain_mlp)
    grad_gate, sum_g = spread_gained(gg_z, w_gate, gain_mlp)
    sum_g, n_k2, n_r2, tok, d_mid = tie(sum_g, n_k2, n_r2, tok, d_mid)
    d_tokens = tokens_back(n_k2, n_r2, tok, d_mid)
    d_tokens, xh, dkv = tie(d_tokens, xh, dkv)
    gk_k, gk_s = weight_sums(xh, dkv, 0, 2 * k_width, ex.lo)
    gk_s, go_y = tie(gk_s, go_y)
    go_y, gk_s = tie(go_y, gk_s)
    gk_y = ex.lo_scatter(gk_s)
    go_y, go_k = tie(go_y, go_k)
    go_l = lo_total(go_k, go_y)
    go_l, gq_z = tie(go_l, gq_z)
    gq_z, go_l = tie(gq_z, go_l)
    go_z = ex.hi_swap(go_l)
    gq_z, gk_y = tie(gq_z, gk_y)
    gk_y, gq_z, gain_attn, w_query = tie(gk_y, gq_z, gain_attn, w_query)
    grad_query, sum_q = query_grads(gq_z, gain_attn, w_query)
    sum_q, gk_k, gk_y = tie(sum_q, gk_k, gk_y)
    gk_l = lo_total(gk_k, gk_y)
    gk_l, go_z = tie(gk_l, go_z)
    go_z, gk_l = tie(go_z, gk_l)
    gk_z = ex.hi_swap(gk_l)
    grad_out = hi_total(go_z).T
    grad_out, gk_z = tie(grad_out, gk_z)
    gk_z, gain_attn, w_key, w_value = tie(gk_z, gain_attn, w_key, w_value)
    grad_key, grad_value, sum_k = key_grads(gk_z, gain_attn, w_key, w_value)
    sum_k, sum_q, sum_g, sum_u = tie(sum_k, sum_q, sum_g, sum_u)
    gains = jnp.stack([sum_q + sum_k, sum_g + sum_u])
    gains_x = ex.flip(gains, 2)
    gains, gains_x = tie(gains, gains_x)
    gains_x, gains = tie(gains_x, gains)
    gains2 = gains + gains_x
    gains_c = ex.flip(gains2, 1)
    gains2, gains_c = tie(gains2, gains_c)
    gains_c, gains2 = tie(gains_c, gains2)
    grad_gain_attn, grad_gain_mlp = gains2 + gains_c
    return (
        layer_out,
        d_tokens,
        grad_gain_attn,
        grad_query,
        grad_key,
        grad_value,
        grad_out,
        grad_gain_mlp,
        grad_gate,
        grad_up,
        grad_down,
    )


def solution(mesh):
    rows = P(("fsdp", "tp"), None)
    in_specs = (
        rows,
        rows,
        P(),
        P(),
        P("fsdp"),
        P("fsdp", "tp"),
        P("fsdp", "tp"),
        P("fsdp", "tp"),
        P("tp", "fsdp"),
        P("fsdp"),
        P("fsdp", "tp"),
        P("fsdp", "tp"),
        P("tp", "fsdp"),
    )
    out_specs = (
        rows,
        rows,
        P("fsdp"),
        P("fsdp", "tp"),
        P("fsdp", "tp"),
        P("fsdp", "tp"),
        P("tp", "fsdp"),
        P("fsdp"),
        P("fsdp", "tp"),
        P("fsdp", "tp"),
        P("tp", "fsdp"),
    )
    return jax.shard_map(
        functools.partial(local, Exchange(mesh)), mesh=mesh, in_specs=in_specs, out_specs=out_specs, check_vma=False
    )
```

```python
import functools

import jax
import jax.numpy as jnp
from jax import lax
from jax.experimental import pallas as pl
from jax.experimental.pallas import tpu as pltpu
from jax.sharding import PartitionSpec as P

HEAD_DIM = 128
EPS = 1e-05
THETA = 10000.0
FLOOR = -1e30
LOG2E = 1.4426950408889634
MIB = 1024 * 1024
F32 = jnp.float32
BF16 = jnp.bfloat16
HI = 4


def angles(places, width):
    half = width // 2
    freq = 1.0 / THETA ** (jnp.arange(half, dtype=F32) * 2.0 / width)
    angle = places.astype(F32)[:, None] * freq[None, :]
    cosine = jnp.cos(angle)
    sine = jnp.sin(angle)
    return (jnp.concatenate([cosine, cosine], -1), jnp.concatenate([sine, sine], -1))


def documents(doc_starts, skip_flags, row_index):
    inside = doc_starts[None, :] <= row_index[:, None]
    segment = jnp.sum(inside.astype(jnp.int32), axis=1) - 1
    begins = jnp.max(jnp.where(inside, doc_starts[None, :], 0), axis=1)
    chosen = segment[:, None] == jnp.arange(doc_starts.shape[0], dtype=jnp.int32)[None, :]
    skipped = jnp.sum(jnp.where(chosen, skip_flags[None, :], 0), axis=1)
    return (begins, (1 - skipped).astype(F32))


def product(left, right):
    return jnp.dot(left, right, preferred_element_type=F32)


def against(left, right):
    return lax.dot_general(left, right, (((1,), (1,)), ((), ())), preferred_element_type=F32)


def outer_sum(left, right):
    return lax.dot_general(left, right, (((0,), (0,)), ((), ())), preferred_element_type=F32)


def block_rows_of(block, bounds, lo, size):
    piece = lax.rem(lax.rem(block, lo) - bounds[2] + lo, lo)
    place = piece * HI + lax.div(block, lo)
    return pl.ds(pl.multiple_of(place * size, size), size)


def closed_keys(block, size, koff_ref, qrow_ref, beg_ref):
    krow = koff_ref[...] + block * size
    return jnp.where((krow <= qrow_ref[...]) & (krow >= beg_ref[...]), 0.0, FLOOR)


def attend_kernel(heads, lo, bounds, q_ref, kv_ref, qrow_ref, beg_ref, koff_ref, o_ref, lse_ref, top, mass, acc):
    size = koff_ref.shape[0]
    factor = HEAD_DIM**-0.5 * LOG2E
    top[...] = jnp.full_like(top, FLOOR)
    mass[...] = jnp.zeros_like(mass)
    acc[...] = jnp.zeros_like(acc)

    def step(block, carry):
        rows = block_rows_of(block, bounds, lo, size)
        keys = kv_ref[rows, :HEAD_DIM]
        values = kv_ref[rows, HEAD_DIM:].astype(F32).T.astype(BF16)
        closed = closed_keys(block, size, koff_ref, qrow_ref, beg_ref)
        for h in range(heads):
            scores = against(keys, q_ref[:, h * HEAD_DIM : (h + 1) * HEAD_DIM]) * factor + closed
            before = top[h]
            now = jnp.maximum(before, jnp.max(scores, axis=0, keepdims=True))
            weights = jnp.exp2(scores - now)
            fading = jnp.exp2(before - now)
            top[h] = now
            mass[h] = mass[h] * fading + jnp.sum(weights, axis=0, keepdims=True)
            acc[h] = acc[h] * fading + product(values, weights.astype(BF16))
        return carry

    lax.fori_loop(bounds[0], bounds[1] + 1, step, 0)
    for h in range(heads):
        o_ref[:, h * HEAD_DIM : (h + 1) * HEAD_DIM] = (acc[h] / mass[h]).T.astype(BF16)
        lse_ref[h] = top[h] + jnp.log2(mass[h])


def attend_back_kernel(
    heads, lo, bounds, q_ref, kv_ref, o_ref, do_ref, lse_ref, qrow_ref, beg_ref, koff_ref, cos_ref, sin_ref,
    dq_ref, dkv_ref, delta, acc
):
    size = koff_ref.shape[0]
    factor = HEAD_DIM**-0.5
    acc[...] = jnp.zeros_like(acc)
    dkv_ref[...] = jnp.zeros_like(dkv_ref)
    for h in range(heads):
        cols = slice(h * HEAD_DIM, (h + 1) * HEAD_DIM)
        both = do_ref[:, cols].astype(F32) * o_ref[:, cols].astype(F32)
        delta[h] = jnp.sum(both.T, axis=0, keepdims=True)

    def step(block, carry):
        rows = block_rows_of(block, bounds, lo, size)
        keys = kv_ref[rows, :HEAD_DIM]
        values = kv_ref[rows, HEAD_DIM:]
        turned_keys = keys.astype(F32).T.astype(BF16)
        closed = closed_keys(block, size, koff_ref, qrow_ref, beg_ref)
        dkeys = jnp.zeros((size, HEAD_DIM), F32)
        dvalues = jnp.zeros((size, HEAD_DIM), F32)
        for h in range(heads):
            cols = slice(h * HEAD_DIM, (h + 1) * HEAD_DIM)
            queries = q_ref[:, cols]
            grads = do_ref[:, cols]
            scores = against(keys, queries) * (factor * LOG2E) + closed
            probs = jnp.exp2(scores - lse_ref[h])
            dvalues = dvalues + product(probs.astype(BF16), grads)
            dprobs = against(values, grads)
            dscores = (probs * ((dprobs - delta[h]) * factor)).astype(BF16)
            acc[h] = acc[h] + product(turned_keys, dscores)
            dkeys = dkeys + product(dscores, queries)
        dkv_ref[rows, :HEAD_DIM] = dkeys.astype(BF16)
        dkv_ref[rows, HEAD_DIM:] = dvalues.astype(BF16)
        return carry

    lax.fori_loop(bounds[0], bounds[1] + 1, step, 0)
    for h in range(heads):
        grads = acc[h].T
        back = grads * cos_ref[...] - pltpu.roll(grads, HEAD_DIM // 2, 1) * sin_ref[...]
        dq_ref[:, h * HEAD_DIM : (h + 1) * HEAD_DIM] = back.astype(BF16)


VMEM_SPEC = pl.BlockSpec(memory_space=pltpu.VMEM)
SMEM_SPEC = pl.BlockSpec(memory_space=pltpu.SMEM)
NOTHING = pl.CostEstimate(flops=1, bytes_accessed=1, transcendentals=0)


def attend(bounds, q, kv, qrow, beg, koff, lo):
    rows, width = q.shape
    heads = width // HEAD_DIM
    return pl.pallas_call(
        functools.partial(attend_kernel, heads, lo),
        out_shape=(
            jax.ShapeDtypeStruct((rows, width), BF16),
            jax.ShapeDtypeStruct((heads, 1, rows), F32),
        ),
        in_specs=[SMEM_SPEC] + [VMEM_SPEC] * 5,
        out_specs=(VMEM_SPEC, VMEM_SPEC),
        scratch_shapes=[
            pltpu.VMEM((heads, 1, rows), F32),
            pltpu.VMEM((heads, 1, rows), F32),
            pltpu.VMEM((heads, HEAD_DIM, rows), F32),
        ],
        compiler_params=pltpu.CompilerParams(vmem_limit_bytes=16 * MIB),
        cost_estimate=NOTHING,
    )(bounds, q, kv, qrow, beg, koff)


def attend_back(bounds, q, kv, o, do, lse, qrow, beg, koff, cosine, signed, lo):
    rows, width = q.shape
    heads = width // HEAD_DIM
    return pl.pallas_call(
        functools.partial(attend_back_kernel, heads, lo),
        out_shape=(
            jax.ShapeDtypeStruct((rows, width), BF16),
            jax.ShapeDtypeStruct(kv.shape, BF16),
        ),
        in_specs=[SMEM_SPEC] + [VMEM_SPEC] * 10,
        out_specs=(VMEM_SPEC, VMEM_SPEC),
        scratch_shapes=[
            pltpu.VMEM((heads, 1, rows), F32),
            pltpu.VMEM((heads, HEAD_DIM, rows), F32),
        ],
        compiler_params=pltpu.CompilerParams(vmem_limit_bytes=16 * MIB),
        cost_estimate=NOTHING,
    )(bounds, q, kv, o, do, lse, qrow, beg, koff, cosine, signed)


class Exchange:
    def __init__(self, mesh):
        self.shards = mesh.shape["fsdp"]
        self.hi = HI
        self.lo = self.shards // HI
        self.tp = mesh.shape["tp"]
        self.hi_groups = [[h * self.lo + b for h in range(self.hi)] for b in range(self.lo)]

    def lo_shift(self, v, s):
        pairs = [
            (h * self.lo + b, h * self.lo + (b + s) % self.lo) for h in range(self.hi) for b in range(self.lo)
        ]
        return lax.ppermute(v, "fsdp", pairs)

    def flip(self, v, mask):
        return lax.ppermute(v, "tp", [(t, t ^ mask) for t in range(self.tp)])

    def hi_swap(self, v):
        return lax.all_to_all(v, "fsdp", 0, 0, axis_index_groups=self.hi_groups)

    def hi_copies(self, w):
        return self.hi_swap(jnp.broadcast_to(w[None], (self.hi,) + w.shape))

    def lo_gather(self, v):
        return tuple(self.lo_shift(v, -s) for s in range(1, self.lo))

    def lo_scatter(self, v):
        m = v.shape[0] // (self.lo - 1)
        return tuple(self.lo_shift(v[s * m : (s + 1) * m], s + 1) for s in range(self.lo - 1))

    def hi_rows(self, v):
        return self.hi_copies(v).reshape(self.hi * v.shape[0], v.shape[1])

    def turned_lo(self, parts, start):
        if self.lo == 2:
            return [jnp.where(start == 0, parts[0], parts[1]), jnp.where(start == 0, parts[1], parts[0])]
        both = jnp.concatenate([part[None] for part in parts + parts], axis=0)
        both = lax.dynamic_slice_in_dim(both, start, self.lo, axis=0)
        return [both[s] for s in range(self.lo)]

    def to_pieces(self, v):
        n = v.shape[1] // self.shards
        b = lax.axis_index("fsdp") % self.lo
        parts = [
            jnp.concatenate([v[:, (h * self.lo + l) * n : (h * self.lo + l + 1) * n] for h in range(self.hi)], axis=1)
            for l in range(self.lo)
        ]
        return jnp.concatenate(self.turned_lo(parts, b), axis=1)

    def from_pieces(self, v):
        n = v.shape[1] // self.shards
        b = lax.axis_index("fsdp") % self.lo
        own = self.hi * n
        parts = [v[:, s * own : (s + 1) * own] for s in range(self.lo)]
        parts = self.turned_lo(parts, (self.lo - b) % self.lo)
        return jnp.concatenate(
            [parts[l][:, h * n : (h + 1) * n] for h in range(self.hi) for l in range(self.lo)], axis=1
        )

    def quarters(self, w):
        n, k = w.shape
        chunk = -(-k // (self.hi * 128)) * 128
        w = jnp.pad(w, ((0, 0), (0, self.hi * chunk - k)))
        return w.reshape(n, self.hi, chunk).transpose(1, 0, 2)


def kernel_call(kernel, outs, args, flops, scratch=(), limit=16):
    return pl.pallas_call(
        kernel,
        out_shape=outs,
        in_specs=[VMEM_SPEC] * len(args),
        out_specs=jax.tree.map(lambda _: VMEM_SPEC, outs),
        scratch_shapes=list(scratch),
        compiler_params=pltpu.CompilerParams(vmem_limit_bytes=limit * MIB),
        cost_estimate=NOTHING,
    )(*args)


def shape(dims, kind):
    return jax.ShapeDtypeStruct(tuple(dims), kind)


def flat(pieces):
    return [p.reshape(-1, p.shape[-1]) for p in pieces]


def through(x_ref, pieces):
    depth = x_ref.shape[1] // len(pieces)
    total = None
    for s, piece in enumerate(pieces):
        part = product(x_ref[:, s * depth : (s + 1) * depth], piece[...])
        total = part if total is None else total + part
    return total


def turned(v, cosine, signed):
    return v * cosine + pltpu.roll(v, HEAD_DIM // 2, 1) * signed


def key_value(x, pieces, cosine, signed):
    def kernel(x_ref, *refs):
        *ws, cos_ref, sin_ref, out_ref = refs
        raw = through(x_ref, ws)
        out_ref[:, :HEAD_DIM] = turned(raw[:, :HEAD_DIM], cos_ref[...], sin_ref[...]).astype(BF16)
        out_ref[:, HEAD_DIM:] = raw[:, HEAD_DIM:].astype(BF16)

    rows, k = x.shape[0], pieces[0].shape[1]
    return kernel_call(kernel, shape((rows, k), BF16), (x, *pieces, cosine, signed), 2 * rows * k * x.shape[1])


def query(x, pieces, cosine, signed):
    def kernel(x_ref, *refs):
        *ws, cos_ref, sin_ref, out_ref = refs
        raw = through(x_ref, ws)
        for c in range(0, out_ref.shape[1], HEAD_DIM):
            cols = slice(c, c + HEAD_DIM)
            out_ref[:, cols] = turned(raw[:, cols], cos_ref[...], sin_ref[...]).astype(BF16)

    rows, k = x.shape[0], pieces[0].shape[1]
    return kernel_call(kernel, shape((rows, k), BF16), (x, *pieces, cosine, signed), 2 * rows * k * x.shape[1])


def project(x, pieces):
    def kernel(x_ref, *refs):
        *ws, out_ref = refs
        out_ref[...] = through(x_ref, ws).astype(BF16)

    rows, k = x.shape[0], pieces[0].shape[1]
    return kernel_call(kernel, shape((rows, k), BF16), (x, *pieces), 2 * rows * k * x.shape[1])


def expand(terms, extra=None):
    rows = terms[0][0].shape[0]
    half = rows // 2
    lo = len(terms[0][1])
    depth = terms[0][1][0].shape[0]
    width = lo * depth

    def kernel(*refs):
        keep_ref, send_ref = refs[-2:]
        groups = [refs[g * (lo + 1) : (g + 1) * (lo + 1)] for g in range(len(terms))]
        for s in range(lo):
            cols = slice(s * depth, (s + 1) * depth)
            total = None
            for group in groups:
                part = against(group[0][...], group[1 + s][...])
                total = part if total is None else total + part
            keep_ref[:, cols] = total[:half]
            send_ref[:, cols] = total[half:].astype(BF16)

    flops = sum(2 * rows * t[0].shape[1] * width for t in terms)
    args = tuple(a for t in terms for a in (t[0], *t[1]))
    return kernel_call(kernel, (shape((half, width), F32), shape((half, width), BF16)), args, flops)


def feed_forward(upper, lower, gates, ups):
    half, depth = upper.shape
    rows = 2 * half
    lo = len(gates) // 2
    chunk = gates[0].shape[1]

    def kernel(upper_ref, lower_ref, *refs):
        x_ref, gate_ref, up_ref, hidden_ref = refs[-4:]
        x_ref[:half] = upper_ref[...]
        x_ref[half:] = lower_ref[...]
        for side in range(2):
            cols = slice(side * chunk, (side + 1) * chunk)
            gate = through(x_ref, refs[side * lo : (side + 1) * lo])
            up = through(x_ref, refs[(2 + side) * lo : (3 + side) * lo])
            gate_ref[:, cols] = gate
            up_ref[:, cols] = up
            hidden_ref[:, cols] = (gate * jax.nn.sigmoid(gate) * up).astype(BF16)

    dims = (rows, 2 * chunk)
    outs = (shape((rows, depth), BF16), shape(dims, F32), shape(dims, F32), shape(dims, BF16))
    return kernel_call(kernel, outs, (upper, lower, *gates, *ups), 1, limit=20)


def feed_back(upper, lower, downs, gate, up):
    half, depth = upper.shape
    rows, width = gate.shape
    chunk = width // 2
    lo = len(downs) // 2

    def kernel(upper_ref, lower_ref, *refs):
        gate_ref, up_ref, d_ref, dgate_ref, dup_ref = refs[-5:]
        d_ref[:half] = upper_ref[...]
        d_ref[half:] = lower_ref[...]
        for side in range(2):
            cols = slice(side * chunk, (side + 1) * chunk)
            gates = gate_ref[:, cols]
            sigma = jax.nn.sigmoid(gates)
            scaled = through(d_ref, refs[side * lo : (side + 1) * lo]) * sigma
            dgate_ref[:, cols] = (scaled * up_ref[:, cols] * (1.0 + gates * (1.0 - sigma))).astype(BF16)
            dup_ref[:, cols] = (scaled * gates).astype(BF16)

    dims = (rows, width)
    outs = (shape((rows, depth), BF16), shape(dims, BF16), shape(dims, BF16))
    return kernel_call(kernel, outs, (upper, lower, *downs, gate, up), 1, limit=20)


def weight_sums(x, d, first, k, lo, extra=None):
    rows, width = x.shape
    own = width // lo

    def kernel(x_ref, d_ref, *refs):
        keep_ref, send_ref = refs[-2:]
        dcols = d_ref[:, first : first + k]
        for s in range(lo):
            part = slice(s * own, (s + 1) * own)
            total = outer_sum(x_ref[:, part], dcols)
            if extra is not None:
                total = total + refs[0][part, :].astype(F32)
            if s == 0:
                keep_ref[...] = total
            else:
                send_ref[(s - 1) * own : s * own, :] = total.astype(BF16)

    args = (x, d) + (() if extra is None else (extra,))
    outs = (shape((own, k), F32), shape((width - own, k), BF16))
    return kernel_call(kernel, outs, args, 2 * rows * k * width)


def weight_sums_sent(x, d, first, k):
    def kernel(x_ref, d_ref, out_ref):
        out_ref[...] = outer_sum(x_ref[...], d_ref[:, first : first + k]).astype(BF16)

    rows, width = x.shape
    return kernel_call(kernel, shape((width, k), BF16), (x, d), 2 * rows * k * width)


def tie(*values):
    return lax.optimization_barrier(values)


def local(
    ex,
    tokens,
    cotangent,
    doc_starts,
    skip_flags,
    gain_attn,
    w_query,
    w_key,
    w_value,
    w_out,
    gain_mlp,
    w_gate,
    w_up,
    w_down,
):
    count, width = tokens.shape
    q_width = w_query.shape[1]
    k_width = w_key.shape[1]
    hidden_width = w_gate.shape[1]
    n = w_gate.shape[0]
    chunk = -(-hidden_width // (ex.hi * 128)) * 128
    block_rows = count * ex.tp
    fsdp = lax.axis_index("fsdp")
    tp = lax.axis_index("tp")
    offsets = jnp.arange(count, dtype=jnp.int32)
    koff = jnp.concatenate([(tp ^ m) * count + offsets for m in (0, 2, 1, 3)])


    def gained(w, gain):
        return (w.astype(F32) * gain.astype(F32)[:, None]).astype(BF16)

    def normed(x):
        x = x.astype(F32)
        return x, lax.rsqrt(jnp.mean(x * x, axis=-1, keepdims=True) + EPS)

    def rows_of(doc_starts, skip_flags):
        row_index = fsdp * block_rows + koff
        begins, keep_rows = documents(doc_starts, skip_flags, row_index)
        cosine, sine = angles(row_index - begins, HEAD_DIM)
        half = HEAD_DIM // 2
        signed = jnp.concatenate([-sine[:, :half], sine[:, half:]], axis=1)
        bounds = jnp.stack([jnp.min(begins) // block_rows, fsdp, fsdp % ex.lo]).astype(jnp.int32)
        return cosine, signed, row_index[None, :], begins[None, :], bounds, keep_rows[:count, None]

    def cotangents(cotangent, keep):
        cot = ex.to_pieces(cotangent)
        return cot, (keep * cot.astype(F32)).astype(BF16)

    def joined(v, *got):
        return jnp.concatenate([v, *got], axis=0)

    def normed_rows(first, got):
        x, scale = normed(joined(first, got))
        return (x * scale).astype(BF16)

    def attention(qu, own_piece, others, qrow, beg, bounds):
        kv_all = jnp.concatenate(flat((own_piece, *others)), axis=0)
        attended, lse = attend(bounds, qu, kv_all, qrow, beg, koff[:, None], ex.lo)
        return attended, lse, kv_all

    def attention_back(qu, kva, att, datt, lse, qrow, beg, bounds, cosine, signed):
        dq, dkv = attend_back(bounds, qu, kva, att, datt, lse, qrow, beg, koff[:, None], cosine, signed, ex.lo)
        m = dkv.shape[0] // ex.lo
        return dq, dkv[:m], dkv[m:]

    def halves(keep, got):
        g = keep + got.astype(F32)
        return g[: g.shape[0] // 2], g[g.shape[0] // 2 :].astype(BF16)

    def added(keep, got):
        return (keep + got.astype(F32)).astype(BF16).reshape(ex.hi, count, width)

    def summed(kept, got):
        for v in got:
            kept = kept + v.astype(F32)
        return kept

    def middle_of(kept, got, tok, keep):
        middle, scale = normed(tok.astype(F32) + keep * (kept + got.astype(F32)))
        return middle, (middle * scale).astype(BF16)

    def sides(p0, p1, p2, p3):
        return flat((p0, *p1, p2, *p3))

    def feed_back_rows(dgate, dup, *ws):
        gates, ups = sides(*ws[:4]), sides(*ws[4:])
        return expand(
            [
                (dgate[:, :chunk], gates[: ex.lo]),
                (dgate[:, chunk:], gates[ex.lo :]),
                (dup[:, :chunk], ups[: ex.lo]),
                (dup[:, chunk:], ups[ex.lo :]),
            ]
        )

    def down_rows(hid, *ws):
        downs = sides(*ws)
        return expand([(hid[:, :chunk], downs[: ex.lo]), (hid[:, chunk:], downs[ex.lo :])])

    def hi_total(got):
        return jnp.sum(got.astype(F32), axis=0)

    def layer_rows(got, middle, keep):
        return ex.from_pieces((middle + keep * hi_total(got)).astype(BF16))

    def middle_back(got, middle, cot, keep):
        scaled = hi_total(got)
        scale = normed(middle)[1]
        d_middle = (
            cot.astype(F32)
            + scale * scaled
            - middle * scale**3 * jnp.mean(scaled * middle, axis=-1, keepdims=True)
        )
        return d_middle, (keep * d_middle).astype(BF16)

    def lo_total(kept, got):
        total = summed(kept.astype(F32), got).astype(BF16)
        return total.reshape(ex.hi, -1, total.shape[1])

    def spread(got):
        return jnp.concatenate([got[h] for h in range(ex.hi)], axis=1)[:, :hidden_width].astype(F32)

    def spread_gained(got, w, gain):
        total = spread(got)
        return total * gain.astype(F32)[:, None], jnp.sum(total * w.astype(F32), axis=1)

    def query_grads(got, gain, *weights):
        total = hi_total(got)
        w = jnp.concatenate(weights, axis=1).astype(F32)
        return total * gain.astype(F32)[:, None], jnp.sum(total * w, axis=1)

    def key_grads(got, gain, *weights):
        total, part = query_grads(got, gain, *weights)
        return total[:, :k_width], total[:, k_width:], part

    def keys_back(got, cosine, signed):
        total = hi_total(got)
        half = k_width // 2
        dk = total[:, :k_width]
        turned_back = dk * cosine - jnp.concatenate([dk[:, half:], dk[:, :half]], axis=1) * signed
        return jnp.concatenate([turned_back, total[:, k_width:]], axis=1).astype(BF16)

    def attention_rows_back(dq, q0, q1, dkv, kv0, kv1):
        return expand([(dq, flat((q0, *q1))), (dkv, flat((kv0, *kv1)))])

    def tokens_back(kept, got, tok, d_mid):
        scaled = kept + got.astype(F32)
        x, scale = normed(tok)
        d_tokens = d_mid + scale * scaled - x * scale**3 * jnp.mean(scaled * x, axis=-1, keepdims=True)
        return ex.from_pieces(d_tokens.astype(BF16))


    w_query, gain_attn = tie(w_query, gain_attn)
    s_q = gained(w_query, gain_attn)
    q0 = ex.hi_copies(s_q)
    tok = ex.to_pieces(tokens)
    tok_x = ex.flip(tok, 2)
    tok, w_key, w_value, gain_attn = tie(tok, w_key, w_value, gain_attn)
    s_kv = gained(jnp.concatenate([w_key, w_value], axis=1), gain_attn)
    s_kv, w_gate, gain_mlp = tie(s_kv, w_gate, gain_mlp)
    s_g = ex.quarters(gained(w_gate, gain_mlp))
    s_g, tok_x = tie(s_g, tok_x)
    tok_x, doc_starts, skip_flags = tie(tok_x, doc_starts, skip_flags)
    cosine, signed, qrow, beg, bounds, keep = rows_of(doc_starts, skip_flags)
    keep, tok, tok_x = tie(keep, tok, tok_x)
    tok2 = joined(tok, tok_x)
    tok_c = ex.flip(tok2, 1)
    tok2, w_out = tie(tok2, w_out)
    s_o = w_out.T
    s_o, tok_c = tie(s_o, tok_c)
    tok_c, tok2 = tie(tok_c, tok2)
    xh = normed_rows(tok2, tok_c)
    xh, s_kv = tie(xh, s_kv)
    kv0 = ex.hi_copies(s_kv)
    xh, q0 = tie(xh, q0)
    q1 = ex.lo_gather(q0)
    q0, w_up, gain_mlp = tie(q0, w_up, gain_mlp)
    s_u = ex.quarters(gained(w_up, gain_mlp))
    s_u, w_down = tie(s_u, w_down)
    s_d = ex.quarters(w_down.T)
    s_d, s_u = tie(s_d, s_u)
    u0 = ex.hi_swap(s_u)
    s_d, kv0 = tie(s_d, kv0)
    kv0, q1 = tie(kv0, q1)
    q1, cotangent, keep = tie(q1, cotangent, keep)
    cot, dm_own = cotangents(cotangent, keep)
    dm_own, kv0 = tie(dm_own, kv0)
    kv1 = ex.lo_gather(kv0)
    dm_own, s_o = tie(dm_own, s_o)
    o0 = ex.hi_copies(s_o)
    dm_own, u0 = tie(dm_own, u0)
    u2 = ex.flip(u0, 2)
    u0, xh, q0, q1, cosine, signed = tie(u0, xh, q0, q1, cosine, signed)
    qu = query(xh, flat((q0, *q1)), cosine, signed)
    qu, kv1 = tie(qu, kv1)
    kv1, u0 = tie(kv1, u0)
    u1 = ex.lo_gather(u0)
    kv1, xh, kv0, cosine, signed = tie(kv1, xh, kv0, cosine, signed)
    kv = key_value(xh, flat((kv0, *kv1)), cosine, signed)
    kv, u2 = tie(kv, u2)
    u2, kv = tie(u2, kv)
    kr0 = ex.hi_copies(kv)
    u2, o0 = tie(u2, o0)
    o1 = ex.lo_gather(o0)
    o0, u1 = tie(o0, u1)
    u3 = tuple(ex.flip(v, 2) for v in u1)
    u1, kr0 = tie(u1, kr0)
    kr0, s_g = tie(kr0, s_g)
    g0 = ex.hi_swap(s_g)
    kr0, o1 = tie(kr0, o1)
    o1, u3 = tie(o1, u3)
    u3, kr0 = tie(u3, kr0)
    kr1 = ex.lo_gather(kr0)
    u3, g0 = tie(u3, g0)
    g2 = ex.flip(g0, 2)
    g0, kr1 = tie(g0, kr1)
    kr1, dm_own = tie(kr1, dm_own)
    dm4 = ex.hi_rows(dm_own)
    kr1, g0 = tie(kr1, g0)
    g1 = ex.lo_gather(g0)
    kr1, qu, kr0, qrow, beg, bounds = tie(kr1, qu, kr0, qrow, beg, bounds)
    att, lse, kva = attention(qu, kr0, kr1, qrow, beg, bounds)
    kva, g2 = tie(kva, g2)
    g2, dm4 = tie(g2, dm4)
    dm4, g1 = tie(dm4, g1)
    g1, s_d = tie(g1, s_d)
    d0 = ex.hi_swap(s_d)
    g1, att, o0, o1 = tie(g1, att, o0, o1)
    ao_k, ao_s = expand([(att, flat((o0, *o1)))])
    ao_s, g1 = tie(ao_s, g1)
    g3 = tuple(ex.flip(v, 2) for v in g1)
    ao_r = ex.flip(ao_s, 1)
    ao_k, dm4 = tie(ao_k, dm4)
    dm_c = ex.flip(dm4, 1)
    ao_k, g3 = tie(ao_k, g3)
    g3, ao_r = tie(g3, ao_r)
    ao_r, ao_k = tie(ao_r, ao_k)
    ao_k2, ao_s2 = halves(ao_k, ao_r)
    ao_s2, dm_c = tie(ao_s2, dm_c)
    dm_c, ao_s2 = tie(dm_c, ao_s2)
    ao_r2 = ex.flip(ao_s2, 2)
    dm_c, d0 = tie(dm_c, d0)
    d1 = ex.lo_gather(d0)
    d2 = ex.flip(d0, 2)
    d0, ao_r2 = tie(d0, ao_r2)
    ao_r2, ao_k2, tok, keep = tie(ao_r2, ao_k2, tok, keep)
    middle, nrm = middle_of(ao_k2, ao_r2, tok, keep)
    nm4 = ex.hi_rows(nrm)
    middle, d1 = tie(middle, d1)
    d1, d2 = tie(d1, d2)
    d2, d1 = tie(d2, d1)
    d3 = tuple(ex.flip(v, 2) for v in d1)
    d2, nm4 = tie(d2, nm4)
    nm_c = ex.flip(nm4, 1)
    nm4, nm_c = tie(nm4, nm_c)
    nm_c, nm4, g0, g1, g2, g3, u0, u1, u2, u3 = tie(nm_c, nm4, g0, g1, g2, g3, u0, u1, u2, u3)
    nm, gate, up, hid = feed_forward(nm4, nm_c, sides(g0, g1, g2, g3), sides(u0, u1, u2, u3))
    hid, d3 = tie(hid, d3)
    d3, dm4, dm_c, d0, d1, d2, gate, up = tie(d3, dm4, dm_c, d0, d1, d2, gate, up)
    dm, dgate, dup = feed_back(dm4, dm_c, sides(d0, d1, d2, d3), gate, up)
    dup, nm = tie(dup, nm)
    gu_x = weight_sums_sent(nm, dup, chunk, chunk)
    gu_r = ex.flip(gu_x, 2)
    dup, dgate, g0, g1, g2, g3, u0, u1, u2, u3 = tie(dup, dgate, g0, g1, g2, g3, u0, u1, u2, u3)
    e_k, e_s = feed_back_rows(dgate, dup, g0, g1, g2, g3, u0, u1, u2, u3)
    c3_r = ex.flip(e_s, 1)
    e_k, hid, d0, d1, d2, d3 = tie(e_k, hid, d0, d1, d2, d3)
    m_k, m_s = down_rows(hid, d0, d1, d2, d3)
    m_s, c3_r = tie(m_s, c3_r)
    c3_r, dm, hid = tie(c3_r, dm, hid)
    gd_x = weight_sums_sent(dm, hid, chunk, chunk)
    gd_x, m_s = tie(gd_x, m_s)
    mo_r = ex.flip(m_s, 1)
    gd_x, e_k, c3_r = tie(gd_x, e_k, c3_r)
    c3_s = added(e_k, c3_r)
    c3_z = ex.hi_swap(c3_s)
    gd_x, mo_r = tie(gd_x, mo_r)
    mo_r, m_k = tie(mo_r, m_k)
    mo_s = added(m_k, mo_r)
    mo_s, nm, dgate = tie(mo_s, nm, dgate)
    gg_x = weight_sums_sent(nm, dgate, chunk, chunk)
    gg_x, gu_r = tie(gg_x, gu_r)
    gu_r, gd_x = tie(gu_r, gd_x)
    gd_r = ex.flip(gd_x, 2)
    gu_r, c3_z = tie(gu_r, c3_z)
    c3_z, nm, dup, gu_r = tie(c3_z, nm, dup, gu_r)
    gu_k, gu_s = weight_sums(nm, dup, 0, chunk, ex.lo, gu_r)
    gu_s, mo_s = tie(gu_s, mo_s)
    mo_z = ex.hi_swap(mo_s)
    gu_y = ex.lo_scatter(gu_s)
    gu_k, c3_z, middle, cot, keep = tie(gu_k, c3_z, middle, cot, keep)
    d_mid, da_own = middle_back(c3_z, middle, cot, keep)
    da_own, gu_y = tie(da_own, gu_y)
    gu_y, gu_k = tie(gu_y, gu_k)
    gu_l = lo_total(gu_k, gu_y)
    gu_l, mo_z = tie(gu_l, mo_z)
    mo_z, gu_l = tie(mo_z, gu_l)
    gu_z = ex.hi_swap(gu_l)
    mo_z, gd_r = tie(mo_z, gd_r)
    gd_r, dm, hid = tie(gd_r, dm, hid)
    gd_k, gd_s = weight_sums(dm, hid, 0, chunk, ex.lo, gd_r)
    gd_y = ex.lo_scatter(gd_s)
    gd_k, da_own = tie(gd_k, da_own)
    da_x = ex.flip(da_own, 2)
    gd_k, mo_z, middle, keep = tie(gd_k, mo_z, middle, keep)
    layer_out = layer_rows(mo_z, middle, keep)
    layer_out, gg_x = tie(layer_out, gg_x)
    gg_r = ex.flip(gg_x, 2)
    layer_out, da_x = tie(layer_out, da_x)
    da_x, da_own = tie(da_x, da_own)
    da2 = joined(da_own, da_x)
    da_c = ex.flip(da2, 1)
    da2, da_c = tie(da2, da_c)
    da_c, da2 = tie(da_c, da2)
    da = joined(da2, da_c)
    da, o0, o1 = tie(da, o0, o1)
    datt = project(da, flat((o0, *o1)))
    (
        datt,
        qu,
        kva,
        att,
        lse,
        qrow,
        beg,
        bounds,
        cosine,
        signed,
    ) = tie(
        datt,
        qu,
        kva,
        att,
        lse,
        qrow,
        beg,
        bounds,
        cosine,
        signed,
    )
    dq, dk_k, dk_s = attention_back(qu, kva, att, datt, lse, qrow, beg, bounds, cosine, signed)
    dk_s, gu_z = tie(dk_s, gu_z)
    gu_z, gd_y = tie(gu_z, gd_y)
    gd_y, dk_s = tie(gd_y, dk_s)
    dk_y = ex.lo_scatter(dk_s)
    gd_y, gd_k = tie(gd_y, gd_k)
    gd_l = lo_total(gd_k, gd_y)
    gd_z = ex.hi_swap(gd_l)
    gu_z, xh, dq = tie(gu_z, xh, dq)
    gq_k, gq_s = weight_sums(xh, dq, 0, q_width, ex.lo)
    gq_s, gg_r = tie(gq_s, gg_r)
    gg_r, nm, dgate = tie(gg_r, nm, dgate)
    gg_k, gg_s = weight_sums(nm, dgate, 0, chunk, ex.lo, gg_r)
    gg_y = ex.lo_scatter(gg_s)
    gg_k, dk_y = tie(gg_k, dk_y)
    dk_y, dk_k = tie(dk_y, dk_k)
    dk_l = lo_total(dk_k, dk_y)
    dk_l, gu_z, w_up, gain_mlp = tie(dk_l, gu_z, w_up, gain_mlp)
    grad_up, sum_u = spread_gained(gu_z, w_up, gain_mlp)
    sum_u, gd_z = tie(sum_u, gd_z)
    gd_z, dk_l = tie(gd_z, dk_l)
    dk_z = ex.hi_swap(dk_l)
    gd_z, gq_s = tie(gd_z, gq_s)
    gq_y = ex.lo_scatter(gq_s)
    gd_z, gg_y = tie(gd_z, gg_y)
    gg_y, gg_k = tie(gg_y, gg_k)
    gg_l = lo_total(gg_k, gg_y)
    gg_z = ex.hi_swap(gg_l)
    gd_z, dk_z = tie(gd_z, dk_z)
    dk_z, cosine, signed = tie(dk_z, cosine, signed)
    dkv = keys_back(dk_z, cosine, signed)
    dkv, dq, q0, q1, kv0, kv1 = tie(dkv, dq, q0, q1, kv0, kv1)
    n_k, n_s = attention_rows_back(dq, q0, q1, dkv, kv0, kv1)
    n_s, xh, dkv = tie(n_s, xh, dkv)
    gk_k, gk_s = weight_sums(xh, dkv, 0, 2 * k_width, ex.lo)
    gk_y = ex.lo_scatter(gk_s)
    gk_k, da, att = tie(gk_k, da, att)
    go_k, go_s = weight_sums(da, att, 0, q_width, ex.lo)
    go_y = ex.lo_scatter(go_s)
    go_k, n_s = tie(go_k, n_s)
    n_r = ex.flip(n_s, 1)
    go_k, gd_z = tie(go_k, gd_z)
    grad_down = spread(gd_z).T
    grad_down, n_r = tie(grad_down, n_r)
    n_r, n_k = tie(n_r, n_k)
    n_k2, n_s2 = halves(n_k, n_r)
    n_r2 = ex.flip(n_s2, 2)
    n_k2, gq_y = tie(n_k2, gq_y)
    gq_y, gq_k = tie(gq_y, gq_k)
    gq_l = lo_total(gq_k, gq_y)
    gq_l, gg_z = tie(gq_l, gg_z)
    gg_z, gq_l = tie(gg_z, gq_l)
    gq_z = ex.hi_swap(gq_l)
    gg_z, gk_y = tie(gg_z, gk_y)
    gk_y, gk_k = tie(gk_y, gk_k)
    gk_l = lo_total(gk_k, gk_y)
    gk_l, n_r2 = tie(gk_l, n_r2)
    n_r2, gg_z, w_gate, gain_mlp = tie(n_r2, gg_z, w_gate, gain_mlp)
    grad_gate, sum_g = spread_gained(gg_z, w_gate, gain_mlp)
    sum_g, n_k2, n_r2, tok, d_mid = tie(sum_g, n_k2, n_r2, tok, d_mid)
    d_tokens = tokens_back(n_k2, n_r2, tok, d_mid)
    d_tokens, go_y = tie(d_tokens, go_y)
    go_y, go_k = tie(go_y, go_k)
    go_l = lo_total(go_k, go_y)
    go_l, gq_z = tie(go_l, gq_z)
    gq_z, gk_l = tie(gq_z, gk_l)
    gk_z = ex.hi_swap(gk_l)
    gq_z, gain_attn, w_query = tie(gq_z, gain_attn, w_query)
    grad_query, sum_q = query_grads(gq_z, gain_attn, w_query)
    sum_q, gk_z = tie(sum_q, gk_z)
    gk_z, go_l = tie(gk_z, go_l)
    go_z = ex.hi_swap(go_l)
    gk_z, gain_attn, w_key, w_value = tie(gk_z, gain_attn, w_key, w_value)
    grad_key, grad_value, sum_k = key_grads(gk_z, gain_attn, w_key, w_value)
    sum_k, sum_q, sum_g, sum_u = tie(sum_k, sum_q, sum_g, sum_u)
    gains = jnp.stack([sum_q + sum_k, sum_g + sum_u])
    gains_x = ex.flip(gains, 2)
    gains, gains_x = tie(gains, gains_x)
    gains_x, gains = tie(gains_x, gains)
    gains2 = gains + gains_x
    gains_c = ex.flip(gains2, 1)
    gains2, gains_c = tie(gains2, gains_c)
    gains_c, gains2 = tie(gains_c, gains2)
    grad_gain_attn, grad_gain_mlp = gains2 + gains_c
    grad_gain_mlp, go_z = tie(grad_gain_mlp, go_z)
    grad_out = hi_total(go_z).T
    return (
        layer_out,
        d_tokens,
        grad_gain_attn,
        grad_query,
        grad_key,
        grad_value,
        grad_out,
        grad_gain_mlp,
        grad_gate,
        grad_up,
        grad_down,
    )


def solution(mesh):
    rows = P(("fsdp", "tp"), None)
    in_specs = (
        rows,
        rows,
        P(),
        P(),
        P("fsdp"),
        P("fsdp", "tp"),
        P("fsdp", "tp"),
        P("fsdp", "tp"),
        P("tp", "fsdp"),
        P("fsdp"),
        P("fsdp", "tp"),
        P("fsdp", "tp"),
        P("tp", "fsdp"),
    )
    out_specs = (
        rows,
        rows,
        P("fsdp"),
        P("fsdp", "tp"),
        P("fsdp", "tp"),
        P("fsdp", "tp"),
        P("tp", "fsdp"),
        P("fsdp"),
        P("fsdp", "tp"),
        P("fsdp", "tp"),
        P("tp", "fsdp"),
    )
    return jax.shard_map(
        functools.partial(local, Exchange(mesh)), mesh=mesh, in_specs=in_specs, out_specs=out_specs, check_vma=False
    )
```

```python
import functools

import jax
import jax.numpy as jnp
from jax import lax
from jax.experimental import pallas as pl
from jax.experimental.pallas import tpu as pltpu
from jax.sharding import PartitionSpec as P

HEAD_DIM = 128
EPS = 1e-05
THETA = 10000.0
FLOOR = -1e30
LOG2E = 1.4426950408889634
MIB = 1024 * 1024
F32 = jnp.float32
BF16 = jnp.bfloat16
HI = 4


def angles(places, width):
    half = width // 2
    freq = 1.0 / THETA ** (jnp.arange(half, dtype=F32) * 2.0 / width)
    angle = places.astype(F32)[:, None] * freq[None, :]
    cosine = jnp.cos(angle)
    sine = jnp.sin(angle)
    return (jnp.concatenate([cosine, cosine], -1), jnp.concatenate([sine, sine], -1))


def documents(doc_starts, skip_flags, row_index):
    inside = doc_starts[None, :] <= row_index[:, None]
    segment = jnp.sum(inside.astype(jnp.int32), axis=1) - 1
    begins = jnp.max(jnp.where(inside, doc_starts[None, :], 0), axis=1)
    chosen = segment[:, None] == jnp.arange(doc_starts.shape[0], dtype=jnp.int32)[None, :]
    skipped = jnp.sum(jnp.where(chosen, skip_flags[None, :], 0), axis=1)
    return (begins, (1 - skipped).astype(F32))


def product(left, right):
    return jnp.dot(left, right, preferred_element_type=F32)


def against(left, right):
    return lax.dot_general(left, right, (((1,), (1,)), ((), ())), preferred_element_type=F32)


def outer_sum(left, right):
    return lax.dot_general(left, right, (((0,), (0,)), ((), ())), preferred_element_type=F32)


def block_rows_of(block, bounds, lo, size):
    piece = lax.rem(lax.rem(block, lo) - bounds[2] + lo, lo)
    place = piece * HI + lax.div(block, lo)
    return pl.ds(pl.multiple_of(place * size, size), size)


def closed_keys(block, size, koff_ref, qrow_ref, beg_ref):
    krow = koff_ref[...] + block * size
    return jnp.where((krow <= qrow_ref[...]) & (krow >= beg_ref[...]), 0.0, FLOOR)


def attend_kernel(heads, lo, bounds, q_ref, kv_ref, qrow_ref, beg_ref, koff_ref, o_ref, lse_ref, top, mass, acc):
    size = koff_ref.shape[0]
    factor = HEAD_DIM**-0.5 * LOG2E
    top[...] = jnp.full_like(top, FLOOR)
    mass[...] = jnp.zeros_like(mass)
    acc[...] = jnp.zeros_like(acc)

    def step(block, carry):
        rows = block_rows_of(block, bounds, lo, size)
        keys = kv_ref[rows, :HEAD_DIM]
        values = kv_ref[rows, HEAD_DIM:].astype(F32).T.astype(BF16)
        closed = closed_keys(block, size, koff_ref, qrow_ref, beg_ref)
        for h in range(heads):
            scores = against(keys, q_ref[:, h * HEAD_DIM : (h + 1) * HEAD_DIM]) * factor + closed
            before = top[h]
            now = jnp.maximum(before, jnp.max(scores, axis=0, keepdims=True))
            weights = jnp.exp2(scores - now)
            fading = jnp.exp2(before - now)
            top[h] = now
            mass[h] = mass[h] * fading + jnp.sum(weights, axis=0, keepdims=True)
            acc[h] = acc[h] * fading + product(values, weights.astype(BF16))
        return carry

    lax.fori_loop(bounds[0], bounds[1] + 1, step, 0)
    for h in range(heads):
        o_ref[:, h * HEAD_DIM : (h + 1) * HEAD_DIM] = (acc[h] / mass[h]).T.astype(BF16)
        lse_ref[h] = top[h] + jnp.log2(mass[h])


def attend_back_kernel(
    heads, lo, bounds, q_ref, kv_ref, o_ref, do_ref, lse_ref, qrow_ref, beg_ref, koff_ref, cos_ref, sin_ref,
    dq_ref, dkv_ref, delta, acc
):
    size = koff_ref.shape[0]
    factor = HEAD_DIM**-0.5
    acc[...] = jnp.zeros_like(acc)
    dkv_ref[...] = jnp.zeros_like(dkv_ref)
    for h in range(heads):
        cols = slice(h * HEAD_DIM, (h + 1) * HEAD_DIM)
        both = do_ref[:, cols].astype(F32) * o_ref[:, cols].astype(F32)
        delta[h] = jnp.sum(both.T, axis=0, keepdims=True)

    def step(block, carry):
        rows = block_rows_of(block, bounds, lo, size)
        keys = kv_ref[rows, :HEAD_DIM]
        values = kv_ref[rows, HEAD_DIM:]
        turned_keys = keys.astype(F32).T.astype(BF16)
        closed = closed_keys(block, size, koff_ref, qrow_ref, beg_ref)
        dkeys = jnp.zeros((size, HEAD_DIM), F32)
        dvalues = jnp.zeros((size, HEAD_DIM), F32)
        for h in range(heads):
            cols = slice(h * HEAD_DIM, (h + 1) * HEAD_DIM)
            queries = q_ref[:, cols]
            grads = do_ref[:, cols]
            scores = against(keys, queries) * (factor * LOG2E) + closed
            probs = jnp.exp2(scores - lse_ref[h])
            dvalues = dvalues + product(probs.astype(BF16), grads)
            dprobs = against(values, grads)
            dscores = (probs * ((dprobs - delta[h]) * factor)).astype(BF16)
            acc[h] = acc[h] + product(turned_keys, dscores)
            dkeys = dkeys + product(dscores, queries)
        dkv_ref[rows, :HEAD_DIM] = dkeys.astype(BF16)
        dkv_ref[rows, HEAD_DIM:] = dvalues.astype(BF16)
        return carry

    lax.fori_loop(bounds[0], bounds[1] + 1, step, 0)
    for h in range(heads):
        grads = acc[h].T
        back = grads * cos_ref[...] - pltpu.roll(grads, HEAD_DIM // 2, 1) * sin_ref[...]
        dq_ref[:, h * HEAD_DIM : (h + 1) * HEAD_DIM] = back.astype(BF16)


VMEM_SPEC = pl.BlockSpec(memory_space=pltpu.VMEM)
SMEM_SPEC = pl.BlockSpec(memory_space=pltpu.SMEM)
NOTHING = pl.CostEstimate(flops=1, bytes_accessed=1, transcendentals=0)


def attend(bounds, q, kv, qrow, beg, koff, lo):
    rows, width = q.shape
    heads = width // HEAD_DIM
    return pl.pallas_call(
        functools.partial(attend_kernel, heads, lo),
        out_shape=(
            jax.ShapeDtypeStruct((rows, width), BF16),
            jax.ShapeDtypeStruct((heads, 1, rows), F32),
        ),
        in_specs=[SMEM_SPEC] + [VMEM_SPEC] * 5,
        out_specs=(VMEM_SPEC, VMEM_SPEC),
        scratch_shapes=[
            pltpu.VMEM((heads, 1, rows), F32),
            pltpu.VMEM((heads, 1, rows), F32),
            pltpu.VMEM((heads, HEAD_DIM, rows), F32),
        ],
        compiler_params=pltpu.CompilerParams(vmem_limit_bytes=16 * MIB),
        cost_estimate=NOTHING,
    )(bounds, q, kv, qrow, beg, koff)


def attend_back(bounds, q, kv, o, do, lse, qrow, beg, koff, cosine, signed, lo):
    rows, width = q.shape
    heads = width // HEAD_DIM
    return pl.pallas_call(
        functools.partial(attend_back_kernel, heads, lo),
        out_shape=(
            jax.ShapeDtypeStruct((rows, width), BF16),
            jax.ShapeDtypeStruct(kv.shape, BF16),
        ),
        in_specs=[SMEM_SPEC] + [VMEM_SPEC] * 10,
        out_specs=(VMEM_SPEC, VMEM_SPEC),
        scratch_shapes=[
            pltpu.VMEM((heads, 1, rows), F32),
            pltpu.VMEM((heads, HEAD_DIM, rows), F32),
        ],
        compiler_params=pltpu.CompilerParams(vmem_limit_bytes=16 * MIB),
        cost_estimate=NOTHING,
    )(bounds, q, kv, o, do, lse, qrow, beg, koff, cosine, signed)


class Exchange:
    def __init__(self, mesh):
        self.shards = mesh.shape["fsdp"]
        self.hi = HI
        self.lo = self.shards // HI
        self.tp = mesh.shape["tp"]
        self.hi_groups = [[h * self.lo + b for h in range(self.hi)] for b in range(self.lo)]

    def lo_shift(self, v, s):
        pairs = [
            (h * self.lo + b, h * self.lo + (b + s) % self.lo) for h in range(self.hi) for b in range(self.lo)
        ]
        return lax.ppermute(v, "fsdp", pairs)

    def flip(self, v, mask):
        return lax.ppermute(v, "tp", [(t, t ^ mask) for t in range(self.tp)])

    def hi_swap(self, v):
        return lax.all_to_all(v, "fsdp", 0, 0, axis_index_groups=self.hi_groups)

    def hi_copies(self, w):
        return self.hi_swap(jnp.broadcast_to(w[None], (self.hi,) + w.shape))

    def lo_gather(self, v):
        return tuple(self.lo_shift(v, -s) for s in range(1, self.lo))

    def lo_scatter(self, v):
        m = v.shape[0] // (self.lo - 1)
        return tuple(self.lo_shift(v[s * m : (s + 1) * m], s + 1) for s in range(self.lo - 1))

    def hi_rows(self, v):
        return self.hi_copies(v).reshape(self.hi * v.shape[0], v.shape[1])

    def turned_lo(self, parts, start):
        if self.lo == 2:
            return [jnp.where(start == 0, parts[0], parts[1]), jnp.where(start == 0, parts[1], parts[0])]
        both = jnp.concatenate([part[None] for part in parts + parts], axis=0)
        both = lax.dynamic_slice_in_dim(both, start, self.lo, axis=0)
        return [both[s] for s in range(self.lo)]

    def to_pieces(self, v):
        n = v.shape[1] // self.shards
        b = lax.axis_index("fsdp") % self.lo
        parts = [
            jnp.concatenate([v[:, (h * self.lo + l) * n : (h * self.lo + l + 1) * n] for h in range(self.hi)], axis=1)
            for l in range(self.lo)
        ]
        return jnp.concatenate(self.turned_lo(parts, b), axis=1)

    def from_pieces(self, v):
        n = v.shape[1] // self.shards
        b = lax.axis_index("fsdp") % self.lo
        own = self.hi * n
        parts = [v[:, s * own : (s + 1) * own] for s in range(self.lo)]
        parts = self.turned_lo(parts, (self.lo - b) % self.lo)
        return jnp.concatenate(
            [parts[l][:, h * n : (h + 1) * n] for h in range(self.hi) for l in range(self.lo)], axis=1
        )

    def quarters(self, w):
        n, k = w.shape
        chunk = -(-k // (self.hi * 128)) * 128
        w = jnp.pad(w, ((0, 0), (0, self.hi * chunk - k)))
        return w.reshape(n, self.hi, chunk).transpose(1, 0, 2)


def kernel_call(kernel, outs, args, flops, scratch=(), limit=16):
    return pl.pallas_call(
        kernel,
        out_shape=outs,
        in_specs=[VMEM_SPEC] * len(args),
        out_specs=jax.tree.map(lambda _: VMEM_SPEC, outs),
        scratch_shapes=list(scratch),
        compiler_params=pltpu.CompilerParams(vmem_limit_bytes=limit * MIB),
        cost_estimate=NOTHING,
    )(*args)


def shape(dims, kind):
    return jax.ShapeDtypeStruct(tuple(dims), kind)


def flat(pieces):
    return [p.reshape(-1, p.shape[-1]) for p in pieces]


def through(x_ref, pieces):
    depth = x_ref.shape[1] // len(pieces)
    total = None
    for s, piece in enumerate(pieces):
        part = product(x_ref[:, s * depth : (s + 1) * depth], piece[...])
        total = part if total is None else total + part
    return total


def turned(v, cosine, signed):
    return v * cosine + pltpu.roll(v, HEAD_DIM // 2, 1) * signed


def key_value(x, pieces, cosine, signed):
    def kernel(x_ref, *refs):
        *ws, cos_ref, sin_ref, out_ref = refs
        raw = through(x_ref, ws)
        out_ref[:, :HEAD_DIM] = turned(raw[:, :HEAD_DIM], cos_ref[...], sin_ref[...]).astype(BF16)
        out_ref[:, HEAD_DIM:] = raw[:, HEAD_DIM:].astype(BF16)

    rows, k = x.shape[0], pieces[0].shape[1]
    return kernel_call(kernel, shape((rows, k), BF16), (x, *pieces, cosine, signed), 2 * rows * k * x.shape[1])


def query(x, pieces, cosine, signed):
    def kernel(x_ref, *refs):
        *ws, cos_ref, sin_ref, out_ref = refs
        raw = through(x_ref, ws)
        for c in range(0, out_ref.shape[1], HEAD_DIM):
            cols = slice(c, c + HEAD_DIM)
            out_ref[:, cols] = turned(raw[:, cols], cos_ref[...], sin_ref[...]).astype(BF16)

    rows, k = x.shape[0], pieces[0].shape[1]
    return kernel_call(kernel, shape((rows, k), BF16), (x, *pieces, cosine, signed), 2 * rows * k * x.shape[1])


def project(x, pieces):
    def kernel(x_ref, *refs):
        *ws, out_ref = refs
        out_ref[...] = through(x_ref, ws).astype(BF16)

    rows, k = x.shape[0], pieces[0].shape[1]
    return kernel_call(kernel, shape((rows, k), BF16), (x, *pieces), 2 * rows * k * x.shape[1])


def expand(terms, extra=None):
    rows = terms[0][0].shape[0]
    half = rows // 2
    lo = len(terms[0][1])
    depth = terms[0][1][0].shape[0]
    width = lo * depth

    def kernel(*refs):
        keep_ref, send_ref = refs[-2:]
        groups = [refs[g * (lo + 1) : (g + 1) * (lo + 1)] for g in range(len(terms))]
        for s in range(lo):
            cols = slice(s * depth, (s + 1) * depth)
            total = None
            for group in groups:
                part = against(group[0][...], group[1 + s][...])
                total = part if total is None else total + part
            keep_ref[:, cols] = total[:half]
            send_ref[:, cols] = total[half:].astype(BF16)

    flops = sum(2 * rows * t[0].shape[1] * width for t in terms)
    args = tuple(a for t in terms for a in (t[0], *t[1]))
    return kernel_call(kernel, (shape((half, width), F32), shape((half, width), BF16)), args, flops)


def feed_forward(upper, lower, gates, ups):
    half, depth = upper.shape
    rows = 2 * half
    lo = len(gates) // 2
    chunk = gates[0].shape[1]

    def kernel(upper_ref, lower_ref, *refs):
        x_ref, gate_ref, up_ref, hidden_ref = refs[-4:]
        x_ref[:half] = upper_ref[...]
        x_ref[half:] = lower_ref[...]
        for side in range(2):
            cols = slice(side * chunk, (side + 1) * chunk)
            gate = through(x_ref, refs[side * lo : (side + 1) * lo])
            up = through(x_ref, refs[(2 + side) * lo : (3 + side) * lo])
            gate_ref[:, cols] = gate
            up_ref[:, cols] = up
            hidden_ref[:, cols] = (gate * jax.nn.sigmoid(gate) * up).astype(BF16)

    dims = (rows, 2 * chunk)
    outs = (shape((rows, depth), BF16), shape(dims, F32), shape(dims, F32), shape(dims, BF16))
    return kernel_call(kernel, outs, (upper, lower, *gates, *ups), 1, limit=20)


def feed_back(upper, lower, downs, gate, up):
    half, depth = upper.shape
    rows, width = gate.shape
    chunk = width // 2
    lo = len(downs) // 2

    def kernel(upper_ref, lower_ref, *refs):
        gate_ref, up_ref, d_ref, dgate_ref, dup_ref = refs[-5:]
        d_ref[:half] = upper_ref[...]
        d_ref[half:] = lower_ref[...]
        for side in range(2):
            cols = slice(side * chunk, (side + 1) * chunk)
            gates = gate_ref[:, cols]
            sigma = jax.nn.sigmoid(gates)
            scaled = through(d_ref, refs[side * lo : (side + 1) * lo]) * sigma
            dgate_ref[:, cols] = (scaled * up_ref[:, cols] * (1.0 + gates * (1.0 - sigma))).astype(BF16)
            dup_ref[:, cols] = (scaled * gates).astype(BF16)

    dims = (rows, width)
    outs = (shape((rows, depth), BF16), shape(dims, BF16), shape(dims, BF16))
    return kernel_call(kernel, outs, (upper, lower, *downs, gate, up), 1, limit=20)


def weight_sums(x, d, first, k, lo, extra=None):
    rows, width = x.shape
    own = width // lo

    def kernel(x_ref, d_ref, *refs):
        keep_ref, send_ref = refs[-2:]
        dcols = d_ref[:, first : first + k]
        for s in range(lo):
            part = slice(s * own, (s + 1) * own)
            total = outer_sum(x_ref[:, part], dcols)
            if extra is not None:
                total = total + refs[0][part, :].astype(F32)
            if s == 0:
                keep_ref[...] = total
            else:
                send_ref[(s - 1) * own : s * own, :] = total.astype(BF16)

    args = (x, d) + (() if extra is None else (extra,))
    outs = (shape((own, k), F32), shape((width - own, k), BF16))
    return kernel_call(kernel, outs, args, 2 * rows * k * width)


def weight_sums_sent(x, d, first, k):
    def kernel(x_ref, d_ref, out_ref):
        out_ref[...] = outer_sum(x_ref[...], d_ref[:, first : first + k]).astype(BF16)

    rows, width = x.shape
    return kernel_call(kernel, shape((width, k), BF16), (x, d), 2 * rows * k * width)


def tie(*values):
    return lax.optimization_barrier(values)


def local(
    ex,
    tokens,
    cotangent,
    doc_starts,
    skip_flags,
    gain_attn,
    w_query,
    w_key,
    w_value,
    w_out,
    gain_mlp,
    w_gate,
    w_up,
    w_down,
):
    count, width = tokens.shape
    q_width = w_query.shape[1]
    k_width = w_key.shape[1]
    hidden_width = w_gate.shape[1]
    n = w_gate.shape[0]
    chunk = -(-hidden_width // (ex.hi * 128)) * 128
    block_rows = count * ex.tp
    fsdp = lax.axis_index("fsdp")
    tp = lax.axis_index("tp")
    offsets = jnp.arange(count, dtype=jnp.int32)
    koff = jnp.concatenate([(tp ^ m) * count + offsets for m in (0, 2, 1, 3)])


    def gained(w, gain):
        return (w.astype(F32) * gain.astype(F32)[:, None]).astype(BF16)

    def normed(x):
        x = x.astype(F32)
        return x, lax.rsqrt(jnp.mean(x * x, axis=-1, keepdims=True) + EPS)

    def rows_of(doc_starts, skip_flags):
        row_index = fsdp * block_rows + koff
        begins, keep_rows = documents(doc_starts, skip_flags, row_index)
        cosine, sine = angles(row_index - begins, HEAD_DIM)
        half = HEAD_DIM // 2
        signed = jnp.concatenate([-sine[:, :half], sine[:, half:]], axis=1)
        bounds = jnp.stack([jnp.min(begins) // block_rows, fsdp, fsdp % ex.lo]).astype(jnp.int32)
        return cosine, signed, row_index[None, :], begins[None, :], bounds, keep_rows[:count, None]

    def cotangents(cotangent, keep):
        cot = ex.to_pieces(cotangent)
        return cot, (keep * cot.astype(F32)).astype(BF16)

    def joined(v, *got):
        return jnp.concatenate([v, *got], axis=0)

    def normed_rows(first, got):
        x, scale = normed(joined(first, got))
        return (x * scale).astype(BF16)

    def attention(qu, own_piece, others, qrow, beg, bounds):
        kv_all = jnp.concatenate(flat((own_piece, *others)), axis=0)
        attended, lse = attend(bounds, qu, kv_all, qrow, beg, koff[:, None], ex.lo)
        return attended, lse, kv_all

    def attention_back(qu, kva, att, datt, lse, qrow, beg, bounds, cosine, signed):
        dq, dkv = attend_back(bounds, qu, kva, att, datt, lse, qrow, beg, koff[:, None], cosine, signed, ex.lo)
        m = dkv.shape[0] // ex.lo
        return dq, dkv[:m], dkv[m:]

    def halves(keep, got):
        g = keep + got.astype(F32)
        return g[: g.shape[0] // 2], g[g.shape[0] // 2 :].astype(BF16)

    def added(keep, got):
        return (keep + got.astype(F32)).astype(BF16).reshape(ex.hi, count, width)

    def summed(kept, got):
        for v in got:
            kept = kept + v.astype(F32)
        return kept

    def middle_of(kept, got, tok, keep):
        middle, scale = normed(tok.astype(F32) + keep * (kept + got.astype(F32)))
        return middle, (middle * scale).astype(BF16)

    def sides(p0, p1, p2, p3):
        return flat((p0, *p1, p2, *p3))

    def feed_back_rows(dgate, dup, *ws):
        gates, ups = sides(*ws[:4]), sides(*ws[4:])
        return expand(
            [
                (dgate[:, :chunk], gates[: ex.lo]),
                (dgate[:, chunk:], gates[ex.lo :]),
                (dup[:, :chunk], ups[: ex.lo]),
                (dup[:, chunk:], ups[ex.lo :]),
            ]
        )

    def down_rows(hid, *ws):
        downs = sides(*ws)
        return expand([(hid[:, :chunk], downs[: ex.lo]), (hid[:, chunk:], downs[ex.lo :])])

    def hi_total(got):
        return jnp.sum(got.astype(F32), axis=0)

    def layer_rows(got, middle, keep):
        return ex.from_pieces((middle + keep * hi_total(got)).astype(BF16))

    def middle_back(got, middle, cot, keep):
        scaled = hi_total(got)
        scale = normed(middle)[1]
        d_middle = (
            cot.astype(F32)
            + scale * scaled
            - middle * scale**3 * jnp.mean(scaled * middle, axis=-1, keepdims=True)
        )
        return d_middle, (keep * d_middle).astype(BF16)

    def lo_total(kept, got):
        total = summed(kept.astype(F32), got).astype(BF16)
        return total.reshape(ex.hi, -1, total.shape[1])

    def spread(got):
        return jnp.concatenate([got[h] for h in range(ex.hi)], axis=1)[:, :hidden_width].astype(F32)

    def spread_gained(got, w, gain):
        total = spread(got)
        return total * gain.astype(F32)[:, None], jnp.sum(total * w.astype(F32), axis=1)

    def query_grads(got, gain, *weights):
        total = hi_total(got)
        w = jnp.concatenate(weights, axis=1).astype(F32)
        return total * gain.astype(F32)[:, None], jnp.sum(total * w, axis=1)

    def key_grads(got, gain, *weights):
        total, part = query_grads(got, gain, *weights)
        return total[:, :k_width], total[:, k_width:], part

    def keys_back(got, cosine, signed):
        total = hi_total(got)
        half = k_width // 2
        dk = total[:, :k_width]
        turned_back = dk * cosine - jnp.concatenate([dk[:, half:], dk[:, :half]], axis=1) * signed
        return jnp.concatenate([turned_back, total[:, k_width:]], axis=1).astype(BF16)

    def attention_rows_back(dq, q0, q1, dkv, kv0, kv1):
        return expand([(dq, flat((q0, *q1))), (dkv, flat((kv0, *kv1)))])

    def tokens_back(kept, got, tok, d_mid):
        scaled = kept + got.astype(F32)
        x, scale = normed(tok)
        d_tokens = d_mid + scale * scaled - x * scale**3 * jnp.mean(scaled * x, axis=-1, keepdims=True)
        return ex.from_pieces(d_tokens.astype(BF16))


    w_query, gain_attn = tie(w_query, gain_attn)
    s_q = gained(w_query, gain_attn)
    q0 = ex.hi_copies(s_q)
    tok = ex.to_pieces(tokens)
    tok_x = ex.flip(tok, 2)
    tok, w_key, w_value, gain_attn = tie(tok, w_key, w_value, gain_attn)
    s_kv = gained(jnp.concatenate([w_key, w_value], axis=1), gain_attn)
    s_kv, w_gate, gain_mlp = tie(s_kv, w_gate, gain_mlp)
    s_g = ex.quarters(gained(w_gate, gain_mlp))
    s_g, tok_x = tie(s_g, tok_x)
    tok_x, doc_starts, skip_flags = tie(tok_x, doc_starts, skip_flags)
    cosine, signed, qrow, beg, bounds, keep = rows_of(doc_starts, skip_flags)
    keep, tok, tok_x = tie(keep, tok, tok_x)
    tok2 = joined(tok, tok_x)
    tok_c = ex.flip(tok2, 1)
    tok2, w_out = tie(tok2, w_out)
    s_o = w_out.T
    s_o, tok_c = tie(s_o, tok_c)
    tok_c, tok2 = tie(tok_c, tok2)
    xh = normed_rows(tok2, tok_c)
    xh, s_kv = tie(xh, s_kv)
    kv0 = ex.hi_copies(s_kv)
    xh, q0 = tie(xh, q0)
    q1 = ex.lo_gather(q0)
    q0, w_up, gain_mlp = tie(q0, w_up, gain_mlp)
    s_u = ex.quarters(gained(w_up, gain_mlp))
    s_u, w_down = tie(s_u, w_down)
    s_d = ex.quarters(w_down.T)
    s_d, s_u = tie(s_d, s_u)
    u0 = ex.hi_swap(s_u)
    s_d, kv0 = tie(s_d, kv0)
    kv0, q1 = tie(kv0, q1)
    q1, cotangent, keep = tie(q1, cotangent, keep)
    cot, dm_own = cotangents(cotangent, keep)
    dm_own, kv0 = tie(dm_own, kv0)
    kv1 = ex.lo_gather(kv0)
    dm_own, s_o = tie(dm_own, s_o)
    o0 = ex.hi_copies(s_o)
    dm_own, u0 = tie(dm_own, u0)
    u2 = ex.flip(u0, 2)
    u0, xh, q0, q1, cosine, signed = tie(u0, xh, q0, q1, cosine, signed)
    qu = query(xh, flat((q0, *q1)), cosine, signed)
    qu, kv1 = tie(qu, kv1)
    kv1, u0 = tie(kv1, u0)
    u1 = ex.lo_gather(u0)
    kv1, xh, kv0, cosine, signed = tie(kv1, xh, kv0, cosine, signed)
    kv = key_value(xh, flat((kv0, *kv1)), cosine, signed)
    kv, u2 = tie(kv, u2)
    u2, kv = tie(u2, kv)
    kr0 = ex.hi_copies(kv)
    u2, o0 = tie(u2, o0)
    o1 = ex.lo_gather(o0)
    o0, u1 = tie(o0, u1)
    u3 = tuple(ex.flip(v, 2) for v in u1)
    u1, kr0 = tie(u1, kr0)
    kr0, s_g = tie(kr0, s_g)
    g0 = ex.hi_swap(s_g)
    kr0, o1 = tie(kr0, o1)
    o1, u3 = tie(o1, u3)
    u3, kr0 = tie(u3, kr0)
    kr1 = ex.lo_gather(kr0)
    u3, g0 = tie(u3, g0)
    g2 = ex.flip(g0, 2)
    g0, kr1 = tie(g0, kr1)
    kr1, dm_own = tie(kr1, dm_own)
    dm4 = ex.hi_rows(dm_own)
    kr1, g0 = tie(kr1, g0)
    g1 = ex.lo_gather(g0)
    kr1, qu, kr0, qrow, beg, bounds = tie(kr1, qu, kr0, qrow, beg, bounds)
    att, lse, kva = attention(qu, kr0, kr1, qrow, beg, bounds)
    kva, g2 = tie(kva, g2)
    g2, dm4 = tie(g2, dm4)
    dm4, g1 = tie(dm4, g1)
    g1, s_d = tie(g1, s_d)
    d0 = ex.hi_swap(s_d)
    g1, att, o0, o1 = tie(g1, att, o0, o1)
    ao_k, ao_s = expand([(att, flat((o0, *o1)))])
    ao_s, g1 = tie(ao_s, g1)
    g3 = tuple(ex.flip(v, 2) for v in g1)
    ao_r = ex.flip(ao_s, 1)
    ao_k, dm4 = tie(ao_k, dm4)
    dm_c = ex.flip(dm4, 1)
    ao_k, g3 = tie(ao_k, g3)
    g3, ao_r = tie(g3, ao_r)
    ao_r, ao_k = tie(ao_r, ao_k)
    ao_k2, ao_s2 = halves(ao_k, ao_r)
    ao_s2, dm_c = tie(ao_s2, dm_c)
    dm_c, ao_s2 = tie(dm_c, ao_s2)
    ao_r2 = ex.flip(ao_s2, 2)
    dm_c, d0 = tie(dm_c, d0)
    d1 = ex.lo_gather(d0)
    d2 = ex.flip(d0, 2)
    d0, ao_r2 = tie(d0, ao_r2)
    ao_r2, ao_k2, tok, keep = tie(ao_r2, ao_k2, tok, keep)
    middle, nrm = middle_of(ao_k2, ao_r2, tok, keep)
    nm4 = ex.hi_rows(nrm)
    middle, d1 = tie(middle, d1)
    d1, d2 = tie(d1, d2)
    d2, d1 = tie(d2, d1)
    d3 = tuple(ex.flip(v, 2) for v in d1)
    d2, nm4 = tie(d2, nm4)
    nm_c = ex.flip(nm4, 1)
    nm4, nm_c = tie(nm4, nm_c)
    nm_c, nm4, g0, g1, g2, g3, u0, u1, u2, u3 = tie(nm_c, nm4, g0, g1, g2, g3, u0, u1, u2, u3)
    nm, gate, up, hid = feed_forward(nm4, nm_c, sides(g0, g1, g2, g3), sides(u0, u1, u2, u3))
    hid, d3 = tie(hid, d3)
    d3, dm4, dm_c, d0, d1, d2, gate, up = tie(d3, dm4, dm_c, d0, d1, d2, gate, up)
    dm, dgate, dup = feed_back(dm4, dm_c, sides(d0, d1, d2, d3), gate, up)
    dup, nm = tie(dup, nm)
    gu_x = weight_sums_sent(nm, dup, chunk, chunk)
    gu_r = ex.flip(gu_x, 2)
    dup, dgate, g0, g1, g2, g3, u0, u1, u2, u3 = tie(dup, dgate, g0, g1, g2, g3, u0, u1, u2, u3)
    e_k, e_s = feed_back_rows(dgate, dup, g0, g1, g2, g3, u0, u1, u2, u3)
    c3_r = ex.flip(e_s, 1)
    e_k, hid, d0, d1, d2, d3 = tie(e_k, hid, d0, d1, d2, d3)
    m_k, m_s = down_rows(hid, d0, d1, d2, d3)
    m_s, c3_r = tie(m_s, c3_r)
    c3_r, dm, hid = tie(c3_r, dm, hid)
    gd_x = weight_sums_sent(dm, hid, chunk, chunk)
    gd_x, m_s = tie(gd_x, m_s)
    mo_r = ex.flip(m_s, 1)
    gd_x, e_k, c3_r = tie(gd_x, e_k, c3_r)
    c3_s = added(e_k, c3_r)
    c3_z = ex.hi_swap(c3_s)
    gd_x, mo_r = tie(gd_x, mo_r)
    mo_r, m_k = tie(mo_r, m_k)
    mo_s = added(m_k, mo_r)
    mo_s, nm, dgate = tie(mo_s, nm, dgate)
    gg_x = weight_sums_sent(nm, dgate, chunk, chunk)
    gg_x, gu_r = tie(gg_x, gu_r)
    gu_r, gd_x = tie(gu_r, gd_x)
    gd_r = ex.flip(gd_x, 2)
    gu_r, c3_z = tie(gu_r, c3_z)
    c3_z, nm, dup, gu_r = tie(c3_z, nm, dup, gu_r)
    gu_k, gu_s = weight_sums(nm, dup, 0, chunk, ex.lo, gu_r)
    gu_s, mo_s = tie(gu_s, mo_s)
    mo_z = ex.hi_swap(mo_s)
    gu_y = ex.lo_scatter(gu_s)
    gu_k, c3_z, middle, cot, keep = tie(gu_k, c3_z, middle, cot, keep)
    d_mid, da_own = middle_back(c3_z, middle, cot, keep)
    da_own, gu_y = tie(da_own, gu_y)
    gu_y, gu_k = tie(gu_y, gu_k)
    gu_l = lo_total(gu_k, gu_y)
    gu_l, mo_z = tie(gu_l, mo_z)
    mo_z, gu_l = tie(mo_z, gu_l)
    gu_z = ex.hi_swap(gu_l)
    mo_z, gd_r = tie(mo_z, gd_r)
    gd_r, dm, hid = tie(gd_r, dm, hid)
    gd_k, gd_s = weight_sums(dm, hid, 0, chunk, ex.lo, gd_r)
    gd_y = ex.lo_scatter(gd_s)
    gd_k, da_own = tie(gd_k, da_own)
    da_x = ex.flip(da_own, 2)
    gd_k, gg_x = tie(gd_k, gg_x)
    gg_r = ex.flip(gg_x, 2)
    gd_k, da_x = tie(gd_k, da_x)
    da_x, da_own = tie(da_x, da_own)
    da2 = joined(da_own, da_x)
    da_c = ex.flip(da2, 1)
    da2, da_c = tie(da2, da_c)
    da_c, da2 = tie(da_c, da2)
    da = joined(da2, da_c)
    da, o0, o1 = tie(da, o0, o1)
    datt = project(da, flat((o0, *o1)))
    (
        datt,
        qu,
        kva,
        att,
        lse,
        qrow,
        beg,
        bounds,
        cosine,
        signed,
    ) = tie(
        datt,
        qu,
        kva,
        att,
        lse,
        qrow,
        beg,
        bounds,
        cosine,
        signed,
    )
    dq, dk_k, dk_s = attention_back(qu, kva, att, datt, lse, qrow, beg, bounds, cosine, signed)
    dk_s, gu_z = tie(dk_s, gu_z)
    gu_z, gd_y = tie(gu_z, gd_y)
    gd_y, dk_s = tie(gd_y, dk_s)
    dk_y = ex.lo_scatter(dk_s)
    gd_y, gd_k = tie(gd_y, gd_k)
    gd_l = lo_total(gd_k, gd_y)
    gd_z = ex.hi_swap(gd_l)
    gu_z, xh, dq = tie(gu_z, xh, dq)
    gq_k, gq_s = weight_sums(xh, dq, 0, q_width, ex.lo)
    gq_s, gg_r = tie(gq_s, gg_r)
    gg_r, nm, dgate = tie(gg_r, nm, dgate)
    gg_k, gg_s = weight_sums(nm, dgate, 0, chunk, ex.lo, gg_r)
    gg_y = ex.lo_scatter(gg_s)
    gg_k, dk_y = tie(gg_k, dk_y)
    dk_y, dk_k = tie(dk_y, dk_k)
    dk_l = lo_total(dk_k, dk_y)
    dk_l, gu_z, w_up, gain_mlp = tie(dk_l, gu_z, w_up, gain_mlp)
    grad_up, sum_u = spread_gained(gu_z, w_up, gain_mlp)
    sum_u, gd_z = tie(sum_u, gd_z)
    gd_z, dk_l = tie(gd_z, dk_l)
    dk_z = ex.hi_swap(dk_l)
    gd_z, gq_s = tie(gd_z, gq_s)
    gq_y = ex.lo_scatter(gq_s)
    gd_z, gg_y = tie(gd_z, gg_y)
    gg_y, gg_k = tie(gg_y, gg_k)
    gg_l = lo_total(gg_k, gg_y)
    gg_z = ex.hi_swap(gg_l)
    gd_z, dk_z = tie(gd_z, dk_z)
    dk_z, cosine, signed = tie(dk_z, cosine, signed)
    dkv = keys_back(dk_z, cosine, signed)
    dkv, dq, q0, q1, kv0, kv1 = tie(dkv, dq, q0, q1, kv0, kv1)
    n_k, n_s = attention_rows_back(dq, q0, q1, dkv, kv0, kv1)
    n_s, xh, dkv = tie(n_s, xh, dkv)
    gk_k, gk_s = weight_sums(xh, dkv, 0, 2 * k_width, ex.lo)
    gk_y = ex.lo_scatter(gk_s)
    gk_k, da, att = tie(gk_k, da, att)
    go_k, go_s = weight_sums(da, att, 0, q_width, ex.lo)
    go_y = ex.lo_scatter(go_s)
    go_k, n_s = tie(go_k, n_s)
    n_r = ex.flip(n_s, 1)
    go_k, gd_z = tie(go_k, gd_z)
    grad_down = spread(gd_z).T
    grad_down, n_r = tie(grad_down, n_r)
    n_r, n_k = tie(n_r, n_k)
    n_k2, n_s2 = halves(n_k, n_r)
    n_r2 = ex.flip(n_s2, 2)
    n_k2, gq_y = tie(n_k2, gq_y)
    gq_y, gq_k = tie(gq_y, gq_k)
    gq_l = lo_total(gq_k, gq_y)
    gq_l, gg_z = tie(gq_l, gg_z)
    gg_z, gq_l = tie(gg_z, gq_l)
    gq_z = ex.hi_swap(gq_l)
    gg_z, gk_y = tie(gg_z, gk_y)
    gk_y, gk_k = tie(gk_y, gk_k)
    gk_l = lo_total(gk_k, gk_y)
    gk_l, n_r2 = tie(gk_l, n_r2)
    n_r2, gg_z, w_gate, gain_mlp = tie(n_r2, gg_z, w_gate, gain_mlp)
    grad_gate, sum_g = spread_gained(gg_z, w_gate, gain_mlp)
    sum_g, n_k2, n_r2, tok, d_mid = tie(sum_g, n_k2, n_r2, tok, d_mid)
    d_tokens = tokens_back(n_k2, n_r2, tok, d_mid)
    d_tokens, go_y = tie(d_tokens, go_y)
    go_y, go_k = tie(go_y, go_k)
    go_l = lo_total(go_k, go_y)
    go_l, gq_z = tie(go_l, gq_z)
    gq_z, gk_l = tie(gq_z, gk_l)
    gk_z = ex.hi_swap(gk_l)
    gq_z, mo_z, middle, keep = tie(gq_z, mo_z, middle, keep)
    layer_out = layer_rows(mo_z, middle, keep)
    layer_out, gq_z, gain_attn, w_query = tie(layer_out, gq_z, gain_attn, w_query)
    grad_query, sum_q = query_grads(gq_z, gain_attn, w_query)
    sum_q, gk_z = tie(sum_q, gk_z)
    gk_z, go_l = tie(gk_z, go_l)
    go_z = ex.hi_swap(go_l)
    gk_z, gain_attn, w_key, w_value = tie(gk_z, gain_attn, w_key, w_value)
    grad_key, grad_value, sum_k = key_grads(gk_z, gain_attn, w_key, w_value)
    sum_k, sum_q, sum_g, sum_u = tie(sum_k, sum_q, sum_g, sum_u)
    gains = jnp.stack([sum_q + sum_k, sum_g + sum_u])
    gains_x = ex.flip(gains, 2)
    gains, gains_x = tie(gains, gains_x)
    gains_x, gains = tie(gains_x, gains)
    gains2 = gains + gains_x
    gains_c = ex.flip(gains2, 1)
    gains2, gains_c = tie(gains2, gains_c)
    gains_c, gains2 = tie(gains_c, gains2)
    grad_gain_attn, grad_gain_mlp = gains2 + gains_c
    grad_gain_mlp, go_z = tie(grad_gain_mlp, go_z)
    grad_out = hi_total(go_z).T
    return (
        layer_out,
        d_tokens,
        grad_gain_attn,
        grad_query,
        grad_key,
        grad_value,
        grad_out,
        grad_gain_mlp,
        grad_gate,
        grad_up,
        grad_down,
    )


def solution(mesh):
    rows = P(("fsdp", "tp"), None)
    in_specs = (
        rows,
        rows,
        P(),
        P(),
        P("fsdp"),
        P("fsdp", "tp"),
        P("fsdp", "tp"),
        P("fsdp", "tp"),
        P("tp", "fsdp"),
        P("fsdp"),
        P("fsdp", "tp"),
        P("fsdp", "tp"),
        P("tp", "fsdp"),
    )
    out_specs = (
        rows,
        rows,
        P("fsdp"),
        P("fsdp", "tp"),
        P("fsdp", "tp"),
        P("fsdp", "tp"),
        P("tp", "fsdp"),
        P("fsdp"),
        P("fsdp", "tp"),
        P("fsdp", "tp"),
        P("tp", "fsdp"),
    )
    return jax.shard_map(
        functools.partial(local, Exchange(mesh)), mesh=mesh, in_specs=in_specs, out_specs=out_specs, check_vma=False
    )
```

```python
import functools

import jax
import jax.numpy as jnp
from jax import lax
from jax.experimental import pallas as pl
from jax.experimental.pallas import tpu as pltpu
from jax.sharding import PartitionSpec as P

HEAD_DIM = 128
EPS = 1e-05
THETA = 10000.0
FLOOR = -1e30
LOG2E = 1.4426950408889634
MIB = 1024 * 1024
F32 = jnp.float32
BF16 = jnp.bfloat16
HI = 4


def angles(places, width):
    half = width // 2
    freq = 1.0 / THETA ** (jnp.arange(half, dtype=F32) * 2.0 / width)
    angle = places.astype(F32)[:, None] * freq[None, :]
    cosine = jnp.cos(angle)
    sine = jnp.sin(angle)
    return (jnp.concatenate([cosine, cosine], -1), jnp.concatenate([sine, sine], -1))


def documents(doc_starts, skip_flags, row_index):
    inside = doc_starts[None, :] <= row_index[:, None]
    segment = jnp.sum(inside.astype(jnp.int32), axis=1) - 1
    begins = jnp.max(jnp.where(inside, doc_starts[None, :], 0), axis=1)
    chosen = segment[:, None] == jnp.arange(doc_starts.shape[0], dtype=jnp.int32)[None, :]
    skipped = jnp.sum(jnp.where(chosen, skip_flags[None, :], 0), axis=1)
    return (begins, (1 - skipped).astype(F32))


def product(left, right):
    return jnp.dot(left, right, preferred_element_type=F32)


def against(left, right):
    return lax.dot_general(left, right, (((1,), (1,)), ((), ())), preferred_element_type=F32)


def outer_sum(left, right):
    return lax.dot_general(left, right, (((0,), (0,)), ((), ())), preferred_element_type=F32)


def block_rows_of(block, bounds, lo, size):
    piece = lax.rem(lax.rem(block, lo) - bounds[2] + lo, lo)
    place = piece * HI + lax.div(block, lo)
    return pl.ds(pl.multiple_of(place * size, size), size)


def closed_keys(block, size, koff_ref, qrow_ref, beg_ref):
    krow = koff_ref[...] + block * size
    return jnp.where((krow <= qrow_ref[...]) & (krow >= beg_ref[...]), 0.0, FLOOR)


def attend_kernel(heads, lo, bounds, q_ref, kv_ref, qrow_ref, beg_ref, koff_ref, o_ref, lse_ref, top, mass, acc):
    size = koff_ref.shape[0]
    factor = HEAD_DIM**-0.5 * LOG2E
    top[...] = jnp.full_like(top, FLOOR)
    mass[...] = jnp.zeros_like(mass)
    acc[...] = jnp.zeros_like(acc)

    def step(block, carry):
        rows = block_rows_of(block, bounds, lo, size)
        keys = kv_ref[rows, :HEAD_DIM]
        values = kv_ref[rows, HEAD_DIM:].astype(F32).T.astype(BF16)
        closed = closed_keys(block, size, koff_ref, qrow_ref, beg_ref)
        for h in range(heads):
            scores = against(keys, q_ref[:, h * HEAD_DIM : (h + 1) * HEAD_DIM]) * factor + closed
            before = top[h]
            now = jnp.maximum(before, jnp.max(scores, axis=0, keepdims=True))
            weights = jnp.exp2(scores - now)
            fading = jnp.exp2(before - now)
            top[h] = now
            mass[h] = mass[h] * fading + jnp.sum(weights, axis=0, keepdims=True)
            acc[h] = acc[h] * fading + product(values, weights.astype(BF16))
        return carry

    lax.fori_loop(bounds[0], bounds[1] + 1, step, 0)
    for h in range(heads):
        o_ref[:, h * HEAD_DIM : (h + 1) * HEAD_DIM] = (acc[h] / mass[h]).T.astype(BF16)
        lse_ref[h] = top[h] + jnp.log2(mass[h])


def attend_back_kernel(
    heads, lo, bounds, q_ref, kv_ref, o_ref, do_ref, lse_ref, qrow_ref, beg_ref, koff_ref, cos_ref, sin_ref,
    dq_ref, dkv_ref, delta, acc
):
    size = koff_ref.shape[0]
    factor = HEAD_DIM**-0.5
    acc[...] = jnp.zeros_like(acc)
    dkv_ref[...] = jnp.zeros_like(dkv_ref)
    for h in range(heads):
        cols = slice(h * HEAD_DIM, (h + 1) * HEAD_DIM)
        both = do_ref[:, cols].astype(F32) * o_ref[:, cols].astype(F32)
        delta[h] = jnp.sum(both.T, axis=0, keepdims=True)

    def step(block, carry):
        rows = block_rows_of(block, bounds, lo, size)
        keys = kv_ref[rows, :HEAD_DIM]
        values = kv_ref[rows, HEAD_DIM:]
        turned_keys = keys.astype(F32).T.astype(BF16)
        closed = closed_keys(block, size, koff_ref, qrow_ref, beg_ref)
        dkeys = jnp.zeros((size, HEAD_DIM), F32)
        dvalues = jnp.zeros((size, HEAD_DIM), F32)
        for h in range(heads):
            cols = slice(h * HEAD_DIM, (h + 1) * HEAD_DIM)
            queries = q_ref[:, cols]
            grads = do_ref[:, cols]
            scores = against(keys, queries) * (factor * LOG2E) + closed
            probs = jnp.exp2(scores - lse_ref[h])
            dvalues = dvalues + product(probs.astype(BF16), grads)
            dprobs = against(values, grads)
            dscores = (probs * ((dprobs - delta[h]) * factor)).astype(BF16)
            acc[h] = acc[h] + product(turned_keys, dscores)
            dkeys = dkeys + product(dscores, queries)
        dkv_ref[rows, :HEAD_DIM] = dkeys.astype(BF16)
        dkv_ref[rows, HEAD_DIM:] = dvalues.astype(BF16)
        return carry

    lax.fori_loop(bounds[0], bounds[1] + 1, step, 0)
    for h in range(heads):
        grads = acc[h].T
        back = grads * cos_ref[...] - pltpu.roll(grads, HEAD_DIM // 2, 1) * sin_ref[...]
        dq_ref[:, h * HEAD_DIM : (h + 1) * HEAD_DIM] = back.astype(BF16)


VMEM_SPEC = pl.BlockSpec(memory_space=pltpu.VMEM)
SMEM_SPEC = pl.BlockSpec(memory_space=pltpu.SMEM)
NOTHING = pl.CostEstimate(flops=1, bytes_accessed=1, transcendentals=0)


def attend(bounds, q, kv, qrow, beg, koff, lo):
    rows, width = q.shape
    heads = width // HEAD_DIM
    return pl.pallas_call(
        functools.partial(attend_kernel, heads, lo),
        out_shape=(
            jax.ShapeDtypeStruct((rows, width), BF16),
            jax.ShapeDtypeStruct((heads, 1, rows), F32),
        ),
        in_specs=[SMEM_SPEC] + [VMEM_SPEC] * 5,
        out_specs=(VMEM_SPEC, VMEM_SPEC),
        scratch_shapes=[
            pltpu.VMEM((heads, 1, rows), F32),
            pltpu.VMEM((heads, 1, rows), F32),
            pltpu.VMEM((heads, HEAD_DIM, rows), F32),
        ],
        compiler_params=pltpu.CompilerParams(vmem_limit_bytes=16 * MIB),
        cost_estimate=NOTHING,
    )(bounds, q, kv, qrow, beg, koff)


def attend_back(bounds, q, kv, o, do, lse, qrow, beg, koff, cosine, signed, lo):
    rows, width = q.shape
    heads = width // HEAD_DIM
    return pl.pallas_call(
        functools.partial(attend_back_kernel, heads, lo),
        out_shape=(
            jax.ShapeDtypeStruct((rows, width), BF16),
            jax.ShapeDtypeStruct(kv.shape, BF16),
        ),
        in_specs=[SMEM_SPEC] + [VMEM_SPEC] * 10,
        out_specs=(VMEM_SPEC, VMEM_SPEC),
        scratch_shapes=[
            pltpu.VMEM((heads, 1, rows), F32),
            pltpu.VMEM((heads, HEAD_DIM, rows), F32),
        ],
        compiler_params=pltpu.CompilerParams(vmem_limit_bytes=16 * MIB),
        cost_estimate=NOTHING,
    )(bounds, q, kv, o, do, lse, qrow, beg, koff, cosine, signed)


class Exchange:
    def __init__(self, mesh):
        self.shards = mesh.shape["fsdp"]
        self.hi = HI
        self.lo = self.shards // HI
        self.tp = mesh.shape["tp"]
        self.hi_groups = [[h * self.lo + b for h in range(self.hi)] for b in range(self.lo)]

    def lo_shift(self, v, s):
        pairs = [
            (h * self.lo + b, h * self.lo + (b + s) % self.lo) for h in range(self.hi) for b in range(self.lo)
        ]
        return lax.ppermute(v, "fsdp", pairs)

    def flip(self, v, mask):
        return lax.ppermute(v, "tp", [(t, t ^ mask) for t in range(self.tp)])

    def hi_swap(self, v):
        return lax.all_to_all(v, "fsdp", 0, 0, axis_index_groups=self.hi_groups)

    def hi_copies(self, w):
        return self.hi_swap(jnp.broadcast_to(w[None], (self.hi,) + w.shape))

    def lo_gather(self, v):
        return tuple(self.lo_shift(v, -s) for s in range(1, self.lo))

    def lo_scatter(self, v):
        m = v.shape[0] // (self.lo - 1)
        return tuple(self.lo_shift(v[s * m : (s + 1) * m], s + 1) for s in range(self.lo - 1))

    def hi_rows(self, v):
        return self.hi_copies(v).reshape(self.hi * v.shape[0], v.shape[1])

    def turned_lo(self, parts, start):
        if self.lo == 2:
            return [jnp.where(start == 0, parts[0], parts[1]), jnp.where(start == 0, parts[1], parts[0])]
        both = jnp.concatenate([part[None] for part in parts + parts], axis=0)
        both = lax.dynamic_slice_in_dim(both, start, self.lo, axis=0)
        return [both[s] for s in range(self.lo)]

    def to_pieces(self, v):
        n = v.shape[1] // self.shards
        b = lax.axis_index("fsdp") % self.lo
        parts = [
            jnp.concatenate([v[:, (h * self.lo + l) * n : (h * self.lo + l + 1) * n] for h in range(self.hi)], axis=1)
            for l in range(self.lo)
        ]
        return jnp.concatenate(self.turned_lo(parts, b), axis=1)

    def from_pieces(self, v):
        n = v.shape[1] // self.shards
        b = lax.axis_index("fsdp") % self.lo
        own = self.hi * n
        parts = [v[:, s * own : (s + 1) * own] for s in range(self.lo)]
        parts = self.turned_lo(parts, (self.lo - b) % self.lo)
        return jnp.concatenate(
            [parts[l][:, h * n : (h + 1) * n] for h in range(self.hi) for l in range(self.lo)], axis=1
        )

    def quarters(self, w):
        n, k = w.shape
        chunk = -(-k // (self.hi * 128)) * 128
        w = jnp.pad(w, ((0, 0), (0, self.hi * chunk - k)))
        return w.reshape(n, self.hi, chunk).transpose(1, 0, 2)


def kernel_call(kernel, outs, args, flops, scratch=(), limit=16):
    return pl.pallas_call(
        kernel,
        out_shape=outs,
        in_specs=[VMEM_SPEC] * len(args),
        out_specs=jax.tree.map(lambda _: VMEM_SPEC, outs),
        scratch_shapes=list(scratch),
        compiler_params=pltpu.CompilerParams(vmem_limit_bytes=limit * MIB),
        cost_estimate=NOTHING,
    )(*args)


def shape(dims, kind):
    return jax.ShapeDtypeStruct(tuple(dims), kind)


def flat(pieces):
    return [p.reshape(-1, p.shape[-1]) for p in pieces]


def through(x_ref, pieces):
    depth = x_ref.shape[1] // len(pieces)
    total = None
    for s, piece in enumerate(pieces):
        part = product(x_ref[:, s * depth : (s + 1) * depth], piece[...])
        total = part if total is None else total + part
    return total


def turned(v, cosine, signed):
    return v * cosine + pltpu.roll(v, HEAD_DIM // 2, 1) * signed


def key_value(x, pieces, cosine, signed):
    def kernel(x_ref, *refs):
        *ws, cos_ref, sin_ref, out_ref = refs
        raw = through(x_ref, ws)
        out_ref[:, :HEAD_DIM] = turned(raw[:, :HEAD_DIM], cos_ref[...], sin_ref[...]).astype(BF16)
        out_ref[:, HEAD_DIM:] = raw[:, HEAD_DIM:].astype(BF16)

    rows, k = x.shape[0], pieces[0].shape[1]
    return kernel_call(kernel, shape((rows, k), BF16), (x, *pieces, cosine, signed), 2 * rows * k * x.shape[1])


def query(x, pieces, cosine, signed):
    def kernel(x_ref, *refs):
        *ws, cos_ref, sin_ref, out_ref = refs
        raw = through(x_ref, ws)
        for c in range(0, out_ref.shape[1], HEAD_DIM):
            cols = slice(c, c + HEAD_DIM)
            out_ref[:, cols] = turned(raw[:, cols], cos_ref[...], sin_ref[...]).astype(BF16)

    rows, k = x.shape[0], pieces[0].shape[1]
    return kernel_call(kernel, shape((rows, k), BF16), (x, *pieces, cosine, signed), 2 * rows * k * x.shape[1])


def project(x, pieces):
    def kernel(x_ref, *refs):
        *ws, out_ref = refs
        out_ref[...] = through(x_ref, ws).astype(BF16)

    rows, k = x.shape[0], pieces[0].shape[1]
    return kernel_call(kernel, shape((rows, k), BF16), (x, *pieces), 2 * rows * k * x.shape[1])


def expand(terms, extra=None):
    rows = terms[0][0].shape[0]
    half = rows // 2
    lo = len(terms[0][1])
    depth = terms[0][1][0].shape[0]
    width = lo * depth

    def kernel(*refs):
        keep_ref, send_ref = refs[-2:]
        groups = [refs[g * (lo + 1) : (g + 1) * (lo + 1)] for g in range(len(terms))]
        for s in range(lo):
            cols = slice(s * depth, (s + 1) * depth)
            total = None
            for group in groups:
                part = against(group[0][...], group[1 + s][...])
                total = part if total is None else total + part
            keep_ref[:, cols] = total[:half]
            send_ref[:, cols] = total[half:].astype(BF16)

    flops = sum(2 * rows * t[0].shape[1] * width for t in terms)
    args = tuple(a for t in terms for a in (t[0], *t[1]))
    return kernel_call(kernel, (shape((half, width), F32), shape((half, width), BF16)), args, flops)


def feed_forward(upper, lower, gates, ups):
    half, depth = upper.shape
    rows = 2 * half
    lo = len(gates) // 2
    chunk = gates[0].shape[1]

    def kernel(upper_ref, lower_ref, *refs):
        x_ref, gate_ref, up_ref, hidden_ref = refs[-4:]
        x_ref[:half] = upper_ref[...]
        x_ref[half:] = lower_ref[...]
        for side in range(2):
            cols = slice(side * chunk, (side + 1) * chunk)
            gate = through(x_ref, refs[side * lo : (side + 1) * lo])
            up = through(x_ref, refs[(2 + side) * lo : (3 + side) * lo])
            gate_ref[:, cols] = gate
            up_ref[:, cols] = up
            hidden_ref[:, cols] = (gate * jax.nn.sigmoid(gate) * up).astype(BF16)

    dims = (rows, 2 * chunk)
    outs = (shape((rows, depth), BF16), shape(dims, F32), shape(dims, F32), shape(dims, BF16))
    return kernel_call(kernel, outs, (upper, lower, *gates, *ups), 1, limit=20)


def feed_back(upper, lower, downs, gate, up):
    half, depth = upper.shape
    rows, width = gate.shape
    chunk = width // 2
    lo = len(downs) // 2

    def kernel(upper_ref, lower_ref, *refs):
        gate_ref, up_ref, d_ref, dgate_ref, dup_ref = refs[-5:]
        d_ref[:half] = upper_ref[...]
        d_ref[half:] = lower_ref[...]
        for side in range(2):
            cols = slice(side * chunk, (side + 1) * chunk)
            gates = gate_ref[:, cols]
            sigma = jax.nn.sigmoid(gates)
            scaled = through(d_ref, refs[side * lo : (side + 1) * lo]) * sigma
            dgate_ref[:, cols] = (scaled * up_ref[:, cols] * (1.0 + gates * (1.0 - sigma))).astype(BF16)
            dup_ref[:, cols] = (scaled * gates).astype(BF16)

    dims = (rows, width)
    outs = (shape((rows, depth), BF16), shape(dims, BF16), shape(dims, BF16))
    return kernel_call(kernel, outs, (upper, lower, *downs, gate, up), 1, limit=20)


def weight_sums(x, d, first, k, lo, extra=None):
    rows, width = x.shape
    own = width // lo

    def kernel(x_ref, d_ref, *refs):
        keep_ref, send_ref = refs[-2:]
        dcols = d_ref[:, first : first + k]
        for s in range(lo):
            part = slice(s * own, (s + 1) * own)
            total = outer_sum(x_ref[:, part], dcols)
            if extra is not None:
                total = total + refs[0][part, :].astype(F32)
            if s == 0:
                keep_ref[...] = total
            else:
                send_ref[(s - 1) * own : s * own, :] = total.astype(BF16)

    args = (x, d) + (() if extra is None else (extra,))
    outs = (shape((own, k), F32), shape((width - own, k), BF16))
    return kernel_call(kernel, outs, args, 2 * rows * k * width)


def weight_sums_sent(x, d, first, k):
    def kernel(x_ref, d_ref, out_ref):
        out_ref[...] = outer_sum(x_ref[...], d_ref[:, first : first + k]).astype(BF16)

    rows, width = x.shape
    return kernel_call(kernel, shape((width, k), BF16), (x, d), 2 * rows * k * width)


def tie(*values):
    return lax.optimization_barrier(values)


def local(
    ex,
    tokens,
    cotangent,
    doc_starts,
    skip_flags,
    gain_attn,
    w_query,
    w_key,
    w_value,
    w_out,
    gain_mlp,
    w_gate,
    w_up,
    w_down,
):
    count, width = tokens.shape
    q_width = w_query.shape[1]
    k_width = w_key.shape[1]
    hidden_width = w_gate.shape[1]
    n = w_gate.shape[0]
    chunk = -(-hidden_width // (ex.hi * 128)) * 128
    block_rows = count * ex.tp
    fsdp = lax.axis_index("fsdp")
    tp = lax.axis_index("tp")
    offsets = jnp.arange(count, dtype=jnp.int32)
    koff = jnp.concatenate([(tp ^ m) * count + offsets for m in (0, 2, 1, 3)])


    def gained(w, gain):
        return (w.astype(F32) * gain.astype(F32)[:, None]).astype(BF16)

    def normed(x):
        x = x.astype(F32)
        return x, lax.rsqrt(jnp.mean(x * x, axis=-1, keepdims=True) + EPS)

    def rows_of(doc_starts, skip_flags):
        row_index = fsdp * block_rows + koff
        begins, keep_rows = documents(doc_starts, skip_flags, row_index)
        cosine, sine = angles(row_index - begins, HEAD_DIM)
        half = HEAD_DIM // 2
        signed = jnp.concatenate([-sine[:, :half], sine[:, half:]], axis=1)
        bounds = jnp.stack([jnp.min(begins) // block_rows, fsdp, fsdp % ex.lo]).astype(jnp.int32)
        return cosine, signed, row_index[None, :], begins[None, :], bounds, keep_rows[:count, None]

    def cotangents(cotangent, keep):
        cot = ex.to_pieces(cotangent)
        return cot, (keep * cot.astype(F32)).astype(BF16)

    def joined(v, *got):
        return jnp.concatenate([v, *got], axis=0)

    def normed_rows(first, got):
        x, scale = normed(joined(first, got))
        return (x * scale).astype(BF16)

    def attention(qu, own_piece, others, qrow, beg, bounds):
        kv_all = jnp.concatenate(flat((own_piece, *others)), axis=0)
        attended, lse = attend(bounds, qu, kv_all, qrow, beg, koff[:, None], ex.lo)
        return attended, lse, kv_all

    def attention_back(qu, kva, att, datt, lse, qrow, beg, bounds, cosine, signed):
        dq, dkv = attend_back(bounds, qu, kva, att, datt, lse, qrow, beg, koff[:, None], cosine, signed, ex.lo)
        m = dkv.shape[0] // ex.lo
        return dq, dkv[:m], dkv[m:]

    def halves(keep, got):
        g = keep + got.astype(F32)
        return g[: g.shape[0] // 2], g[g.shape[0] // 2 :].astype(BF16)

    def added(keep, got):
        return (keep + got.astype(F32)).astype(BF16).reshape(ex.hi, count, width)

    def summed(kept, got):
        for v in got:
            kept = kept + v.astype(F32)
        return kept

    def middle_of(kept, got, tok, keep):
        middle, scale = normed(tok.astype(F32) + keep * (kept + got.astype(F32)))
        return middle, (middle * scale).astype(BF16)

    def sides(p0, p1, p2, p3):
        return flat((p0, *p1, p2, *p3))

    def feed_back_rows(dgate, dup, *ws):
        gates, ups = sides(*ws[:4]), sides(*ws[4:])
        return expand(
            [
                (dgate[:, :chunk], gates[: ex.lo]),
                (dgate[:, chunk:], gates[ex.lo :]),
                (dup[:, :chunk], ups[: ex.lo]),
                (dup[:, chunk:], ups[ex.lo :]),
            ]
        )

    def down_rows(hid, *ws):
        downs = sides(*ws)
        return expand([(hid[:, :chunk], downs[: ex.lo]), (hid[:, chunk:], downs[ex.lo :])])

    def hi_total(got):
        return jnp.sum(got.astype(F32), axis=0)

    def layer_rows(got, middle, keep):
        return ex.from_pieces((middle + keep * hi_total(got)).astype(BF16))

    def middle_back(got, middle, cot, keep):
        scaled = hi_total(got)
        scale = normed(middle)[1]
        d_middle = (
            cot.astype(F32)
            + scale * scaled
            - middle * scale**3 * jnp.mean(scaled * middle, axis=-1, keepdims=True)
        )
        return d_middle, (keep * d_middle).astype(BF16)

    def lo_total(kept, got):
        total = summed(kept.astype(F32), got).astype(BF16)
        return total.reshape(ex.hi, -1, total.shape[1])

    def spread(got):
        return jnp.concatenate([got[h] for h in range(ex.hi)], axis=1)[:, :hidden_width].astype(F32)

    def spread_gained(got, w, gain):
        total = spread(got)
        return total * gain.astype(F32)[:, None], jnp.sum(total * w.astype(F32), axis=1)

    def query_grads(got, gain, *weights):
        total = hi_total(got)
        w = jnp.concatenate(weights, axis=1).astype(F32)
        return total * gain.astype(F32)[:, None], jnp.sum(total * w, axis=1)

    def key_grads(got, gain, *weights):
        total, part = query_grads(got, gain, *weights)
        return total[:, :k_width], total[:, k_width:], part

    def keys_back(got, cosine, signed):
        total = hi_total(got)
        half = k_width // 2
        dk = total[:, :k_width]
        turned_back = dk * cosine - jnp.concatenate([dk[:, half:], dk[:, :half]], axis=1) * signed
        return jnp.concatenate([turned_back, total[:, k_width:]], axis=1).astype(BF16)

    def attention_rows_back(dq, q0, q1, dkv, kv0, kv1):
        return expand([(dq, flat((q0, *q1))), (dkv, flat((kv0, *kv1)))])

    def tokens_back(kept, got, tok, d_mid):
        scaled = kept + got.astype(F32)
        x, scale = normed(tok)
        d_tokens = d_mid + scale * scaled - x * scale**3 * jnp.mean(scaled * x, axis=-1, keepdims=True)
        return ex.from_pieces(d_tokens.astype(BF16))


    w_query, gain_attn = tie(w_query, gain_attn)
    s_q = gained(w_query, gain_attn)
    q0 = ex.hi_copies(s_q)
    tok = ex.to_pieces(tokens)
    tok_x = ex.flip(tok, 2)
    tok, w_key, w_value, gain_attn = tie(tok, w_key, w_value, gain_attn)
    s_kv = gained(jnp.concatenate([w_key, w_value], axis=1), gain_attn)
    s_kv, w_gate, gain_mlp = tie(s_kv, w_gate, gain_mlp)
    s_g = ex.quarters(gained(w_gate, gain_mlp))
    s_g, tok_x = tie(s_g, tok_x)
    tok_x, doc_starts, skip_flags = tie(tok_x, doc_starts, skip_flags)
    cosine, signed, qrow, beg, bounds, keep = rows_of(doc_starts, skip_flags)
    keep, tok, tok_x = tie(keep, tok, tok_x)
    tok2 = joined(tok, tok_x)
    tok_c = ex.flip(tok2, 1)
    tok2, w_out = tie(tok2, w_out)
    s_o = w_out.T
    s_o, tok_c = tie(s_o, tok_c)
    tok_c, tok2 = tie(tok_c, tok2)
    xh = normed_rows(tok2, tok_c)
    xh, s_kv = tie(xh, s_kv)
    kv0 = ex.hi_copies(s_kv)
    xh, q0 = tie(xh, q0)
    q1 = ex.lo_gather(q0)
    q0, w_up, gain_mlp = tie(q0, w_up, gain_mlp)
    s_u = ex.quarters(gained(w_up, gain_mlp))
    s_u, w_down = tie(s_u, w_down)
    s_d = ex.quarters(w_down.T)
    s_d, s_u = tie(s_d, s_u)
    u0 = ex.hi_swap(s_u)
    s_d, kv0 = tie(s_d, kv0)
    kv0, q1 = tie(kv0, q1)
    q1, cotangent, keep = tie(q1, cotangent, keep)
    cot, dm_own = cotangents(cotangent, keep)
    dm_own, kv0 = tie(dm_own, kv0)
    kv1 = ex.lo_gather(kv0)
    dm_own, s_o = tie(dm_own, s_o)
    o0 = ex.hi_copies(s_o)
    dm_own, u0 = tie(dm_own, u0)
    u2 = ex.flip(u0, 2)
    u0, xh, q0, q1, cosine, signed = tie(u0, xh, q0, q1, cosine, signed)
    qu = query(xh, flat((q0, *q1)), cosine, signed)
    qu, kv1 = tie(qu, kv1)
    kv1, u0 = tie(kv1, u0)
    u1 = ex.lo_gather(u0)
    kv1, xh, kv0, cosine, signed = tie(kv1, xh, kv0, cosine, signed)
    kv = key_value(xh, flat((kv0, *kv1)), cosine, signed)
    kv, u2 = tie(kv, u2)
    u2, kv = tie(u2, kv)
    kr0 = ex.hi_copies(kv)
    u2, o0 = tie(u2, o0)
    o1 = ex.lo_gather(o0)
    o0, u1 = tie(o0, u1)
    u3 = tuple(ex.flip(v, 2) for v in u1)
    u1, kr0 = tie(u1, kr0)
    kr0, s_g = tie(kr0, s_g)
    g0 = ex.hi_swap(s_g)
    kr0, o1 = tie(kr0, o1)
    o1, u3 = tie(o1, u3)
    u3, kr0 = tie(u3, kr0)
    kr1 = ex.lo_gather(kr0)
    u3, g0 = tie(u3, g0)
    g2 = ex.flip(g0, 2)
    g0, kr1 = tie(g0, kr1)
    kr1, dm_own = tie(kr1, dm_own)
    dm4 = ex.hi_rows(dm_own)
    kr1, g0 = tie(kr1, g0)
    g1 = ex.lo_gather(g0)
    kr1, qu, kr0, qrow, beg, bounds = tie(kr1, qu, kr0, qrow, beg, bounds)
    att, lse, kva = attention(qu, kr0, kr1, qrow, beg, bounds)
    kva, g2 = tie(kva, g2)
    g2, dm4 = tie(g2, dm4)
    dm4, g1 = tie(dm4, g1)
    g1, s_d = tie(g1, s_d)
    d0 = ex.hi_swap(s_d)
    g1, att, o0, o1 = tie(g1, att, o0, o1)
    ao_k, ao_s = expand([(att, flat((o0, *o1)))])
    ao_s, g1 = tie(ao_s, g1)
    g3 = tuple(ex.flip(v, 2) for v in g1)
    ao_r = ex.flip(ao_s, 1)
    ao_k, dm4 = tie(ao_k, dm4)
    dm_c = ex.flip(dm4, 1)
    ao_k, g3 = tie(ao_k, g3)
    g3, ao_r = tie(g3, ao_r)
    ao_r, ao_k = tie(ao_r, ao_k)
    ao_k2, ao_s2 = halves(ao_k, ao_r)
    ao_s2, dm_c = tie(ao_s2, dm_c)
    dm_c, ao_s2 = tie(dm_c, ao_s2)
    ao_r2 = ex.flip(ao_s2, 2)
    dm_c, d0 = tie(dm_c, d0)
    d1 = ex.lo_gather(d0)
    d2 = ex.flip(d0, 2)
    d0, ao_r2 = tie(d0, ao_r2)
    ao_r2, ao_k2, tok, keep = tie(ao_r2, ao_k2, tok, keep)
    middle, nrm = middle_of(ao_k2, ao_r2, tok, keep)
    nm4 = ex.hi_rows(nrm)
    middle, d1 = tie(middle, d1)
    d1, d2 = tie(d1, d2)
    d2, d1 = tie(d2, d1)
    d3 = tuple(ex.flip(v, 2) for v in d1)
    d2, nm4 = tie(d2, nm4)
    nm_c = ex.flip(nm4, 1)
    nm4, nm_c = tie(nm4, nm_c)
    nm_c, nm4, g0, g1, g2, g3, u0, u1, u2, u3 = tie(nm_c, nm4, g0, g1, g2, g3, u0, u1, u2, u3)
    nm, gate, up, hid = feed_forward(nm4, nm_c, sides(g0, g1, g2, g3), sides(u0, u1, u2, u3))
    hid, d3 = tie(hid, d3)
    d3, dm4, dm_c, d0, d1, d2, gate, up = tie(d3, dm4, dm_c, d0, d1, d2, gate, up)
    dm, dgate, dup = feed_back(dm4, dm_c, sides(d0, d1, d2, d3), gate, up)
    dup, nm = tie(dup, nm)
    gu_x = weight_sums_sent(nm, dup, chunk, chunk)
    gu_r = ex.flip(gu_x, 2)
    dup, dgate, g0, g1, g2, g3, u0, u1, u2, u3 = tie(dup, dgate, g0, g1, g2, g3, u0, u1, u2, u3)
    e_k, e_s = feed_back_rows(dgate, dup, g0, g1, g2, g3, u0, u1, u2, u3)
    c3_r = ex.flip(e_s, 1)
    e_k, hid, d0, d1, d2, d3 = tie(e_k, hid, d0, d1, d2, d3)
    m_k, m_s = down_rows(hid, d0, d1, d2, d3)
    m_s, c3_r = tie(m_s, c3_r)
    c3_r, dm, hid = tie(c3_r, dm, hid)
    gd_x = weight_sums_sent(dm, hid, chunk, chunk)
    gd_x, m_s = tie(gd_x, m_s)
    mo_r = ex.flip(m_s, 1)
    gd_x, e_k, c3_r = tie(gd_x, e_k, c3_r)
    c3_s = added(e_k, c3_r)
    c3_z = ex.hi_swap(c3_s)
    gd_x, mo_r = tie(gd_x, mo_r)
    mo_r, m_k = tie(mo_r, m_k)
    mo_s = added(m_k, mo_r)
    mo_s, nm, dgate = tie(mo_s, nm, dgate)
    gg_x = weight_sums_sent(nm, dgate, chunk, chunk)
    gg_x, gu_r = tie(gg_x, gu_r)
    gu_r, gd_x = tie(gu_r, gd_x)
    gd_r = ex.flip(gd_x, 2)
    gu_r, c3_z = tie(gu_r, c3_z)
    c3_z, nm, dup, gu_r = tie(c3_z, nm, dup, gu_r)
    gu_k, gu_s = weight_sums(nm, dup, 0, chunk, ex.lo, gu_r)
    gu_s, mo_s = tie(gu_s, mo_s)
    mo_z = ex.hi_swap(mo_s)
    gu_y = ex.lo_scatter(gu_s)
    gu_k, c3_z, middle, cot, keep = tie(gu_k, c3_z, middle, cot, keep)
    d_mid, da_own = middle_back(c3_z, middle, cot, keep)
    da_own, gu_y = tie(da_own, gu_y)
    gu_y, gu_k = tie(gu_y, gu_k)
    gu_l = lo_total(gu_k, gu_y)
    gu_l, mo_z = tie(gu_l, mo_z)
    mo_z, gu_l = tie(mo_z, gu_l)
    gu_z = ex.hi_swap(gu_l)
    mo_z, gd_r = tie(mo_z, gd_r)
    gd_r, dm, hid = tie(gd_r, dm, hid)
    gd_k, gd_s = weight_sums(dm, hid, 0, chunk, ex.lo, gd_r)
    gd_y = ex.lo_scatter(gd_s)
    gd_k, da_own = tie(gd_k, da_own)
    da_x = ex.flip(da_own, 2)
    gd_k, gg_x = tie(gd_k, gg_x)
    gg_r = ex.flip(gg_x, 2)
    gd_k, da_x = tie(gd_k, da_x)
    da_x, da_own = tie(da_x, da_own)
    da2 = joined(da_own, da_x)
    da_c = ex.flip(da2, 1)
    da2, da_c = tie(da2, da_c)
    da_c, da2 = tie(da_c, da2)
    da = joined(da2, da_c)
    da, o0, o1 = tie(da, o0, o1)
    datt = project(da, flat((o0, *o1)))
    (
        datt,
        qu,
        kva,
        att,
        lse,
        qrow,
        beg,
        bounds,
        cosine,
        signed,
    ) = tie(
        datt,
        qu,
        kva,
        att,
        lse,
        qrow,
        beg,
        bounds,
        cosine,
        signed,
    )
    dq, dk_k, dk_s = attention_back(qu, kva, att, datt, lse, qrow, beg, bounds, cosine, signed)
    dk_s, gu_z = tie(dk_s, gu_z)
    gu_z, gd_y = tie(gu_z, gd_y)
    gd_y, dk_s = tie(gd_y, dk_s)
    dk_y = ex.lo_scatter(dk_s)
    gd_y, gd_k = tie(gd_y, gd_k)
    gd_l = lo_total(gd_k, gd_y)
    gd_z = ex.hi_swap(gd_l)
    gu_z, xh, dq = tie(gu_z, xh, dq)
    gq_k, gq_s = weight_sums(xh, dq, 0, q_width, ex.lo)
    gq_s, gg_r = tie(gq_s, gg_r)
    gg_r, nm, dgate = tie(gg_r, nm, dgate)
    gg_k, gg_s = weight_sums(nm, dgate, 0, chunk, ex.lo, gg_r)
    gg_y = ex.lo_scatter(gg_s)
    gg_k, dk_y = tie(gg_k, dk_y)
    dk_y, dk_k = tie(dk_y, dk_k)
    dk_l = lo_total(dk_k, dk_y)
    dk_l, gd_z = tie(dk_l, gd_z)
    gd_z, dk_l = tie(gd_z, dk_l)
    dk_z = ex.hi_swap(dk_l)
    gd_z, gq_s = tie(gd_z, gq_s)
    gq_y = ex.lo_scatter(gq_s)
    gd_z, gg_y = tie(gd_z, gg_y)
    gg_y, gg_k = tie(gg_y, gg_k)
    gg_l = lo_total(gg_k, gg_y)
    gg_z = ex.hi_swap(gg_l)
    gd_z, dk_z = tie(gd_z, dk_z)
    dk_z, cosine, signed = tie(dk_z, cosine, signed)
    dkv = keys_back(dk_z, cosine, signed)
    dkv, dq, q0, q1, kv0, kv1 = tie(dkv, dq, q0, q1, kv0, kv1)
    n_k, n_s = attention_rows_back(dq, q0, q1, dkv, kv0, kv1)
    n_s, xh, dkv = tie(n_s, xh, dkv)
    gk_k, gk_s = weight_sums(xh, dkv, 0, 2 * k_width, ex.lo)
    gk_y = ex.lo_scatter(gk_s)
    gk_k, da, att = tie(gk_k, da, att)
    go_k, go_s = weight_sums(da, att, 0, q_width, ex.lo)
    go_y = ex.lo_scatter(go_s)
    go_k, n_s = tie(go_k, n_s)
    n_r = ex.flip(n_s, 1)
    go_k, n_r = tie(go_k, n_r)
    n_r, n_k = tie(n_r, n_k)
    n_k2, n_s2 = halves(n_k, n_r)
    n_r2 = ex.flip(n_s2, 2)
    n_k2, gq_y = tie(n_k2, gq_y)
    gq_y, gq_k = tie(gq_y, gq_k)
    gq_l = lo_total(gq_k, gq_y)
    gq_l, gg_z = tie(gq_l, gg_z)
    gg_z, gq_l = tie(gg_z, gq_l)
    gq_z = ex.hi_swap(gq_l)
    gg_z, gk_y = tie(gg_z, gk_y)
    gk_y, gk_k = tie(gk_y, gk_k)
    gk_l = lo_total(gk_k, gk_y)
    gk_l, n_r2 = tie(gk_l, n_r2)
    n_r2, gg_z, w_gate, gain_mlp = tie(n_r2, gg_z, w_gate, gain_mlp)
    grad_gate, sum_g = spread_gained(gg_z, w_gate, gain_mlp)
    sum_g, n_k2, n_r2, tok, d_mid = tie(sum_g, n_k2, n_r2, tok, d_mid)
    d_tokens = tokens_back(n_k2, n_r2, tok, d_mid)
    d_tokens, go_y = tie(d_tokens, go_y)
    go_y, go_k = tie(go_y, go_k)
    go_l = lo_total(go_k, go_y)
    go_l, gq_z = tie(go_l, gq_z)
    gq_z, gk_l = tie(gq_z, gk_l)
    gk_z = ex.hi_swap(gk_l)
    gq_z, mo_z, middle, keep = tie(gq_z, mo_z, middle, keep)
    layer_out = layer_rows(mo_z, middle, keep)
    layer_out, gd_z = tie(layer_out, gd_z)
    grad_down = spread(gd_z).T
    grad_down, gu_z, w_up, gain_mlp = tie(grad_down, gu_z, w_up, gain_mlp)
    grad_up, sum_u = spread_gained(gu_z, w_up, gain_mlp)
    sum_u, gq_z, gain_attn, w_query = tie(sum_u, gq_z, gain_attn, w_query)
    grad_query, sum_q = query_grads(gq_z, gain_attn, w_query)
    sum_q, gk_z = tie(sum_q, gk_z)
    gk_z, go_l = tie(gk_z, go_l)
    go_z = ex.hi_swap(go_l)
    gk_z, gain_attn, w_key, w_value = tie(gk_z, gain_attn, w_key, w_value)
    grad_key, grad_value, sum_k = key_grads(gk_z, gain_attn, w_key, w_value)
    sum_k, sum_q, sum_g, sum_u = tie(sum_k, sum_q, sum_g, sum_u)
    gains = jnp.stack([sum_q + sum_k, sum_g + sum_u])
    gains_x = ex.flip(gains, 2)
    gains, gains_x = tie(gains, gains_x)
    gains_x, gains = tie(gains_x, gains)
    gains2 = gains + gains_x
    gains_c = ex.flip(gains2, 1)
    gains2, gains_c = tie(gains2, gains_c)
    gains_c, gains2 = tie(gains_c, gains2)
    grad_gain_attn, grad_gain_mlp = gains2 + gains_c
    grad_gain_mlp, go_z = tie(grad_gain_mlp, go_z)
    grad_out = hi_total(go_z).T
    return (
        layer_out,
        d_tokens,
        grad_gain_attn,
        grad_query,
        grad_key,
        grad_value,
        grad_out,
        grad_gain_mlp,
        grad_gate,
        grad_up,
        grad_down,
    )


def solution(mesh):
    rows = P(("fsdp", "tp"), None)
    in_specs = (
        rows,
        rows,
        P(),
        P(),
        P("fsdp"),
        P("fsdp", "tp"),
        P("fsdp", "tp"),
        P("fsdp", "tp"),
        P("tp", "fsdp"),
        P("fsdp"),
        P("fsdp", "tp"),
        P("fsdp", "tp"),
        P("tp", "fsdp"),
    )
    out_specs = (
        rows,
        rows,
        P("fsdp"),
        P("fsdp", "tp"),
        P("fsdp", "tp"),
        P("fsdp", "tp"),
        P("tp", "fsdp"),
        P("fsdp"),
        P("fsdp", "tp"),
        P("fsdp", "tp"),
        P("tp", "fsdp"),
    )
    return jax.shard_map(
        functools.partial(local, Exchange(mesh)), mesh=mesh, in_specs=in_specs, out_specs=out_specs, check_vma=False
    )
```
